256 devices in a mesh: gx: 32 (over z, x), gy: 8 (over y, core).
Axes of the slice: x: 4, y: 4, z: 8, core: 2. Of those that a mesh axis runs over, the one named last changes fastest.
Arguments:
- density: float32 [128, 64, 256], P('gx', 'gy'), may hold values from 0.3 to 1
- passive_void_mask: int32 [128, 64, 256], P('gx', 'gy'), may hold values 0 or 1
- support_node_mask: int32 [128, 64, 256], P('gx', 'gy'), may hold values 0 or 1
- loaded_node_mask: int32 [2, 128, 64, 256], P(None, 'gx', 'gy'), may hold values 0 or 1
- traction: float32 [2, 3, 128, 64, 256], P(None, None, 'gx', 'gy'), may hold values from -6 to 6
Outputs:
- displacement: float32 [2, 3, 128, 64, 256], P(None, None, 'gx', 'gy')
- sensitivity: float32 [128, 64, 256], P('gx', 'gy')
- compliance: float32 [2], replicated
The draws below stay inside these ranges and needn't reach their ends.
All inputs are finite; a program needn't handle non-finite values. No bound on the sum of `passive_void_mask` or of `support_node_mask` or of `loaded_node_mask` on one device may be relied on, other than what follows from the above.
Results may differ from the reference program's by a relative error of at most 0.0003.
Values sent between devices are 32-bit elements; how exact they have to be, the bound alone decides.
A program may use at most 64 MiB of HBM per device.

```python
import math
import jax
import jax.numpy as jnp
import numpy as np
from jax import lax

ELEMENTS_HEIGHT = 256
LEVELS = 3
SWEEPS = 4
ELEMENTS_LENGTH = 128
ELEMENTS_WIDTH = 64
N_GX = 32


def set_ends(array, stream_key, smallest, top_value):
    longest = array.shape.index(max(array.shape))
    spots = []
    for shift in (0, 1):
        where = [jax.random.randint(jax.random.fold_in(stream_key, axis), (), 0, length) for axis, length in enumerate(array.shape)]
        where[longest] = (where[longest] + shift) % array.shape[longest]
        spots.append(tuple(where))
    return array.at[spots[0]].set(smallest).at[spots[1]].set(top_value)


def block_levels(stream_key, shape, pieces, smallest, largest):
    factor_of, own = 1.0, jax.random.fold_in(stream_key, 6)
    for dim, shards_of in pieces:
        heights = jnp.exp(jax.random.uniform(jax.random.fold_in(own, dim), (shards_of,), jnp.float32, smallest / len(pieces), largest / len(pieces)))
        factor_of = factor_of * jnp.repeat(heights, shape[dim] // shards_of).reshape([-1 if axis == dim else 1 for axis in range(len(shape))])
    return factor_of


def gaussian(rng, extent, scale, bound, cuts=(), kind=jnp.bfloat16):
    values = scale * jax.random.normal(rng, extent, jnp.float32)
    if cuts:
        values = values * block_levels(rng, extent, cuts, -0.22, 0.18)
    return jnp.clip(values, -bound, bound).astype(kind)


def setup_inputs(seed: int = 0) -> dict:
    keys = jax.random.split(jax.random.key(seed), 6)
    density = jnp.clip(0.3 + 0.7 * jax.random.uniform(keys[0], (ELEMENTS_LENGTH, ELEMENTS_WIDTH, ELEMENTS_HEIGHT), jnp.float32) ** block_levels(keys[0], (ELEMENTS_LENGTH, ELEMENTS_WIDTH, ELEMENTS_HEIGHT), ((0, 32), (1, 8)), -0.2, 0.2), 0.3, 1.0)
    passive_void_mask = set_ends((jax.random.randint(keys[1], (ELEMENTS_LENGTH, ELEMENTS_WIDTH, ELEMENTS_HEIGHT), 0, 8) < 1).astype(jnp.int32), jax.random.fold_in(keys[1], 1), 0, 1)
    support_node_mask = set_ends((jax.random.randint(keys[2], (ELEMENTS_LENGTH, ELEMENTS_WIDTH, ELEMENTS_HEIGHT), 0, 8) < 1).astype(jnp.int32), jax.random.fold_in(keys[2], 1), 0, 1)
    loaded_node_mask = set_ends((jax.random.randint(keys[3], (2, ELEMENTS_LENGTH, ELEMENTS_WIDTH, ELEMENTS_HEIGHT), 0, 2) < 1).astype(jnp.int32), jax.random.fold_in(keys[3], 1), 0, 1)
    traction = gaussian(keys[4], (2, 3, ELEMENTS_LENGTH, ELEMENTS_WIDTH, ELEMENTS_HEIGHT), 1.0, 6.0, ((2, 32), (3, 8)), jnp.float32)
    return dict(density=density, passive_void_mask=passive_void_mask, support_node_mask=support_node_mask, loaded_node_mask=loaded_node_mask, traction=traction)


damping = 0.5
stiff_min = 0.001
penalty = 3.0
sharpness = 8.0
threshold = 0.5
filter_radius = 3.0
corner_list = [(0, 0, 0), (0, 0, 1), (0, 1, 0), (0, 1, 1), (1, 0, 0), (1, 0, 1), (1, 1, 0), (1, 1, 1)]

def element_stiffness():
    poisson = 0.3
    lame_first = poisson / ((1.0 + poisson) * (1.0 - 2.0 * poisson))
    lame_shear = 1.0 / (2.0 * (1.0 + poisson))
    elastic = np.zeros((6, 6))
    elastic[:3, :3] = lame_first
    for number in range(3):
        elastic[number, number] = lame_first + 2.0 * lame_shear
        elastic[number + 3, number + 3] = lame_shear
    points = [0.5 - 0.5 / math.sqrt(3.0), 0.5 + 0.5 / math.sqrt(3.0)]
    matrix = np.zeros((24, 24))
    for point_x in points:
        for point_y in points:
            for point_z in points:
                where_at = (point_x, point_y, point_z)
                strain = np.zeros((6, 24))
                for number, corner in enumerate(corner_list):
                    slopes = []
                    for direction in range(3):
                        factor = 1.0
                        for second in range(3):
                            if second == direction:
                                factor = factor * (1.0 if corner[second] else -1.0)
                            elif corner[second]:
                                factor = factor * where_at[second]
                            else:
                                factor = factor * (1.0 - where_at[second])
                        slopes.append(factor)
                    column = 3 * number
                    strain[0, column] = slopes[0]
                    strain[1, column + 1] = slopes[1]
                    strain[2, column + 2] = slopes[2]
                    strain[3, column] = slopes[1]
                    strain[3, column + 1] = slopes[0]
                    strain[4, column + 1] = slopes[2]
                    strain[4, column + 2] = slopes[1]
                    strain[5, column] = slopes[2]
                    strain[5, column + 2] = slopes[0]
                matrix = matrix + strain.T @ elastic @ strain / 8.0
    return matrix.reshape(8, 3, 8, 3).astype(np.float32)

def filter_offsets():
    entries = []
    for offset_x in range(-2, 3):
        for offset_y in range(-2, 3):
            for offset_z in range(-2, 3):
                weight = filter_radius - math.sqrt(offset_x * offset_x + offset_y * offset_y + offset_z * offset_z)
                if weight > 0.0:
                    entries.append((offset_x, offset_y, offset_z, weight))
    return entries

def weighted_sum(padded, begin, counts):
    running = jnp.zeros(counts, jnp.float32)
    for offset_x, offset_y, offset_z, weight in filter_offsets():
        start_x = begin[0] + offset_x
        start_y = begin[1] + offset_y
        start_z = begin[2] + offset_z
        running = running + weight * padded[start_x:start_x + counts[0], start_y:start_y + counts[1], start_z:start_z + counts[2]]
    return running

def projection(filtered):
    edge_value = jnp.tanh(sharpness * threshold)
    total_range = edge_value + jnp.tanh(sharpness * (1.0 - threshold))
    level_value = jnp.tanh(sharpness * (filtered - threshold))
    return ((edge_value + level_value) / total_range, sharpness * (1.0 - level_value * level_value) / total_range)

def element_apply(field_pad, stiff_pad, scale_factor, wanted):
    element_table = jnp.asarray(element_stiffness())
    count_x = field_pad.shape[2] - 2
    count_y = field_pad.shape[3] - 2
    count_z = field_pad.shape[4] - 2
    results = []
    energies = []
    for load_index in range(field_pad.shape[0]):
        stacked = jnp.stack([field_pad[load_index, :, step_x:step_x + count_x + 1, step_y:step_y + count_y + 1, step_z:step_z + count_z + 1] for step_x, step_y, step_z in corner_list])
        forces = jnp.einsum('acbd,bdxyz->acxyz', element_table, stacked, precision=lax.Precision.HIGHEST)
        if wanted != 'energy':
            weighted = forces * (scale_factor * stiff_pad)
            running = jnp.zeros((3, count_x, count_y, count_z), jnp.float32)
            for number, (step_x, step_y, step_z) in enumerate(corner_list):
                running = running + weighted[number, :, 1 - step_x:1 - step_x + count_x, 1 - step_y:1 - step_y + count_y, 1 - step_z:1 - step_z + count_z]
            results.append(running)
        if wanted != 'result':
            energies.append(lax.optimization_barrier(jnp.sum(stacked[:, :, 1:, 1:, 1:] * forces[:, :, 1:, 1:, 1:], axis=(0, 1))))
    result = jnp.stack(results) if results else None
    energy = jnp.stack(energies) if energies else None
    return (result, energy)

def node_diagonal(stiff_pad, scale_factor):
    count_x = stiff_pad.shape[0] - 1
    count_y = stiff_pad.shape[1] - 1
    count_z = stiff_pad.shape[2] - 1
    running = jnp.zeros((count_x, count_y, count_z), jnp.float32)
    for step_x, step_y, step_z in corner_list:
        running = running + stiff_pad[1 - step_x:1 - step_x + count_x, 1 - step_y:1 - step_y + count_y, 1 - step_z:1 - step_z + count_z]
    return float(element_stiffness()[0, 0, 0, 0]) * scale_factor * running

def coarsen(stiffness):
    count_x, count_y, count_z = stiffness.shape
    return lax.optimization_barrier(jnp.mean(stiffness.reshape(count_x // 2, 2, count_y // 2, 2, count_z // 2, 2), axis=(1, 3, 5)))

def restrict_axis(values, dimension):
    length = values.shape[dimension] - 1
    even_rows = lax.slice_in_dim(values, 0, length, 2, dimension)
    middle = lax.slice_in_dim(values, 1, length + 1, 2, dimension)
    upper_rows = lax.slice_in_dim(values, 2, length + 1, 2, dimension)
    return 0.5 * even_rows + middle + 0.5 * upper_rows

def prolong_axis(values, dimension):
    count_rows = values.shape[dimension] - 1
    lesser = lax.slice_in_dim(values, 0, count_rows, 1, dimension)
    higher = lax.slice_in_dim(values, 1, count_rows + 1, 1, dimension)
    paired = jnp.stack([lesser, 0.5 * (lesser + higher)], axis=dimension + 1)
    new_shape = list(lesser.shape)
    new_shape[dimension] = 2 * count_rows
    return paired.reshape(new_shape)

def blocked_apply(field, stiffness, scale_factor, wanted):
    count_x = field.shape[2]
    block_rows = count_x // N_GX
    field_pad = jnp.pad(field, ((0, 0), (0, 0), (1, 1), (1, 1), (1, 1)))
    stiff_pad = jnp.pad(stiffness, ((1, 0), (1, 0), (1, 0)))

    def one_block(block_index):
        block_start = (block_index * block_rows).astype(jnp.int32)
        part_field = lax.dynamic_slice_in_dim(field_pad, block_start, block_rows + 2, 2)
        part_stiff = lax.dynamic_slice_in_dim(stiff_pad, block_start, block_rows + 1, 0)
        return element_apply(part_field, part_stiff, scale_factor, wanted)
    image, energy = lax.map(one_block, jnp.arange(N_GX, dtype=jnp.int32))
    if image is not None:
        image = jnp.moveaxis(image, 0, 2).reshape(field.shape)
    if energy is not None:
        energy = jnp.moveaxis(energy, 0, 1).reshape(field.shape[0], count_x, field.shape[3], field.shape[4])
    return (image, energy)

def reference_cycle(level_index, right_side, stiffs, diags, keep_node):
    scale_factor = 2.0 ** level_index
    approx = damping * right_side / diags[level_index]
    if level_index == LEVELS - 1:
        for sweep_index in range(SWEEPS - 1):
            image = blocked_apply(approx, stiffs[level_index], scale_factor, 'result')[0]
            approx = approx + damping * (right_side - image) / diags[level_index]
        return approx
    image = blocked_apply(approx, stiffs[level_index], scale_factor, 'result')[0]
    if level_index == 0:
        image = keep_node * image
    coarse = jnp.pad(right_side - image, ((0, 0), (0, 0), (1, 0), (1, 0), (1, 0)))
    for dimension in (2, 3, 4):
        coarse = restrict_axis(coarse, dimension)
    correction = reference_cycle(level_index + 1, coarse, stiffs, diags, keep_node)
    correction = jnp.pad(correction, ((0, 0), (0, 0), (0, 1), (0, 1), (0, 1)))
    for dimension in (2, 3, 4):
        correction = prolong_axis(correction, dimension)
    if level_index == 0:
        correction = keep_node * correction
    approx = approx + correction
    image = blocked_apply(approx, stiffs[level_index], scale_factor, 'result')[0]
    if level_index == 0:
        image = keep_node * image
    return approx + damping * (right_side - image) / diags[level_index]

def reference(density, passive_void_mask, support_node_mask, loaded_node_mask, traction):
    shape_all = density.shape
    inside = jnp.pad(jnp.ones(shape_all, jnp.float32), 2)
    numerator = weighted_sum(jnp.pad(density, 2), (2, 2, 2), shape_all)
    denominator = weighted_sum(inside, (2, 2, 2), shape_all)
    shaped, slope_value = projection(numerator / denominator)
    keep_elem = 1.0 - passive_void_mask.astype(jnp.float32)
    physical = keep_elem * shaped
    stiffness = stiff_min + (1.0 - stiff_min) * physical ** penalty
    stiffs = [stiffness]
    for level_index in range(1, LEVELS):
        stiffs.append(coarsen(stiffs[-1]))
    diags = [node_diagonal(jnp.pad(stiffs[level_index], ((1, 0), (1, 0), (1, 0))), 2.0 ** level_index) for level_index in range(LEVELS)]
    keep_node = 1.0 - support_node_mask.astype(jnp.float32)
    right_side = keep_node * (loaded_node_mask.astype(jnp.float32)[:, None] * traction)
    precond = reference_cycle(0, right_side, stiffs, diags, keep_node)
    image = keep_node * blocked_apply(precond, stiffness, 1.0, 'result')[0]
    preconditioned_inner_product = lax.optimization_barrier(jnp.sum(right_side * precond, axis=(1, 2, 3, 4)))
    curvature = lax.optimization_barrier(jnp.sum(precond * image, axis=(1, 2, 3, 4)))
    conjugate_step_size = preconditioned_inner_product / curvature
    displacement = conjugate_step_size[:, None, None, None, None] * precond
    compliance = conjugate_step_size * preconditioned_inner_product / (ELEMENTS_LENGTH * ELEMENTS_WIDTH * ELEMENTS_HEIGHT)
    energy = lax.optimization_barrier(jnp.sum(blocked_apply(displacement, stiffness, 1.0, 'energy')[1], axis=0))
    ratio_field = -energy * penalty * physical ** (penalty - 1.0) * (1.0 - stiff_min) * keep_elem * slope_value / denominator
    sensitivity = weighted_sum(jnp.pad(ratio_field, 2), (2, 2, 2), shape_all)
    return (displacement, sensitivity, compliance)
```

```python
import math

import jax
import jax.numpy as jnp
from jax import lax
from jax.experimental import pallas as pl
from jax.experimental.pallas import tpu as pltpu
from jax.sharding import PartitionSpec as P

NX, NY = 32, 8
BX, BY, BZ = 4, 8, 256
CELLS = NX * BX * NY * BY * BZ
F32 = jnp.float32

POISSON = 0.3
LAME1 = POISSON / ((1.0 + POISSON) * (1.0 - 2.0 * POISSON))
LAME2 = 1.0 / (2.0 * (1.0 + POISSON))
RATIO = LAME1 / LAME2
DIAG = (LAME1 + 4.0 * LAME2) / 9.0
EDGE = math.tanh(4.0)

R3_SLOTS = [(a, b) for a in range(-4, 6) for b in range(-2, 4) if (a, b) != (0, 0)]
S1_SLOTS = [(a, b) for a in range(-2, 3) for b in range(-1, 2) if (a, b) != (0, 0)]


def iota(shape, dim):
    return lax.broadcasted_iota(jnp.int32, shape, dim)


def weight(a, b, c):
    return max(3.0 - math.sqrt(a * a + b * b + c * c), 0.0)


def z_up(v, z, by=1):
    n = v.shape[1]
    return jnp.where(iota(v.shape, 1) % z < z - by, pltpu.roll(v, n - by, 1), 0.0)


def z_down(v, z, by=1):
    n = v.shape[1]
    return jnp.where(iota(v.shape, 1) % z >= by, pltpu.roll(v, by, 1), 0.0)


def y_up(v, by=1):
    return pltpu.roll(v, v.shape[0] - by, 0)


def y_down(v, by=1):
    return pltpu.roll(v, by, 0)


def mm(a, b):
    return jnp.dot(a, b, preferred_element_type=F32, precision=lax.Precision.HIGHEST)


def couple(a, s):
    def key(*dims):
        return tuple(1 if d in dims else 0 for d in range(3))

    f = [dict() for _ in range(3)]
    trace = RATIO * (a[0][key(0)] + a[1][key(1)] + a[2][key(2)])
    third = None if s is None else s * (1.0 / 3.0)

    def times(x, scale, k):
        if scale is None:
            return x if k == 1.0 else x * k
        return x * scale

    for i in range(3):
        f[i][key(i)] = times(trace + 2.0 * a[i][key(i)], s, 1.0)
    for i in range(3):
        for j in range(i + 1, 3):
            shear = times(a[i][key(j)] + a[j][key(i)], s, 1.0)
            f[i][key(j)] = shear
            f[j][key(i)] = shear
    for k in range(3):
        i, j = [d for d in range(3) if d != k]
        p, q = a[i][key(i, k)], a[j][key(j, k)]
        both = RATIO * (p + q)
        f[i][key(i, k)] = times(both + 3.0 * p, third, 1.0 / 3.0)
        f[j][key(j, k)] = times(both + 3.0 * q, third, 1.0 / 3.0)
    mixed = [a[i][key(*[d for d in range(3) if d != i])] for i in range(3)]
    total = mixed[0] + mixed[1] + mixed[2]
    for i in range(3):
        f[i][key(*[d for d in range(3) if d != i])] = times(mixed[i] + total, third, 1.0 / 3.0)
        bubble = a[i][(1, 1, 1)] * ((RATIO + 4.0) / 9.0)
        f[i][(1, 1, 1)] = bubble if s is None else bubble * s
    return f


HYZ = [(0, 0), (0, 1), (1, 0), (1, 1)]


def modes_of(low, high):
    a = [dict() for _ in range(3)]
    for c in range(3):
        for k, (hy, hz) in enumerate(HYZ):
            if k:
                a[c][(0, hy, hz)] = low[4 * c + k] + high[4 * c + k]
            a[c][(1, hy, hz)] = high[4 * c + k] - low[4 * c + k]
    return a


def spread_planes(x_ref, first, xoff, planes, g_ref, z, tiles):
    def body(p, carry):
        for c in range(3):
            v = x_ref[first + c, xoff + p]
            up = z_up(v, z)
            for hz, t in ((0, v + up), (1, up - v)):
                tu = y_up(t)
                for hy, g in ((0, t + tu), (1, tu - t)):
                    for tile in range(tiles):
                        r, q = tile_place(tile, v.shape[1])
                        g_ref[tile, p, 4 * c + 2 * hy + hz] = g[r : r + 8, q : q + 128]
        return carry

    lax.fori_loop(0, planes, body, 0)


def tile_place(tile, lanes):
    per = lanes // 128
    return 8 * (tile // per), 128 * (tile % per)


def element_planes(g_ref, h_ref, s_ref, soff, scale, elements, tiles, lanes):
    per = lanes // 128

    def over_tile(tile, carry):
        r = pl.multiple_of(8 * (tile // per), 8)
        q = pl.multiple_of(128 * (tile % per), 128)

        def body(e, held):
            low, acc = held[:12], held[12:]
            high = tuple(g_ref[tile, e + 1, k] for k in range(12))
            s = s_ref[soff + e, pl.ds(r, 8), pl.ds(q, 128)] * (scale * LAME2 / 16.0)
            f = couple(modes_of(low, high), s)
            fresh = []
            for c in range(3):
                for k, (hy, hz) in enumerate(HYZ):
                    fd = f[c][(1, hy, hz)]
                    if k:
                        fs = f[c][(0, hy, hz)]
                        h_ref[tile, e, 4 * c + k] = acc[4 * c + k] + (fs - fd)
                        fresh.append(fs + fd)
                    else:
                        h_ref[tile, e, 4 * c + k] = acc[4 * c + k] - fd
                        fresh.append(fd)
            return high + tuple(fresh)

        start = tuple(g_ref[tile, 0, k] for k in range(12))
        zeros = tuple(jnp.zeros((8, 128), F32) for _ in range(12))
        lax.fori_loop(0, elements, body, start + zeros)
        return carry

    lax.fori_loop(0, tiles, over_tile, 0)


def gather_nodes(h_ref, e, c, z, lanes):
    def load(k):
        rows = []
        for half in range(2):
            tiles = [h_ref[half * (lanes // 128) + q, e, 4 * c + k] for q in range(lanes // 128)]
            rows.append(tiles[0] if len(tiles) == 1 else jnp.concatenate(tiles, axis=1))
        return jnp.concatenate(rows, axis=0)

    t = []
    for hz in range(2):
        hs, hd = load(hz), load(2 + hz)
        t.append((hs - hd) + y_down(hs + hd))
    return (t[0] - t[1]) + z_down(t[0] + t[1], z)


def apply_level(x_ref, groups, xoff, s_ref, soff, scale, elements, g_ref, h_ref, z, lanes, use):
    tiles = 2 * lanes // 128

    def one(l, carry):
        spread_planes(x_ref, 3 * l, xoff, elements + 1, g_ref, z, tiles)
        element_planes(g_ref, h_ref, s_ref, soff, scale, elements, tiles, lanes)

        def nodes(e, inner):
            for c in range(3):
                use(3 * l + c, e, gather_nodes(h_ref, e, c, z, lanes))
            return inner

        lax.fori_loop(1, elements, nodes, 0)
        return carry

    lax.fori_loop(0, groups, one, 0)


def filter_plane(load, p):
    a = [load(p), load(p - 1) + load(p + 1), load(p - 2) + load(p + 2)]
    f = []
    for c in range(3):
        h = []
        for b in range(3):
            t = None
            for i in range(3):
                w = weight(i, b, c)
                if w > 0.0:
                    t = w * a[i] if t is None else t + w * a[i]
            h.append(t)
        out = h[0]
        if h[1] is not None:
            out = out + (y_up(h[1]) + y_down(h[1]))
        if h[2] is not None:
            out = out + (y_up(h[2], 2) + y_down(h[2], 2))
        f.append(out)
    z = f[0].shape[1]
    return (
        f[0]
        + (z_up(f[1], z) + z_down(f[1], z))
        + (z_up(f[2], z, 2) + z_down(f[2], z, 2))
    )


SCRATCH = dict(
    df=(12, 8, BZ), pf=(8, 8, BZ), bf=(7, 7, 8, BZ),
    sup=(4, 8, BZ), lod=(2, 4, 8, BZ), tra=(2, 3, 4, 8, BZ), pas=(4, 8, BZ),
    ya_up=(4, 8, BZ), ya_dn=(4, 8, BZ), yb_up=(4, 8, BZ), yb_dn=(2, 4, 8, BZ),
    ra_lo=(12, 8, BZ), ra_hi=(12, 8, BZ), rb_lo=(7, 8, BZ), rb_hi=(2, 7, 8, BZ),
    gden=(3, 16, BZ), d16=(12, 16, BZ), s16=(8, 16, BZ), coef=(8, 8, BZ),
    b16=(6, 7, 16, BZ), x0=(6, 7, 16, BZ), keep=(7, 16, BZ), invd=(7, 16, BZ),
    g=(4, 7, 12, 8, 128), h=(4, 6, 12, 8, 128), r0=(6, 4, 8, BZ),
    zl=(18, 8, BZ), zr=(18, 8, 128), zc=(2, 8, 128),
    pb=(6, 3, 8, 128), pbu=(3, 3, 8, 128), pbd=(3, 3, 8, 128),
    s1s=(2, 8, 128), rs1=(len(S1_SLOTS), 2, 8, 128),
    rd1=(2, 6, 3, 8, 128), rd2=(2, 6, 1, 8, 128),
    rp1=(3, 2, 3, 3, 8, 128), rp2=(2, 2, 3, 1, 8, 128),
    s1=(8, 16, 128), invd1=(7, 16, 128), b1=(6, 7, 16, 128), x1=(6, 7, 16, 128),
    g1=(2, 7, 12, 8, 128), h1=(2, 6, 12, 8, 128), r1=(6, 3, 16, 128),
    t2l=(4, 8, BZ), t2r=(4, 8, 128), t2=(8, 128), t2v=(4, 8, 128), rb2=(len(R3_SLOTS), 8, 128),
    s2=(10, 16, 128), invd2=(10, 16, 128), b2=(3, 10, 16, 128), x2=(3, 10, 16, 128),
    g2=(2, 10, 12, 8, 128), h2=(2, 9, 12, 8, 128),
    yy2=(12, 16, 128), w2=(12, 16, BZ), yy1=(30, 16, 128), v1=(30, 16, BZ),
    sums=(8, 128), ry=(7, 8, 128), sy=(8, 128), rx=(31, 8, 128),
    rt=(2, 8, 8, BZ), yt=(4, 8, BZ), rt_lo=(8, 8, BZ), rt_hi=(8, 8, BZ),
    f16=(8, 16, BZ), fil=(2, 4, 8, BZ),
)
INTS = ("sup", "lod", "pas")
NAMES = list(SCRATCH)
N_SEMS = 64


def kernel(dens, pas_in, sup_in, lod_in, tra_in, disp, sens, comp, *scratch):
    m = dict(zip(NAMES, scratch))
    load_sem, send_sem, recv_sem, group_send, group_recv = scratch[len(NAMES) :]
    gx, gy = lax.axis_index("gx"), lax.axis_index("gy")
    me = gx * NY + gy

    def device(ax, ay):
        return lax.rem(gx + ax + NX, NX), lax.rem(gy + ay + NY, NY)

    barrier = pltpu.get_barrier_semaphore()

    def greet(k, carry):
        other = lax.rem(me + k, NX * NY)
        pl.semaphore_signal(
            barrier, inc=1, device_id=(other // NY, lax.rem(other, NY)),
            device_id_type=pl.DeviceIdType.MESH,
        )
        return carry

    lax.fori_loop(1, NX * NY, greet, 0)

    loads = [
        pltpu.make_async_copy(dens, m["df"].at[pl.ds(4, 4)], load_sem.at[0]),
        pltpu.make_async_copy(pas_in, m["pas"], load_sem.at[1]),
        pltpu.make_async_copy(sup_in, m["sup"], load_sem.at[2]),
        pltpu.make_async_copy(lod_in, m["lod"], load_sem.at[3]),
        pltpu.make_async_copy(tra_in, m["tra"], load_sem.at[4]),
    ]
    for copy in loads:
        copy.start()

    counter = [0]

    def message(src, dst, ax, ay):
        k = counter[0]
        counter[0] += 1
        return pltpu.make_async_remote_copy(
            src_ref=src, dst_ref=dst, send_sem=send_sem.at[k], recv_sem=recv_sem.at[k],
            device_id=device(ax, ay), device_id_type=pl.DeviceIdType.MESH,
        )

    def sub(z=BZ):
        return iota((8, z), 0)

    def inside(cond):
        return jnp.where(cond, 1.0, 0.0).astype(F32)

    def in_x(x, size):
        return inside((x >= 0) & (x < size))

    row16 = iota((16, BZ), 0)
    y0 = gy * BY + jnp.where(row16 < 12, row16, row16 - 16)
    rows0 = inside((y0 >= 0) & (y0 < NY * BY))
    row16h = iota((16, 128), 0)
    y1 = gy * 4 + jnp.where(row16h < 8, row16h, row16h - 16)
    rows1 = inside((y1 >= 0) & (y1 < NY * 4))
    y2 = gy * 2 + jnp.where(row16h < 8, row16h, row16h - 16)
    rows2 = inside((y2 >= 0) & (y2 < NY * 2))

    def in_y(y):
        return inside((y >= 0) & (y < NY * BY))

    zi = iota((16, BZ), 1)
    cz = [None] + [inside(zi >= d) + inside(zi < BZ - d) for d in (1, 2)]
    cy = [None] + [in_y(y0 - d) + in_y(y0 + d) for d in (1, 2)]
    for a in range(3):
        total = None
        for b in range(3):
            w = weight(a, b, 0) + weight(a, b, 1) * cz[1]
            if weight(a, b, 2) > 0.0:
                w = w + weight(a, b, 2) * cz[2]
            w = w if b == 0 else w * cy[b]
            total = w if total is None else total + w
        m["gden"][a] = total

    loads[1].wait()
    loads[0].wait()
    df, pf, bf = m["df"], m["pf"], m["bf"]
    for x in range(4):
        pf[2 + x] = 1.0 - m["pas"][x].astype(F32)
        p4 = y_down(pf[2 + x], 4)
        m["ya_up"][x] = jnp.where(sub() >= 4, df[4 + x], p4)
        m["ya_dn"][x] = jnp.where(sub() < 4, df[4 + x], p4)
    loads[2].wait()
    loads[3].wait()
    loads[4].wait()
    for x in range(4):
        kept = 1.0 - m["sup"][x].astype(F32)
        bf[6, 1 + x] = kept
        for l in range(2):
            mask = kept * m["lod"][l, x].astype(F32)
            for c in range(3):
                bf[3 * l + c, 1 + x] = mask * m["tra"][l, c, x]
        for f in range(7):
            v = bf[f, 1 + x]
            m["yb_up"][x, f : f + 1] = v[7:8]
            m["yb_dn"][0, x, f : f + 1] = v[0:1]
            m["yb_dn"][1, x, f : f + 1] = v[1:2]
        m["yb_up"][x, 7:8] = jnp.zeros((1, BZ), F32)
        m["yb_dn"][0, x, 7:8] = jnp.zeros((1, BZ), F32)
        m["yb_dn"][1, x, 7:8] = jnp.zeros((1, BZ), F32)

    pl.semaphore_wait(barrier, NX * NY - 1)

    ra_lo, ra_hi, rb_lo, rb_hi = m["ra_lo"], m["ra_hi"], m["rb_lo"], m["rb_hi"]
    own = df.at[pl.ds(4, 4)]
    first = [
        message(m["ya_up"], ra_lo.at[pl.ds(0, 4)], 1, 1),
        message(m["ya_dn"], ra_hi.at[pl.ds(0, 4)], 1, -1),
        message(m["ya_up"], ra_lo.at[pl.ds(8, 4)], -1, 1),
        message(m["ya_dn"], ra_hi.at[pl.ds(8, 4)], -1, -1),
        message(own, df.at[pl.ds(0, 4)], 1, 0),
        message(own, df.at[pl.ds(8, 4)], -1, 0),
        message(pf.at[pl.ds(4, 2)], pf.at[pl.ds(0, 2)], 1, 0),
        message(pf.at[pl.ds(2, 2)], pf.at[pl.ds(6, 2)], -1, 0),
        message(m["ya_up"], ra_lo.at[pl.ds(4, 4)], 0, 1),
        message(m["ya_dn"], ra_hi.at[pl.ds(4, 4)], 0, -1),
    ]
    second = [
        message(m["yb_up"].at[pl.ds(3, 1)], rb_lo.at[pl.ds(0, 1)], 1, 1),
        message(m["yb_dn"].at[:, pl.ds(3, 1)], rb_hi.at[:, pl.ds(0, 1)], 1, -1),
        message(m["yb_up"].at[pl.ds(0, 2)], rb_lo.at[pl.ds(5, 2)], -1, 1),
        message(m["yb_dn"].at[:, pl.ds(0, 2)], rb_hi.at[:, pl.ds(5, 2)], -1, -1),
        message(bf.at[:, pl.ds(4, 1)], bf.at[:, pl.ds(0, 1)], 1, 0),
        message(bf.at[:, pl.ds(1, 2)], bf.at[:, pl.ds(5, 2)], -1, 0),
        message(m["yb_up"], rb_lo.at[pl.ds(1, 4)], 0, 1),
        message(m["yb_dn"], rb_hi.at[:, pl.ds(1, 4)], 0, -1),
    ]
    for copy in first + second:
        copy.start()
    for copy in first:
        copy.wait_recv()

    d16, s16 = m["d16"], m["s16"]

    def put_density(p, carry):
        halo = jnp.where(sub() < 4, ra_hi[p], ra_lo[p])
        both = jnp.concatenate([df[p], halo], axis=0)
        here = in_x(gx * BX + p - 4, NX * BX)
        d16[p] = jnp.where(rows0 * here > 0.0, both, 0.0)
        return carry

    lax.fori_loop(0, 12, put_density, 0)

    def stiffen(i, carry):
        x = gx * BX + i - 2
        number = filter_plane(lambda p: d16[p], i + 2)
        cx1 = in_x(x - 1, NX * BX) + in_x(x + 1, NX * BX)
        cx2 = in_x(x - 2, NX * BX) + in_x(x + 2, NX * BX)
        denom = m["gden"][0] + cx1 * m["gden"][1] + cx2 * m["gden"][2]
        level = jnp.tanh(8.0 * (number / denom - 0.5))
        slope = (1.0 - level * level) * (8.0 / (2.0 * EDGE))
        halo = pltpu.roll(jnp.where(sub() >= 4, ra_hi[i + 2], ra_lo[i + 2]), 4, 0)
        solid = jnp.concatenate([pf[i], halo], axis=0)
        phys = solid * ((EDGE + level) * (1.0 / (2.0 * EDGE)))
        stiff = 0.001 + 0.999 * (phys * phys * phys)
        s16[i] = jnp.where(rows0 * in_x(x, NX * BX) > 0.0, stiff, 0.0)
        coef = -3.0 * 0.999 * (phys * phys) * solid * slope / denom
        m["coef"][i] = coef[0:8]
        return carry

    lax.fori_loop(0, 8, stiffen, 0)

    zi2, zo2 = iota((BZ, 128), 0), iota((BZ, 128), 1)
    pairs_z = inside(zi2 // 2 == zo2) * 0.125
    flat = jnp.concatenate([(s16[2 + 2 * i] + s16[3 + 2 * i])[0:8] for i in range(2)], axis=0)
    flat = mm(flat, pairs_z)
    for i in range(2):
        v = flat[8 * i : 8 * i + 8]
        m["zc"][i] = v + y_up(v)
        half = m["zc"][i, pl.ds(0, 4, stride=2)]
        m["s1s"][i, 0:4] = half
        m["s1s"][i, 4:8] = half

    def group(src, dst, slots, k):
        for n, (dx, dy) in enumerate(slots):
            pltpu.make_async_remote_copy(
                src_ref=src(dx, dy), dst_ref=dst.at[n], send_sem=group_send.at[k],
                recv_sem=group_recv.at[k], device_id=device(-dx, -dy),
                device_id_type=pl.DeviceIdType.MESH,
            ).start()

    def group_done(dst, sem, k):
        pltpu.make_async_copy(dst, dst, sem.at[k]).wait()

    group(lambda dx, dy: m["s1s"], m["rs1"], S1_SLOTS, 0)

    for copy in second:
        copy.wait_recv()

    x0, b16, keep, invd = m["x0"], m["b16"], m["keep"], m["invd"]

    def halo_rows(p, f):
        lo = rb_lo[p, f : f + 1]
        hi0, hi1 = rb_hi[0, p, f : f + 1], rb_hi[1, p, f : f + 1]
        return jnp.where(
            sub() == 7, lo, jnp.where(sub() == 0, hi0, jnp.where(sub() == 1, hi1, 0.0))
        )

    def begin(p, carry):
        x = gx * BX + p - 1
        t = s16[p] + s16[p + 1]
        t = t + y_down(t)
        t = t + z_down(t, BZ)
        here = rows0 * in_x(x, NX * BX)
        kept = here * jnp.concatenate([bf[6, p], halo_rows(p, 6)], axis=0)
        inv = jnp.where(here > 0.0, kept * (0.5 / DIAG) / t, 0.0)
        keep[p] = kept
        invd[p] = inv
        for f in range(6):
            b = jnp.concatenate([bf[f, p], halo_rows(p, f)], axis=0)
            b16[f, p] = b
            x0[f, p] = inv * b
        return carry

    lax.fori_loop(0, 7, begin, 0)

    def residual(f, e, image):
        m["r0"][f, e - 1] = keep[e, 0:8] * (b16[f, e, 0:8] - image[0:8])

    apply_level(x0, 2, 0, s16, 1, 1.0, 5, m["g"], m["h"], BZ, BZ, residual)

    near = jnp.abs(zi2 - 2 * zo2)
    rest_z = jnp.where(near == 0, 1.0, jnp.where(near == 1, 0.5, 0.0)).astype(F32)

    def rest_x(f, carry):
        r = [m["r0"][f, x] for x in range(4)]
        m["zl"][3 * f] = r[0] + 0.5 * r[1]
        m["zl"][3 * f + 1] = 0.5 * (r[1] + r[3]) + r[2]
        m["zl"][3 * f + 2] = 0.5 * r[3]
        return carry

    lax.fori_loop(0, 6, rest_x, 0)
    flat = mm(m["zl"][...].reshape(144, BZ), rest_z)
    m["zr"][...] = flat.reshape(18, 8, 128)
    pb, pbu, pbd = m["pb"], m["pbu"], m["pbd"]
    sh = sub(128)

    def rest_y(f, carry):
        for i in range(3):
            v = m["zr"][3 * f + i]
            low = jnp.where(sh > 0, y_down(v), 0.0)
            m["zr"][3 * f + i] = v + 0.5 * (low + y_up(v))
            pb[f, i] = jnp.zeros((8, 128), F32)
            pb[f, i, 0:4] = m["zr"][3 * f + i, pl.ds(0, 4, stride=2)]
            pb[f, i, 4:5] = 0.5 * v[7:8]
        return carry

    lax.fori_loop(0, 6, rest_y, 0)

    def pack_y(c, carry):
        for i in range(3):
            one, two = pb[c, i], pb[3 + c, i]
            turned = y_down(one, 4)
            pbu[c, i] = jnp.where(
                (sh >= 6) | (sh == 0), turned, jnp.where((sh >= 2) & (sh <= 4), two, 0.0)
            )
            pbd[c, i] = jnp.where((sh >= 4) & (sh <= 6), turned, jnp.where(sh < 3, two, 0.0))
        return carry

    lax.fori_loop(0, 3, pack_y, 0)

    rd1, rd2, rp1, rp2 = m["rd1"], m["rd2"], m["rp1"], m["rp2"]

    def part(ref, lo, n):
        return ref.at[:, pl.ds(lo, n)]

    third = [
        message(part(pbu, 2, 1), rp2.at[0, 0], 2, 1),
        message(part(pbd, 2, 1), rp2.at[0, 1], 2, -1),
        message(part(pb, 2, 1), rd2.at[0], 2, 0),
        message(part(pbu, 0, 1), rp2.at[1, 0], -2, 1),
        message(part(pbd, 0, 1), rp2.at[1, 1], -2, -1),
        message(part(pb, 0, 1), rd2.at[1], -2, 0),
        message(pbu, rp1.at[0, 0], 1, 1),
        message(pbd, rp1.at[0, 1], 1, -1),
        message(pb, rd1.at[0], 1, 0),
        message(pbu, rp1.at[2, 0], -1, 1),
        message(pbd, rp1.at[2, 1], -1, -1),
        message(pb, rd1.at[1], -1, 0),
        message(pbu, rp1.at[1, 0], 0, 1),
        message(pbd, rp1.at[1, 1], 0, -1),
    ]
    for copy in third:
        copy.start()

    rs1, s1, invd1 = m["rs1"], m["s1"], m["invd1"]
    group_done(rs1, group_recv, 0)
    for p in range(8):
        x = p - 3
        dx, i = x // 2, x % 2
        mid = m["s1s"][i] if dx == 0 else rs1[S1_SLOTS.index((dx, 0)), i]
        top = rs1[S1_SLOTS.index((dx, 1)), i]
        low = rs1[S1_SLOTS.index((dx, -1)), i]
        frame = jnp.concatenate(
            [jnp.where(sh < 4, mid, top), jnp.where(sh >= 4, low, 0.0)], axis=0
        )
        here = rows1 * in_x(gx * 2 + x, NX * 2)
        s1[p] = jnp.where(here > 0.0, frame, 0.0)

    def diag1(p, carry):
        t = s1[p] + s1[p + 1]
        t = t + y_down(t)
        t = t + z_down(t, 128)
        here = rows1 * in_x(gx * 2 + p - 2, NX * 2)
        invd1[p] = jnp.where(here > 0.0, (0.5 / (2.0 * DIAG)) / t, 0.0)
        return carry

    lax.fori_loop(0, 7, diag1, 0)

    zi1, zo1 = iota((128, 128), 0), iota((128, 128), 1)
    pairs_2 = inside(zi1 // 2 == zo1 % 64) * 0.125
    t2l, t2r, t2 = m["t2l"], m["t2r"], m["t2"]
    own2 = s1[3] + s1[4]
    below2 = s1[1] + s1[2]
    wide = mm(jnp.concatenate([own2 + y_up(own2), below2 + y_up(below2)], axis=0), pairs_2)
    w_own, w_sum = wide[0:16], wide[0:16] + wide[16:32]
    dg = w_sum + y_down(w_sum, 2)
    dg = dg + z_down(dg, 64)
    dg = jnp.where(dg > 0.0, (0.5 / (4.0 * DIAG)) / dg, 0.0)
    t2r[3] = jnp.where(iota((8, 128), 1) < 64, w_own[0:8], dg[0:8])
    t2[6:8] = t2r[3, pl.ds(0, 2, stride=2)]

    for copy in third:
        copy.wait_recv()

    b1, x1 = m["b1"], m["x1"]
    okx = {d: (gx + d >= 0) & (gx + d < NX) for d in range(-2, 3)}
    oky = {d: (gy + d >= 0) & (gy + d < NY) for d in range(-1, 2)}

    def share(dx, dy, index, i):
        if dx == 0 and dy == 0:
            return pb[index, i]
        if dy == 0:
            v = rd1[0 if dx < 0 else 1, index, i] if abs(dx) == 1 else rd2[0 if dx < 0 else 1, index, 0]
        else:
            k = 0 if dy < 0 else 1
            v = rp1[dx + 1, k, index, i] if abs(dx) < 2 else rp2[0 if dx < 0 else 1, k, index, 0]
        return jnp.where(okx[dx] & oky[dy], v, 0.0)

    def sources(x):
        return [(dx, x - 2 * dx) for dx in range(-2, 3) if 0 <= x - 2 * dx <= 2 and (abs(dx) < 2 or (dx, x) in ((-2, -2), (2, 4)))]

    def right_side_1(c, carry):
        for p in range(7):
            x = p - 2
            up = down = None
            for dx, i in sources(x):
                u, d = share(dx, -1, c, i), share(dx, 1, c, i)
                up = u if up is None else up + u
                down = d if down is None else down + d
            for l in range(2):
                mid = None
                for dx, i in sources(x):
                    v = share(dx, 0, 3 * l + c, i)
                    mid = v if mid is None else mid + v
                if l == 1:
                    up, down = y_down(up, 4), y_down(down, 4)
                tile0 = mid + jnp.where(sh == 0, up, jnp.where((sh >= 4) & (sh <= 6), down, 0.0))
                tile1 = jnp.where(sh >= 6, up, 0.0)
                v = jnp.concatenate([tile0, tile1], axis=0)
                b1[3 * l + c, p] = v
                x1[3 * l + c, p] = invd1[p] * v
        return carry

    lax.fori_loop(0, 3, right_side_1, 0)

    def residual_1(f, e, image):
        m["r1"][f, e - 1] = b1[f, e] - image

    apply_level(x1, 2, 0, s1, 1, 2.0, 4, m["g1"], m["h1"], 128, 128, residual_1)

    for c in range(3):
        sides = []
        for l in range(2):
            r = [m["r1"][3 * l + c, x] for x in range(3)]
            v = r[1] + 0.5 * (r[0] + r[2])
            v = v + 0.5 * (y_up(v) + y_down(v))
            sides.append(v[0:8])
        t2l[c] = jnp.concatenate(sides, axis=1)
    t2l[3] = jnp.zeros((8, BZ), F32)
    near = jnp.abs(zi2 % 128 - 2 * (zo2 % 64))
    rest_2 = jnp.where(near == 0, 1.0, jnp.where(near == 1, 0.5, 0.0)).astype(F32)
    rest_2 = jnp.where(zi2 // 128 == zo2 // 64, rest_2, 0.0)
    flat = mm(t2l[...].reshape(32, BZ), rest_2)
    for c in range(3):
        t2r[c] = flat[8 * c : 8 * c + 8]
        t2[2 * c : 2 * c + 2] = t2r[c, pl.ds(0, 2, stride=2)]
    for k in range(4):
        m["t2v"][k] = t2[...] if k == 0 else y_down(t2[...], 2 * k)

    rb2 = m["rb2"]
    group(lambda dx, dy: m["t2v"].at[dy % 4], rb2, R3_SLOTS, 1)
    group_done(rb2, group_recv, 1)

    s2, invd2, b2, x2 = m["s2"], m["invd2"], m["b2"], m["x2"]
    pair = sh // 2
    half = iota((16, 128), 1) < 64
    for p in range(10):
        dx = p - 4

        def tile(dy, dx=dx):
            if (dx, dy) == (0, 0):
                return m["t2v"][0]
            return rb2[R3_SLOTS.index((dx, dy))]

        high = [tile(dy) for dy in range(4)]
        low = [tile(dy) for dy in (-2, -1)]
        here = rows2 * in_x(gx + dx, NX)
        frames = []
        for c in (3, 0, 1, 2):
            t0 = high[0]
            for dy in range(1, 4):
                t0 = jnp.where(pair == (dy + c) % 4, high[dy], t0)
            t1 = jnp.where(
                pair == (2 + c) % 4, low[0], jnp.where(pair == (3 + c) % 4, low[1], 0.0)
            )
            if c:
                t0, t1 = y_up(t0, 2 * c), y_up(t1, 2 * c)
            frames.append(jnp.concatenate([t0, t1], axis=0))
        v = jnp.where(here > 0.0, frames[0], 0.0)
        turned = pltpu.roll(v, 64, 1)
        s2[p] = jnp.where(half, v, turned)
        inv = jnp.where(half, turned, v)
        invd2[p] = inv
        for c in range(3):
            b2[c, p] = frames[1 + c]
            x2[c, p] = inv * frames[1 + c]

    for sweep in range(3):

        def smooth_2(f, e, image, sweep=sweep):
            p = sweep + e
            x2[f, p] = x2[f, p] + invd2[p] * (b2[f, p] - image)

        apply_level(
            x2, 1, sweep, s2, sweep, 4.0, 9 - 2 * sweep, m["g2"], m["h2"], 64, 128, smooth_2
        )

    yy2, w2, yy1, v1 = m["yy2"], m["w2"], m["yy1"], m["v1"]

    def widen_2(p, carry):
        for c in range(3):
            v = x2[c, 3 + p]
            odd = 0.5 * (v + y_up(v))
            k = 4 * c + p
            yy2[k, 8:16] = jnp.zeros((8, 128), F32)
            yy2[k, pl.ds(0, 4, stride=2)] = v[0:4]
            yy2[k, pl.ds(1, 4, stride=2)] = odd[0:4]
            yy2[k, 14:15] = v[15:16]
            yy2[k, 15:16] = odd[15:16]
        return carry

    lax.fori_loop(0, 4, widen_2, 0)
    zi3, zo3 = iota((128, BZ), 0), iota((128, BZ), 1)
    near = jnp.abs(zo3 % 128 - 2 * (zi3 % 64))
    pro_2 = jnp.where(near == 0, 1.0, jnp.where(near == 1, 0.5, 0.0)).astype(F32)
    pro_2 = jnp.where(zi3 // 64 == zo3 // 128, pro_2, 0.0)
    w2[...] = mm(yy2[...].reshape(192, 128), pro_2).reshape(12, 16, BZ)
    for p in range(7):
        x = p - 2
        here = rows1 * in_x(gx * 2 + x, NX * 2)
        for c in range(3):
            k = 4 * c + x // 2 + 1
            v = w2[k] if x % 2 == 0 else 0.5 * (w2[k] + w2[k + 1])
            x1[c, p] = x1[c, p] + here * v[:, 0:128]
            x1[3 + c, p] = x1[3 + c, p] + here * v[:, 128:256]

    def smooth_1(f, e, image):
        x1[f, e] = x1[f, e] + invd1[e] * (b1[f, e] - image)

    apply_level(x1, 2, 0, s1, 1, 2.0, 6, m["g1"], m["h1"], 128, 128, smooth_1)

    def widen_1(f, carry):
        for p in range(5):
            v = x1[f, 1 + p]
            odd = 0.5 * (v + y_up(v))
            k = 5 * f + p
            yy1[k, 8:16] = jnp.zeros((8, 128), F32)
            yy1[k, pl.ds(0, 4, stride=2)] = v[0:4]
            yy1[k, pl.ds(1, 4, stride=2)] = odd[0:4]
            yy1[k, 8:9] = v[4:5]
            yy1[k, 9:10] = odd[4:5]
            yy1[k, 15:16] = odd[15:16]
        return carry

    lax.fori_loop(0, 6, widen_1, 0)
    near = jnp.abs(zo3 - 2 * zi3)
    pro_1 = jnp.where(near == 0, 1.0, jnp.where(near == 1, 0.5, 0.0)).astype(F32)

    def widen_z(f, carry):
        at = pl.ds(5 * f, 5)
        v1[at] = mm(yy1[at].reshape(80, 128), pro_1).reshape(5, 16, BZ)
        return carry

    lax.fori_loop(0, 6, widen_z, 0)

    def correct(f, carry):
        for p in range(7):
            x = p - 1
            k = 5 * f + x // 2 + 1
            v = v1[k] if x % 2 == 0 else 0.5 * (v1[k] + v1[k + 1])
            x0[f, p] = x0[f, p] + keep[p] * v
        return carry

    lax.fori_loop(0, 6, correct, 0)

    def smooth_0(f, e, image):
        x0[f, e] = x0[f, e] + invd[e] * (b16[f, e] - image)

    apply_level(x0, 2, 0, s16, 1, 1.0, 6, m["g"], m["h"], BZ, BZ, smooth_0)

    rt, yt, sums = m["rt"], m["yt"], m["sums"]
    sums[...] = jnp.zeros((8, 128), F32)

    def energies(l, carry):
        spread_planes(x0, 3 * l, 1, 5, m["g"], BZ, 2)
        curve = jnp.zeros((8, 128), F32)
        dot = jnp.zeros((8, 128), F32)
        for tile in range(2):
            q = pl.ds(128 * tile, 128)
            for e in range(4):
                low = [m["g"][tile, e, k] for k in range(12)]
                high = [m["g"][tile, e + 1, k] for k in range(12)]
                a = modes_of(low, high)
                f = couple(a, None)
                energy = None
                for c in range(3):
                    for k in a[c]:
                        t = a[c][k] * f[c][k]
                        energy = t if energy is None else energy + t
                energy = energy * (LAME2 / 16.0)
                curve = curve + energy * s16[2 + e, 0:8, q]
                rt[l, 2 + e, :, q] = energy * m["coef"][2 + e, :, q]
                for c in range(3):
                    dot = dot + b16[3 * l + c, 1 + e, 0:8, q] * x0[3 * l + c, 1 + e, 0:8, q]
        sums[pl.ds(l, 1)] = jnp.sum(dot, axis=0, keepdims=True)
        sums[pl.ds(2 + l, 1)] = jnp.sum(curve, axis=0, keepdims=True)
        return carry

    lax.fori_loop(0, 2, energies, 0)

    ry, sy, rx = m["ry"], m["sy"], m["rx"]
    group(lambda dx, dy: sums, ry, [(0, k) for k in range(1, NY)], 2)
    for x in range(4):
        one, two = rt[0, 2 + x], rt[1, 2 + x]
        yt[x] = jnp.where(
            (sub() < 2) | (sub() >= 6), one,
            jnp.where(sub() < 4, y_down(two, 2), y_up(two, 2)),
        )
    rt_lo, rt_hi = m["rt_lo"], m["rt_hi"]
    fourth = [
        message(yt.at[pl.ds(2, 2)], rt_lo.at[pl.ds(0, 2)], 1, 1),
        message(yt.at[pl.ds(2, 2)], rt_hi.at[pl.ds(0, 2)], 1, -1),
        message(yt.at[pl.ds(0, 2)], rt_lo.at[pl.ds(6, 2)], -1, 1),
        message(yt.at[pl.ds(0, 2)], rt_hi.at[pl.ds(6, 2)], -1, -1),
        message(rt.at[:, pl.ds(4, 2)], rt.at[:, pl.ds(0, 2)], 1, 0),
        message(rt.at[:, pl.ds(2, 2)], rt.at[:, pl.ds(6, 2)], -1, 0),
        message(yt, rt_lo.at[pl.ds(2, 4)], 0, 1),
        message(yt, rt_hi.at[pl.ds(2, 4)], 0, -1),
    ]
    for copy in fourth:
        copy.start()
    group_done(ry, group_recv, 2)
    total = sums[...]
    for k in range(NY - 1):
        total = total + ry[k]
    sy[...] = total
    group(lambda dx, dy: sy, rx, [(k, 0) for k in range(1, NX)], 3)

    for copy in fourth:
        copy.wait_recv()
    f16, fil = m["f16"], m["fil"]

    def filter_load(l, carry):
        def put(p, inner):
            hi, lo = rt_hi[p], rt_lo[p]
            moved = jnp.where(sub() < 4, y_up(hi, 2), y_down(lo, 2))
            plain = jnp.where(sub() < 4, hi, lo)
            halo = jnp.where((sub() >= 2) & (sub() < 6), 0.0, jnp.where(l == 0, plain, moved))
            both = jnp.concatenate([rt[l, p], halo], axis=0)
            here = rows0 * in_x(gx * BX + p - 2, NX * BX)
            f16[p] = jnp.where(here > 0.0, both, 0.0)
            return inner

        lax.fori_loop(0, 8, put, 0)

        def run(x, inner):
            fil[l, x] = filter_plane(lambda p: f16[p], x + 2)[0:8]
            return inner

        lax.fori_loop(0, 4, run, 0)
        return carry

    lax.fori_loop(0, 2, filter_load, 0)

    group_done(rx, group_recv, 3)
    total = sy[...]
    for k in range(NX - 1):
        total = total + rx[k]
    total = jnp.sum(total, axis=1, keepdims=True)
    steps = []
    line = iota((1, 128), 1)
    out = jnp.zeros((1, 128), F32)
    for l in range(2):
        dot, curve = total[l : l + 1], total[2 + l : 3 + l]
        step = dot / curve
        steps.append(step)
        out = jnp.where(line == l, step * dot * (1.0 / CELLS), out)
    comp[...] = out
    for x in range(4):
        sens[x] = fil[0, x] * (steps[0] * steps[0]) + fil[1, x] * (steps[1] * steps[1])
        for l in range(2):
            for c in range(3):
                disp[l, c, x] = x0[3 * l + c, 1 + x, 0:8] * steps[l]

    for copy in first + second + third + fourth:
        copy.wait_send()
    group_done(m["rs1"], group_send, 0)
    group_done(rb2, group_send, 1)
    group_done(ry, group_send, 2)
    group_done(rx, group_send, 3)


def per_device(density, passive_void_mask, support_node_mask, loaded_node_mask, traction):
    scratch = [
        pltpu.VMEM(shape, jnp.int32 if name in INTS else F32) for name, shape in SCRATCH.items()
    ]
    dma = pltpu.SemaphoreType.DMA
    displacement, sensitivity, compliance = pl.pallas_call(
        kernel,
        out_shape=(
            jax.ShapeDtypeStruct((2, 3, BX, BY, BZ), F32),
            jax.ShapeDtypeStruct((BX, BY, BZ), F32),
            jax.ShapeDtypeStruct((1, 128), F32),
        ),
        in_specs=[pl.BlockSpec(memory_space=pl.ANY)] * 5,
        out_specs=tuple(pl.BlockSpec(memory_space=pltpu.VMEM) for _ in range(3)),
        scratch_shapes=scratch
        + [dma((5,)), dma((N_SEMS,)), dma((N_SEMS,)), dma((4,)), dma((4,))],
        compiler_params=pltpu.CompilerParams(
            collective_id=0, has_side_effects=True, vmem_limit_bytes=40 * 2**20
        ),
    )(density, passive_void_mask, support_node_mask, loaded_node_mask, traction)
    return displacement, sensitivity, compliance[0, :2]


def solution(mesh):
    in_specs = (
        P("gx", "gy", None),
        P("gx", "gy", None),
        P("gx", "gy", None),
        P(None, "gx", "gy", None),
        P(None, None, "gx", "gy", None),
    )
    out_specs = (P(None, None, "gx", "gy", None), P("gx", "gy", None), P())
    return jax.shard_map(
        per_device, mesh=mesh, in_specs=in_specs, out_specs=out_specs, check_vma=False
    )
```

```python
import math

import jax
import jax.numpy as jnp
from jax import lax
from jax.experimental import pallas as pl
from jax.experimental.pallas import tpu as pltpu
from jax.sharding import PartitionSpec as P

NX, NY = 32, 8
BX, BY, BZ = 4, 8, 256
CELLS = NX * BX * NY * BY * BZ
F32 = jnp.float32

POISSON = 0.3
LAME1 = POISSON / ((1.0 + POISSON) * (1.0 - 2.0 * POISSON))
LAME2 = 1.0 / (2.0 * (1.0 + POISSON))
RATIO = LAME1 / LAME2
DIAG = (LAME1 + 4.0 * LAME2) / 9.0
EDGE = math.tanh(4.0)

R3_SLOTS = [(a, b) for a in range(-4, 6) for b in range(-2, 4) if (a, b) != (0, 0)]
S1_SLOTS = [(a, b) for a in range(-2, 3) for b in range(-1, 2) if (a, b) != (0, 0)]


def iota(shape, dim):
    return lax.broadcasted_iota(jnp.int32, shape, dim)


def weight(a, b, c):
    return max(3.0 - math.sqrt(a * a + b * b + c * c), 0.0)


def z_up(v, z, by=1):
    n = v.shape[1]
    return jnp.where(iota(v.shape, 1) % z < z - by, pltpu.roll(v, n - by, 1), 0.0)


def z_down(v, z, by=1):
    n = v.shape[1]
    return jnp.where(iota(v.shape, 1) % z >= by, pltpu.roll(v, by, 1), 0.0)


def y_up(v, by=1):
    return pltpu.roll(v, v.shape[0] - by, 0)


def y_down(v, by=1):
    return pltpu.roll(v, by, 0)


def mm(a, b):
    return jnp.dot(a, b, preferred_element_type=F32, precision=lax.Precision.HIGHEST)


def couple(a, s):
    def key(*dims):
        return tuple(1 if d in dims else 0 for d in range(3))

    f = [dict() for _ in range(3)]
    trace = RATIO * (a[0][key(0)] + a[1][key(1)] + a[2][key(2)])
    third = None if s is None else s * (1.0 / 3.0)

    def times(x, scale, k):
        if scale is None:
            return x if k == 1.0 else x * k
        return x * scale

    for i in range(3):
        f[i][key(i)] = times(trace + 2.0 * a[i][key(i)], s, 1.0)
    for i in range(3):
        for j in range(i + 1, 3):
            shear = times(a[i][key(j)] + a[j][key(i)], s, 1.0)
            f[i][key(j)] = shear
            f[j][key(i)] = shear
    for k in range(3):
        i, j = [d for d in range(3) if d != k]
        p, q = a[i][key(i, k)], a[j][key(j, k)]
        both = RATIO * (p + q)
        f[i][key(i, k)] = times(both + 3.0 * p, third, 1.0 / 3.0)
        f[j][key(j, k)] = times(both + 3.0 * q, third, 1.0 / 3.0)
    mixed = [a[i][key(*[d for d in range(3) if d != i])] for i in range(3)]
    total = mixed[0] + mixed[1] + mixed[2]
    for i in range(3):
        f[i][key(*[d for d in range(3) if d != i])] = times(mixed[i] + total, third, 1.0 / 3.0)
        bubble = a[i][(1, 1, 1)] * ((RATIO + 4.0) / 9.0)
        f[i][(1, 1, 1)] = bubble if s is None else bubble * s
    return f


HYZ = [(0, 0), (0, 1), (1, 0), (1, 1)]


def modes_of(low, high):
    a = [dict() for _ in range(3)]
    for c in range(3):
        for k, (hy, hz) in enumerate(HYZ):
            if k:
                a[c][(0, hy, hz)] = low[4 * c + k] + high[4 * c + k]
            a[c][(1, hy, hz)] = high[4 * c + k] - low[4 * c + k]
    return a


def spread_planes(x_ref, first, xoff, planes, g_ref, z, tiles):
    def body(p, carry):
        for c in range(3):
            v = x_ref[first + c, xoff + p]
            up = z_up(v, z)
            for hz, t in ((0, v + up), (1, up - v)):
                tu = y_up(t)
                for hy, g in ((0, t + tu), (1, tu - t)):
                    for tile in range(tiles):
                        r, q = tile_place(tile, v.shape[1])
                        g_ref[tile, p, 4 * c + 2 * hy + hz] = g[r : r + 8, q : q + 128]
        return carry

    lax.fori_loop(0, planes, body, 0, unroll=True)


def tile_place(tile, lanes):
    per = lanes // 128
    return 8 * (tile // per), 128 * (tile % per)


def element_planes(g_ref, h_ref, s_ref, soff, scale, elements, tiles, lanes):
    per = lanes // 128

    def over_tile(tile, carry):
        r = pl.multiple_of(8 * (tile // per), 8)
        q = pl.multiple_of(128 * (tile % per), 128)

        def body(e, held):
            low, acc = held[:12], held[12:]
            high = tuple(g_ref[tile, e + 1, k] for k in range(12))
            s = s_ref[soff + e, pl.ds(r, 8), pl.ds(q, 128)] * (scale * LAME2 / 16.0)
            f = couple(modes_of(low, high), s)
            fresh = []
            for c in range(3):
                for k, (hy, hz) in enumerate(HYZ):
                    fd = f[c][(1, hy, hz)]
                    if k:
                        fs = f[c][(0, hy, hz)]
                        h_ref[tile, e, 4 * c + k] = acc[4 * c + k] + (fs - fd)
                        fresh.append(fs + fd)
                    else:
                        h_ref[tile, e, 4 * c + k] = acc[4 * c + k] - fd
                        fresh.append(fd)
            return high + tuple(fresh)

        start = tuple(g_ref[tile, 0, k] for k in range(12))
        zeros = tuple(jnp.zeros((8, 128), F32) for _ in range(12))
        lax.fori_loop(0, elements, body, start + zeros, unroll=True)
        return carry

    lax.fori_loop(0, tiles, over_tile, 0)


def gather_nodes(h_ref, e, c, z, lanes):
    def load(k):
        rows = []
        for half in range(2):
            tiles = [h_ref[half * (lanes // 128) + q, e, 4 * c + k] for q in range(lanes // 128)]
            rows.append(tiles[0] if len(tiles) == 1 else jnp.concatenate(tiles, axis=1))
        return jnp.concatenate(rows, axis=0)

    t = []
    for hz in range(2):
        hs, hd = load(hz), load(2 + hz)
        t.append((hs - hd) + y_down(hs + hd))
    return (t[0] - t[1]) + z_down(t[0] + t[1], z)


def apply_level(x_ref, groups, xoff, s_ref, soff, scale, elements, g_ref, h_ref, z, lanes, use):
    tiles = 2 * lanes // 128

    def one(l, carry):
        spread_planes(x_ref, 3 * l, xoff, elements + 1, g_ref, z, tiles)
        element_planes(g_ref, h_ref, s_ref, soff, scale, elements, tiles, lanes)

        def nodes(e, inner):
            for c in range(3):
                use(3 * l + c, e, gather_nodes(h_ref, e, c, z, lanes))
            return inner

        lax.fori_loop(1, elements, nodes, 0, unroll=True)
        return carry

    lax.fori_loop(0, groups, one, 0)


def filter_plane(load, p):
    a = [load(p), load(p - 1) + load(p + 1), load(p - 2) + load(p + 2)]
    f = []
    for c in range(3):
        h = []
        for b in range(3):
            t = None
            for i in range(3):
                w = weight(i, b, c)
                if w > 0.0:
                    t = w * a[i] if t is None else t + w * a[i]
            h.append(t)
        out = h[0]
        if h[1] is not None:
            out = out + (y_up(h[1]) + y_down(h[1]))
        if h[2] is not None:
            out = out + (y_up(h[2], 2) + y_down(h[2], 2))
        f.append(out)
    z = f[0].shape[1]
    return (
        f[0]
        + (z_up(f[1], z) + z_down(f[1], z))
        + (z_up(f[2], z, 2) + z_down(f[2], z, 2))
    )


SCRATCH = dict(
    df=(12, 8, BZ), pf=(8, 8, BZ), bf=(7, 7, 8, BZ),
    sup=(4, 8, BZ), lod=(2, 4, 8, BZ), tra=(2, 3, 4, 8, BZ), pas=(4, 8, BZ),
    ya_up=(4, 8, BZ), ya_dn=(4, 8, BZ), yb_up=(4, 8, BZ), yb_dn=(2, 4, 8, BZ),
    ra_lo=(12, 8, BZ), ra_hi=(12, 8, BZ), rb_lo=(7, 8, BZ), rb_hi=(2, 7, 8, BZ),
    gden=(3, 16, BZ), d16=(12, 16, BZ), s16=(8, 16, BZ), coef=(8, 8, BZ),
    b16=(6, 7, 16, BZ), x0=(6, 7, 16, BZ), keep=(7, 16, BZ), invd=(7, 16, BZ),
    g=(4, 7, 12, 8, 128), h=(4, 6, 12, 8, 128), r0=(6, 4, 8, BZ),
    zl=(18, 8, BZ), zr=(18, 8, 128), zc=(2, 8, 128),
    pb=(6, 3, 8, 128), pbu=(3, 3, 8, 128), pbd=(3, 3, 8, 128),
    s1s=(2, 8, 128), rs1=(len(S1_SLOTS), 2, 8, 128),
    rd1=(2, 6, 3, 8, 128), rd2=(2, 6, 1, 8, 128),
    rp1=(3, 2, 3, 3, 8, 128), rp2=(2, 2, 3, 1, 8, 128),
    s1=(8, 16, 128), invd1=(7, 16, 128), b1=(6, 7, 16, 128), x1=(6, 7, 16, 128),
    g1=(2, 7, 12, 8, 128), h1=(2, 6, 12, 8, 128), r1=(6, 3, 16, 128),
    t2l=(4, 8, BZ), t2r=(4, 8, 128), t2=(8, 128), t2v=(4, 8, 128), rb2=(len(R3_SLOTS), 8, 128),
    s2=(10, 16, 128), invd2=(10, 16, 128), b2=(3, 10, 16, 128), x2=(3, 10, 16, 128),
    g2=(2, 10, 12, 8, 128), h2=(2, 9, 12, 8, 128),
    yy2=(12, 16, 128), w2=(12, 16, BZ), yy1=(30, 16, 128), v1=(30, 16, BZ),
    sums=(8, 128), ry=(7, 8, 128), sy=(8, 128), rx=(31, 8, 128),
    rt=(2, 8, 8, BZ), yt=(4, 8, BZ), rt_lo=(8, 8, BZ), rt_hi=(8, 8, BZ),
    f16=(8, 16, BZ), fil=(2, 4, 8, BZ),
)
INTS = ("sup", "lod", "pas")
NAMES = list(SCRATCH)
N_SEMS = 64


def kernel(dens, pas_in, sup_in, lod_in, tra_in, disp, sens, comp, *scratch):
    m = dict(zip(NAMES, scratch))
    load_sem, send_sem, recv_sem, group_send, group_recv, token = scratch[len(NAMES) :]
    gx, gy = lax.axis_index("gx"), lax.axis_index("gy")

    def device(ax, ay):
        return lax.rem(gx + ax + NX, NX), lax.rem(gy + ay + NY, NY)

    barrier = pltpu.get_barrier_semaphore()

    around = [(a, b) for a in (-1, 0, 1) for b in (-1, 0, 1) if (a, b) != (0, 0)]
    for ax, ay in around:
        pl.semaphore_signal(
            barrier, inc=1, device_id=device(ax, ay), device_id_type=pl.DeviceIdType.MESH
        )

    loads = [
        pltpu.make_async_copy(dens, m["df"].at[pl.ds(4, 4)], load_sem.at[0]),
        pltpu.make_async_copy(pas_in, m["pas"], load_sem.at[1]),
        pltpu.make_async_copy(sup_in, m["sup"], load_sem.at[2]),
        pltpu.make_async_copy(lod_in, m["lod"], load_sem.at[3]),
        pltpu.make_async_copy(tra_in, m["tra"], load_sem.at[4]),
    ]
    for copy in loads:
        copy.start()

    counter = [0]

    def message(src, dst, ax, ay):
        k = counter[0]
        counter[0] += 1
        return pltpu.make_async_remote_copy(
            src_ref=src, dst_ref=dst, send_sem=send_sem.at[k], recv_sem=recv_sem.at[k],
            device_id=device(ax, ay), device_id_type=pl.DeviceIdType.MESH,
        )

    def sub(z=BZ):
        return iota((8, z), 0)

    def inside(cond):
        return jnp.where(cond, 1.0, 0.0).astype(F32)

    def in_x(x, size):
        return inside((x >= 0) & (x < size))

    row16 = iota((16, BZ), 0)
    y0 = gy * BY + jnp.where(row16 < 12, row16, row16 - 16)
    rows0 = inside((y0 >= 0) & (y0 < NY * BY))
    row16h = iota((16, 128), 0)
    y1 = gy * 4 + jnp.where(row16h < 8, row16h, row16h - 16)
    rows1 = inside((y1 >= 0) & (y1 < NY * 4))
    y2 = gy * 2 + jnp.where(row16h < 8, row16h, row16h - 16)
    rows2 = inside((y2 >= 0) & (y2 < NY * 2))

    def in_y(y):
        return inside((y >= 0) & (y < NY * BY))

    zi = iota((16, BZ), 1)
    cz = [None] + [inside(zi >= d) + inside(zi < BZ - d) for d in (1, 2)]
    cy = [None] + [in_y(y0 - d) + in_y(y0 + d) for d in (1, 2)]
    for a in range(3):
        total = None
        for b in range(3):
            w = weight(a, b, 0) + weight(a, b, 1) * cz[1]
            if weight(a, b, 2) > 0.0:
                w = w + weight(a, b, 2) * cz[2]
            w = w if b == 0 else w * cy[b]
            total = w if total is None else total + w
        m["gden"][a] = total

    loads[1].wait()
    loads[0].wait()
    df, pf, bf = m["df"], m["pf"], m["bf"]
    for x in range(4):
        pf[2 + x] = 1.0 - m["pas"][x].astype(F32)
        p4 = y_down(pf[2 + x], 4)
        m["ya_up"][x] = jnp.where(sub() >= 4, df[4 + x], p4)
        m["ya_dn"][x] = jnp.where(sub() < 4, df[4 + x], p4)
    loads[2].wait()
    loads[3].wait()
    loads[4].wait()
    for x in range(4):
        kept = 1.0 - m["sup"][x].astype(F32)
        bf[6, 1 + x] = kept
        for l in range(2):
            mask = kept * m["lod"][l, x].astype(F32)
            for c in range(3):
                bf[3 * l + c, 1 + x] = mask * m["tra"][l, c, x]
        for f in range(7):
            v = bf[f, 1 + x]
            m["yb_up"][x, f : f + 1] = v[7:8]
            m["yb_dn"][0, x, f : f + 1] = v[0:1]
            m["yb_dn"][1, x, f : f + 1] = v[1:2]
        m["yb_up"][x, 7:8] = jnp.zeros((1, BZ), F32)
        m["yb_dn"][0, x, 7:8] = jnp.zeros((1, BZ), F32)
        m["yb_dn"][1, x, 7:8] = jnp.zeros((1, BZ), F32)

    pl.semaphore_wait(barrier, len(around))

    ra_lo, ra_hi, rb_lo, rb_hi = m["ra_lo"], m["ra_hi"], m["rb_lo"], m["rb_hi"]
    own = df.at[pl.ds(4, 4)]
    first = [
        message(m["ya_up"], ra_lo.at[pl.ds(0, 4)], 1, 1),
        message(m["ya_dn"], ra_hi.at[pl.ds(0, 4)], 1, -1),
        message(m["ya_up"], ra_lo.at[pl.ds(8, 4)], -1, 1),
        message(m["ya_dn"], ra_hi.at[pl.ds(8, 4)], -1, -1),
        message(own, df.at[pl.ds(0, 4)], 1, 0),
        message(own, df.at[pl.ds(8, 4)], -1, 0),
        message(pf.at[pl.ds(4, 2)], pf.at[pl.ds(0, 2)], 1, 0),
        message(pf.at[pl.ds(2, 2)], pf.at[pl.ds(6, 2)], -1, 0),
        message(m["ya_up"], ra_lo.at[pl.ds(4, 4)], 0, 1),
        message(m["ya_dn"], ra_hi.at[pl.ds(4, 4)], 0, -1),
    ]
    second = [
        message(m["yb_up"].at[pl.ds(3, 1)], rb_lo.at[pl.ds(0, 1)], 1, 1),
        message(m["yb_dn"].at[:, pl.ds(3, 1)], rb_hi.at[:, pl.ds(0, 1)], 1, -1),
        message(m["yb_up"].at[pl.ds(0, 2)], rb_lo.at[pl.ds(5, 2)], -1, 1),
        message(m["yb_dn"].at[:, pl.ds(0, 2)], rb_hi.at[:, pl.ds(5, 2)], -1, -1),
        message(bf.at[:, pl.ds(4, 1)], bf.at[:, pl.ds(0, 1)], 1, 0),
        message(bf.at[:, pl.ds(1, 2)], bf.at[:, pl.ds(5, 2)], -1, 0),
        message(m["yb_up"], rb_lo.at[pl.ds(1, 4)], 0, 1),
        message(m["yb_dn"], rb_hi.at[:, pl.ds(1, 4)], 0, -1),
    ]
    for copy in first + second:
        copy.start()
    for copy in first:
        copy.wait_recv()

    d16, s16 = m["d16"], m["s16"]

    def put_density(p, carry):
        halo = jnp.where(sub() < 4, ra_hi[p], ra_lo[p])
        both = jnp.concatenate([df[p], halo], axis=0)
        here = in_x(gx * BX + p - 4, NX * BX)
        d16[p] = jnp.where(rows0 * here > 0.0, both, 0.0)
        return carry

    lax.fori_loop(0, 12, put_density, 0, unroll=True)

    def stiffen(i, carry):
        x = gx * BX + i - 2
        number = filter_plane(lambda p: d16[p], i + 2)
        cx1 = in_x(x - 1, NX * BX) + in_x(x + 1, NX * BX)
        cx2 = in_x(x - 2, NX * BX) + in_x(x + 2, NX * BX)
        denom = m["gden"][0] + cx1 * m["gden"][1] + cx2 * m["gden"][2]
        level = jnp.tanh(8.0 * (number / denom - 0.5))
        slope = (1.0 - level * level) * (8.0 / (2.0 * EDGE))
        halo = pltpu.roll(jnp.where(sub() >= 4, ra_hi[i + 2], ra_lo[i + 2]), 4, 0)
        solid = jnp.concatenate([pf[i], halo], axis=0)
        phys = solid * ((EDGE + level) * (1.0 / (2.0 * EDGE)))
        stiff = 0.001 + 0.999 * (phys * phys * phys)
        s16[i] = jnp.where(rows0 * in_x(x, NX * BX) > 0.0, stiff, 0.0)
        coef = -3.0 * 0.999 * (phys * phys) * solid * slope / denom
        m["coef"][i] = coef[0:8]
        return carry

    lax.fori_loop(0, 8, stiffen, 0, unroll=True)

    zi2, zo2 = iota((BZ, 128), 0), iota((BZ, 128), 1)
    pairs_z = inside(zi2 // 2 == zo2) * 0.125
    flat = jnp.concatenate([(s16[2 + 2 * i] + s16[3 + 2 * i])[0:8] for i in range(2)], axis=0)
    flat = mm(flat, pairs_z)
    for i in range(2):
        v = flat[8 * i : 8 * i + 8]
        m["zc"][i] = v + y_up(v)
        half = m["zc"][i, pl.ds(0, 4, stride=2)]
        m["s1s"][i, 0:4] = half
        m["s1s"][i, 4:8] = half

    def group(src, dst, slots, k):
        for n, (dx, dy) in enumerate(slots):
            pltpu.make_async_remote_copy(
                src_ref=src(dx, dy), dst_ref=dst.at[n], send_sem=group_send.at[k],
                recv_sem=group_recv.at[k], device_id=device(-dx, -dy),
                device_id_type=pl.DeviceIdType.MESH,
            ).start()

    def group_done(dst, sem, k):
        pltpu.make_async_copy(dst, dst, sem.at[k]).wait()

    group(lambda dx, dy: m["s1s"], m["rs1"], S1_SLOTS, 0)

    for copy in second:
        copy.wait_recv()

    x0, b16, keep, invd = m["x0"], m["b16"], m["keep"], m["invd"]

    def halo_rows(p, f):
        lo = rb_lo[p, f : f + 1]
        hi0, hi1 = rb_hi[0, p, f : f + 1], rb_hi[1, p, f : f + 1]
        return jnp.where(
            sub() == 7, lo, jnp.where(sub() == 0, hi0, jnp.where(sub() == 1, hi1, 0.0))
        )

    def begin(p, carry):
        x = gx * BX + p - 1
        t = s16[p] + s16[p + 1]
        t = t + y_down(t)
        t = t + z_down(t, BZ)
        here = rows0 * in_x(x, NX * BX)
        kept = here * jnp.concatenate([bf[6, p], halo_rows(p, 6)], axis=0)
        inv = jnp.where(here > 0.0, kept * (0.5 / DIAG) / t, 0.0)
        keep[p] = kept
        invd[p] = inv
        for f in range(6):
            b = jnp.concatenate([bf[f, p], halo_rows(p, f)], axis=0)
            b16[f, p] = b
            x0[f, p] = inv * b
        return carry

    lax.fori_loop(0, 7, begin, 0, unroll=True)

    def residual(f, e, image):
        m["r0"][f, e - 1] = keep[e, 0:8] * (b16[f, e, 0:8] - image[0:8])

    apply_level(x0, 2, 0, s16, 1, 1.0, 5, m["g"], m["h"], BZ, BZ, residual)

    near = jnp.abs(zi2 - 2 * zo2)
    rest_z = jnp.where(near == 0, 1.0, jnp.where(near == 1, 0.5, 0.0)).astype(F32)

    def rest_x(f, carry):
        r = [m["r0"][f, x] for x in range(4)]
        m["zl"][3 * f] = r[0] + 0.5 * r[1]
        m["zl"][3 * f + 1] = 0.5 * (r[1] + r[3]) + r[2]
        m["zl"][3 * f + 2] = 0.5 * r[3]
        return carry

    lax.fori_loop(0, 6, rest_x, 0, unroll=True)
    flat = mm(m["zl"][...].reshape(144, BZ), rest_z)
    m["zr"][...] = flat.reshape(18, 8, 128)
    pb, pbu, pbd = m["pb"], m["pbu"], m["pbd"]
    sh = sub(128)

    def rest_y(f, carry):
        for i in range(3):
            v = m["zr"][3 * f + i]
            low = jnp.where(sh > 0, y_down(v), 0.0)
            m["zr"][3 * f + i] = v + 0.5 * (low + y_up(v))
            pb[f, i] = jnp.zeros((8, 128), F32)
            pb[f, i, 0:4] = m["zr"][3 * f + i, pl.ds(0, 4, stride=2)]
            pb[f, i, 4:5] = 0.5 * v[7:8]
        return carry

    lax.fori_loop(0, 6, rest_y, 0, unroll=True)

    def pack_y(c, carry):
        for i in range(3):
            one, two = pb[c, i], pb[3 + c, i]
            turned = y_down(one, 4)
            pbu[c, i] = jnp.where(
                (sh >= 6) | (sh == 0), turned, jnp.where((sh >= 2) & (sh <= 4), two, 0.0)
            )
            pbd[c, i] = jnp.where((sh >= 4) & (sh <= 6), turned, jnp.where(sh < 3, two, 0.0))
        return carry

    lax.fori_loop(0, 3, pack_y, 0, unroll=True)

    rd1, rd2, rp1, rp2 = m["rd1"], m["rd2"], m["rp1"], m["rp2"]

    def part(ref, lo, n):
        return ref.at[:, pl.ds(lo, n)]

    third = [
        message(part(pbu, 2, 1), rp2.at[0, 0], 2, 1),
        message(part(pbd, 2, 1), rp2.at[0, 1], 2, -1),
        message(part(pb, 2, 1), rd2.at[0], 2, 0),
        message(part(pbu, 0, 1), rp2.at[1, 0], -2, 1),
        message(part(pbd, 0, 1), rp2.at[1, 1], -2, -1),
        message(part(pb, 0, 1), rd2.at[1], -2, 0),
        message(pbu, rp1.at[0, 0], 1, 1),
        message(pbd, rp1.at[0, 1], 1, -1),
        message(pb, rd1.at[0], 1, 0),
        message(pbu, rp1.at[2, 0], -1, 1),
        message(pbd, rp1.at[2, 1], -1, -1),
        message(pb, rd1.at[1], -1, 0),
        message(pbu, rp1.at[1, 0], 0, 1),
        message(pbd, rp1.at[1, 1], 0, -1),
    ]
    rs1 = m["rs1"]
    group_done(rs1, group_recv, 0)
    for copy in third:
        copy.start()

    s1, invd1 = m["s1"], m["invd1"]
    for p in range(8):
        x = p - 3
        dx, i = x // 2, x % 2
        mid = m["s1s"][i] if dx == 0 else rs1[S1_SLOTS.index((dx, 0)), i]
        top = rs1[S1_SLOTS.index((dx, 1)), i]
        low = rs1[S1_SLOTS.index((dx, -1)), i]
        frame = jnp.concatenate(
            [jnp.where(sh < 4, mid, top), jnp.where(sh >= 4, low, 0.0)], axis=0
        )
        here = rows1 * in_x(gx * 2 + x, NX * 2)
        s1[p] = jnp.where(here > 0.0, frame, 0.0)

    def diag1(p, carry):
        t = s1[p] + s1[p + 1]
        t = t + y_down(t)
        t = t + z_down(t, 128)
        here = rows1 * in_x(gx * 2 + p - 2, NX * 2)
        invd1[p] = jnp.where(here > 0.0, (0.5 / (2.0 * DIAG)) / t, 0.0)
        return carry

    lax.fori_loop(0, 7, diag1, 0, unroll=True)

    zi1, zo1 = iota((128, 128), 0), iota((128, 128), 1)
    pairs_2 = inside(zi1 // 2 == zo1 % 64) * 0.125
    t2l, t2r, t2 = m["t2l"], m["t2r"], m["t2"]
    own2 = s1[3] + s1[4]
    below2 = s1[1] + s1[2]
    wide = mm(jnp.concatenate([own2 + y_up(own2), below2 + y_up(below2)], axis=0), pairs_2)
    w_own, w_sum = wide[0:16], wide[0:16] + wide[16:32]
    dg = w_sum + y_down(w_sum, 2)
    dg = dg + z_down(dg, 64)
    dg = jnp.where(dg > 0.0, (0.5 / (4.0 * DIAG)) / dg, 0.0)
    t2r[3] = jnp.where(iota((8, 128), 1) < 64, w_own[0:8], dg[0:8])
    t2[6:8] = t2r[3, pl.ds(0, 2, stride=2)]

    for copy in third:
        copy.wait_recv()

    b1, x1 = m["b1"], m["x1"]
    okx = {d: (gx + d >= 0) & (gx + d < NX) for d in range(-2, 3)}
    oky = {d: (gy + d >= 0) & (gy + d < NY) for d in range(-1, 2)}

    def share(dx, dy, index, i):
        if dx == 0 and dy == 0:
            return pb[index, i]
        if dy == 0:
            v = rd1[0 if dx < 0 else 1, index, i] if abs(dx) == 1 else rd2[0 if dx < 0 else 1, index, 0]
        else:
            k = 0 if dy < 0 else 1
            v = rp1[dx + 1, k, index, i] if abs(dx) < 2 else rp2[0 if dx < 0 else 1, k, index, 0]
        return jnp.where(okx[dx] & oky[dy], v, 0.0)

    def sources(x):
        return [(dx, x - 2 * dx) for dx in range(-2, 3) if 0 <= x - 2 * dx <= 2 and (abs(dx) < 2 or (dx, x) in ((-2, -2), (2, 4)))]

    def right_side_1(c, carry):
        for p in range(7):
            x = p - 2
            up = down = None
            for dx, i in sources(x):
                u, d = share(dx, -1, c, i), share(dx, 1, c, i)
                up = u if up is None else up + u
                down = d if down is None else down + d
            for l in range(2):
                mid = None
                for dx, i in sources(x):
                    v = share(dx, 0, 3 * l + c, i)
                    mid = v if mid is None else mid + v
                if l == 1:
                    up, down = y_down(up, 4), y_down(down, 4)
                tile0 = mid + jnp.where(sh == 0, up, jnp.where((sh >= 4) & (sh <= 6), down, 0.0))
                tile1 = jnp.where(sh >= 6, up, 0.0)
                v = jnp.concatenate([tile0, tile1], axis=0)
                b1[3 * l + c, p] = v
                x1[3 * l + c, p] = invd1[p] * v
        return carry

    lax.fori_loop(0, 3, right_side_1, 0)

    def residual_1(f, e, image):
        m["r1"][f, e - 1] = b1[f, e] - image

    apply_level(x1, 2, 0, s1, 1, 2.0, 4, m["g1"], m["h1"], 128, 128, residual_1)

    for c in range(3):
        sides = []
        for l in range(2):
            r = [m["r1"][3 * l + c, x] for x in range(3)]
            v = r[1] + 0.5 * (r[0] + r[2])
            v = v + 0.5 * (y_up(v) + y_down(v))
            sides.append(v[0:8])
        t2l[c] = jnp.concatenate(sides, axis=1)
    t2l[3] = jnp.zeros((8, BZ), F32)
    near = jnp.abs(zi2 % 128 - 2 * (zo2 % 64))
    rest_2 = jnp.where(near == 0, 1.0, jnp.where(near == 1, 0.5, 0.0)).astype(F32)
    rest_2 = jnp.where(zi2 // 128 == zo2 // 64, rest_2, 0.0)
    flat = mm(t2l[...].reshape(32, BZ), rest_2)
    for c in range(3):
        t2r[c] = flat[8 * c : 8 * c + 8]
        t2[2 * c : 2 * c + 2] = t2r[c, pl.ds(0, 2, stride=2)]
    for k in range(4):
        m["t2v"][k] = t2[...] if k == 0 else y_down(t2[...], 2 * k)

    rb2 = m["rb2"]
    group(lambda dx, dy: m["t2v"].at[dy % 4], rb2, R3_SLOTS, 1)
    group_done(rb2, group_recv, 1)
    for ax in (-8, 8):
        pl.semaphore_signal(
            token, inc=1, device_id=device(ax, 0), device_id_type=pl.DeviceIdType.MESH
        )

    s2, invd2, b2, x2 = m["s2"], m["invd2"], m["b2"], m["x2"]
    pair = sh // 2
    half = iota((16, 128), 1) < 64
    for p in range(10):
        dx = p - 4

        def tile(dy, dx=dx):
            if (dx, dy) == (0, 0):
                return m["t2v"][0]
            return rb2[R3_SLOTS.index((dx, dy))]

        high = [tile(dy) for dy in range(4)]
        low = [tile(dy) for dy in (-2, -1)]
        here = rows2 * in_x(gx + dx, NX)
        frames = []
        for c in (3, 0, 1, 2):
            t0 = high[0]
            for dy in range(1, 4):
                t0 = jnp.where(pair == (dy + c) % 4, high[dy], t0)
            t1 = jnp.where(
                pair == (2 + c) % 4, low[0], jnp.where(pair == (3 + c) % 4, low[1], 0.0)
            )
            if c:
                t0, t1 = y_up(t0, 2 * c), y_up(t1, 2 * c)
            frames.append(jnp.concatenate([t0, t1], axis=0))
        v = jnp.where(here > 0.0, frames[0], 0.0)
        turned = pltpu.roll(v, 64, 1)
        s2[p] = jnp.where(half, v, turned)
        inv = jnp.where(half, turned, v)
        invd2[p] = inv
        for c in range(3):
            b2[c, p] = frames[1 + c]
            x2[c, p] = inv * frames[1 + c]

    for sweep in range(3):

        def smooth_2(f, e, image, sweep=sweep):
            p = sweep + e
            x2[f, p] = x2[f, p] + invd2[p] * (b2[f, p] - image)

        apply_level(
            x2, 1, sweep, s2, sweep, 4.0, 9 - 2 * sweep, m["g2"], m["h2"], 64, 128, smooth_2
        )

    yy2, w2, yy1, v1 = m["yy2"], m["w2"], m["yy1"], m["v1"]

    def widen_2(p, carry):
        for c in range(3):
            v = x2[c, 3 + p]
            odd = 0.5 * (v + y_up(v))
            k = 4 * c + p
            yy2[k, 8:16] = jnp.zeros((8, 128), F32)
            yy2[k, pl.ds(0, 4, stride=2)] = v[0:4]
            yy2[k, pl.ds(1, 4, stride=2)] = odd[0:4]
            yy2[k, 14:15] = v[15:16]
            yy2[k, 15:16] = odd[15:16]
        return carry

    lax.fori_loop(0, 4, widen_2, 0, unroll=True)
    zi3, zo3 = iota((128, BZ), 0), iota((128, BZ), 1)
    near = jnp.abs(zo3 % 128 - 2 * (zi3 % 64))
    pro_2 = jnp.where(near == 0, 1.0, jnp.where(near == 1, 0.5, 0.0)).astype(F32)
    pro_2 = jnp.where(zi3 // 64 == zo3 // 128, pro_2, 0.0)
    w2[...] = mm(yy2[...].reshape(192, 128), pro_2).reshape(12, 16, BZ)
    for p in range(7):
        x = p - 2
        here = rows1 * in_x(gx * 2 + x, NX * 2)
        for c in range(3):
            k = 4 * c + x // 2 + 1
            v = w2[k] if x % 2 == 0 else 0.5 * (w2[k] + w2[k + 1])
            x1[c, p] = x1[c, p] + here * v[:, 0:128]
            x1[3 + c, p] = x1[3 + c, p] + here * v[:, 128:256]

    def smooth_1(f, e, image):
        x1[f, e] = x1[f, e] + invd1[e] * (b1[f, e] - image)

    apply_level(x1, 2, 0, s1, 1, 2.0, 6, m["g1"], m["h1"], 128, 128, smooth_1)

    def widen_1(f, carry):
        for p in range(5):
            v = x1[f, 1 + p]
            odd = 0.5 * (v + y_up(v))
            k = 5 * f + p
            yy1[k, 8:16] = jnp.zeros((8, 128), F32)
            yy1[k, pl.ds(0, 4, stride=2)] = v[0:4]
            yy1[k, pl.ds(1, 4, stride=2)] = odd[0:4]
            yy1[k, 8:9] = v[4:5]
            yy1[k, 9:10] = odd[4:5]
            yy1[k, 15:16] = odd[15:16]
        return carry

    lax.fori_loop(0, 6, widen_1, 0)
    near = jnp.abs(zo3 - 2 * zi3)
    pro_1 = jnp.where(near == 0, 1.0, jnp.where(near == 1, 0.5, 0.0)).astype(F32)

    def widen_z(f, carry):
        at = pl.ds(5 * f, 5)
        v1[at] = mm(yy1[at].reshape(80, 128), pro_1).reshape(5, 16, BZ)
        return carry

    lax.fori_loop(0, 6, widen_z, 0, unroll=True)

    def correct(f, carry):
        for p in range(7):
            x = p - 1
            k = 5 * f + x // 2 + 1
            v = v1[k] if x % 2 == 0 else 0.5 * (v1[k] + v1[k + 1])
            x0[f, p] = x0[f, p] + keep[p] * v
        return carry

    lax.fori_loop(0, 6, correct, 0)

    def smooth_0(f, e, image):
        x0[f, e] = x0[f, e] + invd[e] * (b16[f, e] - image)

    apply_level(x0, 2, 0, s16, 1, 1.0, 6, m["g"], m["h"], BZ, BZ, smooth_0)

    rt, yt, sums = m["rt"], m["yt"], m["sums"]
    sums[...] = jnp.zeros((8, 128), F32)

    def energies(l, carry):
        spread_planes(x0, 3 * l, 1, 5, m["g"], BZ, 2)
        curve = jnp.zeros((8, 128), F32)
        dot = jnp.zeros((8, 128), F32)
        for tile in range(2):
            q = pl.ds(128 * tile, 128)
            for e in range(4):
                low = [m["g"][tile, e, k] for k in range(12)]
                high = [m["g"][tile, e + 1, k] for k in range(12)]
                a = modes_of(low, high)
                f = couple(a, None)
                energy = None
                for c in range(3):
                    for k in a[c]:
                        t = a[c][k] * f[c][k]
                        energy = t if energy is None else energy + t
                energy = energy * (LAME2 / 16.0)
                curve = curve + energy * s16[2 + e, 0:8, q]
                rt[l, 2 + e, :, q] = energy * m["coef"][2 + e, :, q]
                for c in range(3):
                    dot = dot + b16[3 * l + c, 1 + e, 0:8, q] * x0[3 * l + c, 1 + e, 0:8, q]
        sums[pl.ds(l, 1)] = jnp.sum(dot, axis=0, keepdims=True)
        sums[pl.ds(2 + l, 1)] = jnp.sum(curve, axis=0, keepdims=True)
        return carry

    lax.fori_loop(0, 2, energies, 0)

    ry, sy, rx = m["ry"], m["sy"], m["rx"]
    group(lambda dx, dy: sums, ry, [(0, k) for k in range(1, NY)], 2)
    for x in range(4):
        one, two = rt[0, 2 + x], rt[1, 2 + x]
        yt[x] = jnp.where(
            (sub() < 2) | (sub() >= 6), one,
            jnp.where(sub() < 4, y_down(two, 2), y_up(two, 2)),
        )
    rt_lo, rt_hi = m["rt_lo"], m["rt_hi"]
    fourth = [
        message(yt.at[pl.ds(2, 2)], rt_lo.at[pl.ds(0, 2)], 1, 1),
        message(yt.at[pl.ds(2, 2)], rt_hi.at[pl.ds(0, 2)], 1, -1),
        message(yt.at[pl.ds(0, 2)], rt_lo.at[pl.ds(6, 2)], -1, 1),
        message(yt.at[pl.ds(0, 2)], rt_hi.at[pl.ds(6, 2)], -1, -1),
        message(rt.at[:, pl.ds(4, 2)], rt.at[:, pl.ds(0, 2)], 1, 0),
        message(rt.at[:, pl.ds(2, 2)], rt.at[:, pl.ds(6, 2)], -1, 0),
        message(yt, rt_lo.at[pl.ds(2, 4)], 0, 1),
        message(yt, rt_hi.at[pl.ds(2, 4)], 0, -1),
    ]
    for copy in fourth:
        copy.start()
    group_done(ry, group_recv, 2)
    total = sums[...]
    for k in range(NY - 1):
        total = total + ry[k]
    sy[...] = total
    pl.semaphore_wait(token, 2)
    group(lambda dx, dy: sy, rx, [(k, 0) for k in range(1, NX)], 3)

    for copy in fourth:
        copy.wait_recv()
    f16, fil = m["f16"], m["fil"]

    def filter_load(l, carry):
        def put(p, inner):
            hi, lo = rt_hi[p], rt_lo[p]
            moved = jnp.where(sub() < 4, y_up(hi, 2), y_down(lo, 2))
            plain = jnp.where(sub() < 4, hi, lo)
            halo = jnp.where((sub() >= 2) & (sub() < 6), 0.0, jnp.where(l == 0, plain, moved))
            both = jnp.concatenate([rt[l, p], halo], axis=0)
            here = rows0 * in_x(gx * BX + p - 2, NX * BX)
            f16[p] = jnp.where(here > 0.0, both, 0.0)
            return inner

        lax.fori_loop(0, 8, put, 0, unroll=True)

        def run(x, inner):
            fil[l, x] = filter_plane(lambda p: f16[p], x + 2)[0:8]
            return inner

        lax.fori_loop(0, 4, run, 0, unroll=True)
        return carry

    lax.fori_loop(0, 2, filter_load, 0)

    group_done(rx, group_recv, 3)
    total = sy[...]
    for k in range(NX - 1):
        total = total + rx[k]
    total = jnp.sum(total, axis=1, keepdims=True)
    steps = []
    line = iota((1, 128), 1)
    out = jnp.zeros((1, 128), F32)
    for l in range(2):
        dot, curve = total[l : l + 1], total[2 + l : 3 + l]
        step = dot / curve
        steps.append(step)
        out = jnp.where(line == l, step * dot * (1.0 / CELLS), out)
    comp[...] = out
    for x in range(4):
        sens[x] = fil[0, x] * (steps[0] * steps[0]) + fil[1, x] * (steps[1] * steps[1])
        for l in range(2):
            for c in range(3):
                disp[l, c, x] = x0[3 * l + c, 1 + x, 0:8] * steps[l]

    for copy in first + second + third + fourth:
        copy.wait_send()
    group_done(m["rs1"], group_send, 0)
    group_done(rb2, group_send, 1)
    group_done(ry, group_send, 2)
    group_done(rx, group_send, 3)


def per_device(density, passive_void_mask, support_node_mask, loaded_node_mask, traction):
    scratch = [
        pltpu.VMEM(shape, jnp.int32 if name in INTS else F32) for name, shape in SCRATCH.items()
    ]
    dma = pltpu.SemaphoreType.DMA
    displacement, sensitivity, compliance = pl.pallas_call(
        kernel,
        out_shape=(
            jax.ShapeDtypeStruct((2, 3, BX, BY, BZ), F32),
            jax.ShapeDtypeStruct((BX, BY, BZ), F32),
            jax.ShapeDtypeStruct((1, 128), F32),
        ),
        in_specs=[pl.BlockSpec(memory_space=pltpu.HBM)] * 5,
        out_specs=tuple(pl.BlockSpec(memory_space=pltpu.VMEM) for _ in range(3)),
        scratch_shapes=scratch
        + [dma((5,)), dma((N_SEMS,)), dma((N_SEMS,)), dma((4,)), dma((4,))]
        + [pltpu.SemaphoreType.REGULAR],
        compiler_params=pltpu.CompilerParams(
            collective_id=0, has_side_effects=True, vmem_limit_bytes=40 * 2**20
        ),
    )(density, passive_void_mask, support_node_mask, loaded_node_mask, traction)
    return displacement, sensitivity, compliance[0, :2]


def solution(mesh):
    in_specs = (
        P("gx", "gy", None),
        P("gx", "gy", None),
        P("gx", "gy", None),
        P(None, "gx", "gy", None),
        P(None, None, "gx", "gy", None),
    )
    out_specs = (P(None, None, "gx", "gy", None), P("gx", "gy", None), P())
    return jax.shard_map(
        per_device, mesh=mesh, in_specs=in_specs, out_specs=out_specs, check_vma=False
    )
```

```python
import math

import jax
import jax.numpy as jnp
from jax import lax
from jax.experimental import pallas as pl
from jax.experimental.pallas import tpu as pltpu
from jax.sharding import PartitionSpec as P

NX, NY = 32, 8
BX, BY, BZ = 4, 8, 256
CELLS = NX * BX * NY * BY * BZ
F32 = jnp.float32

POISSON = 0.3
LAME1 = POISSON / ((1.0 + POISSON) * (1.0 - 2.0 * POISSON))
LAME2 = 1.0 / (2.0 * (1.0 + POISSON))
RATIO = LAME1 / LAME2
DIAG = (LAME1 + 4.0 * LAME2) / 9.0
EDGE = math.tanh(4.0)


def far(slot):
    dx, dy = slot
    hops = 0
    for x in range(4):
        ring = abs((x + dx) % 4 - x)
        hops += min(ring, 4 - ring) + abs((x + dx) // 4)
    for core in range(2):
        hops += 2 * abs((core + dy) // 2)
    return -hops


R3_SLOTS = [(a, b) for a in range(-4, 6) for b in range(-2, 4) if (a, b) != (0, 0)]
R3_SLOTS.sort(key=far)
S1_SLOTS = [(a, b) for a in range(-2, 3) for b in range(-1, 2) if (a, b) != (0, 0)]


def iota(shape, dim):
    return lax.broadcasted_iota(jnp.int32, shape, dim)


def weight(a, b, c):
    return max(3.0 - math.sqrt(a * a + b * b + c * c), 0.0)


def z_up(v, z, by=1):
    n = v.shape[1]
    return jnp.where(iota(v.shape, 1) % z < z - by, pltpu.roll(v, n - by, 1), 0.0)


def z_down(v, z, by=1):
    n = v.shape[1]
    return jnp.where(iota(v.shape, 1) % z >= by, pltpu.roll(v, by, 1), 0.0)


def y_up(v, by=1):
    return pltpu.roll(v, v.shape[0] - by, 0)


def y_down(v, by=1):
    return pltpu.roll(v, by, 0)


def mm(a, b):
    return jnp.dot(a, b, preferred_element_type=F32, precision=lax.Precision.HIGHEST)


def couple(a, s):
    def key(*dims):
        return tuple(1 if d in dims else 0 for d in range(3))

    f = [dict() for _ in range(3)]
    trace = RATIO * (a[0][key(0)] + a[1][key(1)] + a[2][key(2)])
    third = None if s is None else s * (1.0 / 3.0)

    def times(x, scale, k):
        if scale is None:
            return x if k == 1.0 else x * k
        return x * scale

    for i in range(3):
        f[i][key(i)] = times(trace + 2.0 * a[i][key(i)], s, 1.0)
    for i in range(3):
        for j in range(i + 1, 3):
            shear = times(a[i][key(j)] + a[j][key(i)], s, 1.0)
            f[i][key(j)] = shear
            f[j][key(i)] = shear
    for k in range(3):
        i, j = [d for d in range(3) if d != k]
        p, q = a[i][key(i, k)], a[j][key(j, k)]
        both = RATIO * (p + q)
        f[i][key(i, k)] = times(both + 3.0 * p, third, 1.0 / 3.0)
        f[j][key(j, k)] = times(both + 3.0 * q, third, 1.0 / 3.0)
    mixed = [a[i][key(*[d for d in range(3) if d != i])] for i in range(3)]
    total = mixed[0] + mixed[1] + mixed[2]
    for i in range(3):
        f[i][key(*[d for d in range(3) if d != i])] = times(mixed[i] + total, third, 1.0 / 3.0)
        bubble = a[i][(1, 1, 1)] * ((RATIO + 4.0) / 9.0)
        f[i][(1, 1, 1)] = bubble if s is None else bubble * s
    return f


HYZ = [(0, 0), (0, 1), (1, 0), (1, 1)]


def modes_of(low, high):
    a = [dict() for _ in range(3)]
    for c in range(3):
        for k, (hy, hz) in enumerate(HYZ):
            if k:
                a[c][(0, hy, hz)] = low[4 * c + k] + high[4 * c + k]
            a[c][(1, hy, hz)] = high[4 * c + k] - low[4 * c + k]
    return a


def spread_planes(x_ref, first, xoff, planes, g_ref, z, tiles):
    def body(p, carry):
        for c in range(3):
            v = x_ref[first + c, xoff + p]
            up = z_up(v, z)
            for hz, t in ((0, v + up), (1, up - v)):
                tu = y_up(t)
                for hy, g in ((0, t + tu), (1, tu - t)):
                    for tile in range(tiles):
                        r, q = tile_place(tile, v.shape[1])
                        g_ref[tile, p, 4 * c + 2 * hy + hz] = g[r : r + 8, q : q + 128]
        return carry

    lax.fori_loop(0, planes, body, 0, unroll=True)


def tile_place(tile, lanes):
    per = lanes // 128
    return 8 * (tile // per), 128 * (tile % per)


def element_planes(g_ref, h_ref, s_ref, soff, scale, elements, tiles, lanes):
    per = lanes // 128

    def over_tile(tile, carry):
        r = pl.multiple_of(8 * (tile // per), 8)
        q = pl.multiple_of(128 * (tile % per), 128)

        def body(e, held):
            low, acc = held[:12], held[12:]
            high = tuple(g_ref[tile, e + 1, k] for k in range(12))
            s = s_ref[soff + e, pl.ds(r, 8), pl.ds(q, 128)] * (scale * LAME2 / 16.0)
            f = couple(modes_of(low, high), s)
            fresh = []
            for c in range(3):
                for k, (hy, hz) in enumerate(HYZ):
                    fd = f[c][(1, hy, hz)]
                    if k:
                        fs = f[c][(0, hy, hz)]
                        h_ref[tile, e, 4 * c + k] = acc[4 * c + k] + (fs - fd)
                        fresh.append(fs + fd)
                    else:
                        h_ref[tile, e, 4 * c + k] = acc[4 * c + k] - fd
                        fresh.append(fd)
            return high + tuple(fresh)

        start = tuple(g_ref[tile, 0, k] for k in range(12))
        zeros = tuple(jnp.zeros((8, 128), F32) for _ in range(12))
        lax.fori_loop(0, elements, body, start + zeros, unroll=True)
        return carry

    lax.fori_loop(0, tiles, over_tile, 0)


def gather_nodes(h_ref, e, c, z, lanes):
    def load(k):
        rows = []
        for half in range(2):
            tiles = [h_ref[half * (lanes // 128) + q, e, 4 * c + k] for q in range(lanes // 128)]
            rows.append(tiles[0] if len(tiles) == 1 else jnp.concatenate(tiles, axis=1))
        return jnp.concatenate(rows, axis=0)

    t = []
    for hz in range(2):
        hs, hd = load(hz), load(2 + hz)
        t.append((hs - hd) + y_down(hs + hd))
    return (t[0] - t[1]) + z_down(t[0] + t[1], z)


def apply_level(x_ref, groups, xoff, s_ref, soff, scale, elements, g_ref, h_ref, z, lanes, use):
    tiles = 2 * lanes // 128

    def one(l, carry):
        spread_planes(x_ref, 3 * l, xoff, elements + 1, g_ref, z, tiles)
        element_planes(g_ref, h_ref, s_ref, soff, scale, elements, tiles, lanes)

        def nodes(e, inner):
            for c in range(3):
                use(3 * l + c, e, gather_nodes(h_ref, e, c, z, lanes))
            return inner

        lax.fori_loop(1, elements, nodes, 0, unroll=True)
        return carry

    lax.fori_loop(0, groups, one, 0)


def filter_plane(load, p):
    a = [load(p), load(p - 1) + load(p + 1), load(p - 2) + load(p + 2)]
    f = []
    for c in range(3):
        h = []
        for b in range(3):
            t = None
            for i in range(3):
                w = weight(i, b, c)
                if w > 0.0:
                    t = w * a[i] if t is None else t + w * a[i]
            h.append(t)
        out = h[0]
        if h[1] is not None:
            out = out + (y_up(h[1]) + y_down(h[1]))
        if h[2] is not None:
            out = out + (y_up(h[2], 2) + y_down(h[2], 2))
        f.append(out)
    z = f[0].shape[1]
    return (
        f[0]
        + (z_up(f[1], z) + z_down(f[1], z))
        + (z_up(f[2], z, 2) + z_down(f[2], z, 2))
    )


SCRATCH = dict(
    df=(12, 8, BZ), pf=(8, 8, BZ), bf=(7, 7, 8, BZ),
    sup=(4, 8, BZ), lod=(2, 4, 8, BZ), tra=(2, 3, 4, 8, BZ), pas=(4, 8, BZ),
    ya_up=(4, 8, BZ), ya_dn=(4, 8, BZ), yb_up=(4, 8, BZ), yb_dn=(2, 4, 8, BZ),
    ra_lo=(12, 8, BZ), ra_hi=(12, 8, BZ), rb_lo=(7, 8, BZ), rb_hi=(2, 7, 8, BZ),
    gden=(3, 16, BZ), d16=(12, 16, BZ), s16=(8, 16, BZ), coef=(8, 8, BZ),
    b16=(6, 7, 16, BZ), x0=(6, 7, 16, BZ), keep=(7, 16, BZ), invd=(7, 16, BZ),
    g=(4, 7, 12, 8, 128), h=(4, 6, 12, 8, 128), r0=(6, 4, 8, BZ),
    zl=(18, 8, BZ), zr=(18, 8, 128), zc=(2, 8, 128),
    pb=(6, 3, 8, 128), pbp=(4, 3, 8, 128), pbu=(3, 3, 8, 128), pbd=(3, 8, 128),
    pbe=(3, 3, 8, 128),
    s1s=(2, 8, 128), rs1=(len(S1_SLOTS), 2, 8, 128),
    rp=(5, 4, 3, 8, 128), ru=(5, 3, 3, 8, 128), rd=(5, 3, 8, 128), re=(5, 3, 3, 8, 128),
    s1=(8, 16, 128), invd1=(7, 16, 128), b1=(6, 7, 16, 128), x1=(6, 7, 16, 128),
    g1=(2, 7, 12, 8, 128), h1=(2, 6, 12, 8, 128), r1=(6, 3, 16, 128),
    t2l=(4, 8, BZ), t2r=(4, 8, 128), t2=(8, 128), t2v=(4, 8, 128), rb2=(len(R3_SLOTS), 8, 128),
    s2=(10, 16, 128), invd2=(10, 16, 128), b2=(3, 10, 16, 128), x2=(3, 10, 16, 128),
    g2=(2, 10, 12, 8, 128), h2=(2, 9, 12, 8, 128),
    yy2=(12, 16, 128), w2=(12, 16, BZ), yy1=(30, 16, 128), v1=(30, 16, BZ),
    sums=(1, 128), rc=(1, 128), sc=(1, 128), rx=(127, 1, 128),
    rt=(2, 8, 8, BZ), yt=(4, 8, BZ), rt_lo=(8, 8, BZ), rt_hi=(8, 8, BZ),
    f16=(8, 16, BZ), fil=(2, 4, 8, BZ),
)
INTS = ("sup", "lod", "pas")
NAMES = list(SCRATCH)
N_SEMS = 64


def kernel(dens, pas_in, sup_in, lod_in, tra_in, pre_out, fil_out, scal_out, *scratch):
    m = dict(zip(NAMES, scratch))
    load_sem, send_sem, recv_sem, group_send, group_recv, out_sem, token = scratch[len(NAMES) :]
    gx, gy = lax.axis_index("gx"), lax.axis_index("gy")

    def device(ax, ay):
        return lax.rem(gx + ax + NX, NX), lax.rem(gy + ay + NY, NY)

    barrier = pltpu.get_barrier_semaphore()

    around = [(a, b) for a in (-1, 0, 1) for b in (-1, 0, 1) if (a, b) != (0, 0)]
    for ax, ay in around:
        pl.semaphore_signal(
            barrier, inc=1, device_id=device(ax, ay), device_id_type=pl.DeviceIdType.MESH
        )

    loads = [
        pltpu.make_async_copy(dens, m["df"].at[pl.ds(4, 4)], load_sem.at[0]),
        pltpu.make_async_copy(pas_in, m["pas"], load_sem.at[1]),
        pltpu.make_async_copy(sup_in, m["sup"], load_sem.at[2]),
        pltpu.make_async_copy(lod_in, m["lod"], load_sem.at[3]),
        pltpu.make_async_copy(tra_in, m["tra"], load_sem.at[4]),
    ]
    for copy in loads:
        copy.start()

    counter = [0]

    def message(src, dst, ax, ay):
        k = counter[0]
        counter[0] += 1
        return pltpu.make_async_remote_copy(
            src_ref=src, dst_ref=dst, send_sem=send_sem.at[k], recv_sem=recv_sem.at[k],
            device_id=device(ax, ay), device_id_type=pl.DeviceIdType.MESH,
        )

    def sub(z=BZ):
        return iota((8, z), 0)

    def inside(cond):
        return jnp.where(cond, 1.0, 0.0).astype(F32)

    def in_x(x, size):
        return inside((x >= 0) & (x < size))

    row16 = iota((16, BZ), 0)
    y0 = gy * BY + jnp.where(row16 < 12, row16, row16 - 16)
    rows0 = inside((y0 >= 0) & (y0 < NY * BY))
    row16h = iota((16, 128), 0)
    y1 = gy * 4 + jnp.where(row16h < 8, row16h, row16h - 16)
    rows1 = inside((y1 >= 0) & (y1 < NY * 4))
    y2 = gy * 2 + jnp.where(row16h < 8, row16h, row16h - 16)
    rows2 = inside((y2 >= 0) & (y2 < NY * 2))

    def in_y(y):
        return inside((y >= 0) & (y < NY * BY))

    zi = iota((16, BZ), 1)
    cz = [None] + [inside(zi >= d) + inside(zi < BZ - d) for d in (1, 2)]
    cy = [None] + [in_y(y0 - d) + in_y(y0 + d) for d in (1, 2)]
    for a in range(3):
        total = None
        for b in range(3):
            w = weight(a, b, 0) + weight(a, b, 1) * cz[1]
            if weight(a, b, 2) > 0.0:
                w = w + weight(a, b, 2) * cz[2]
            w = w if b == 0 else w * cy[b]
            total = w if total is None else total + w
        m["gden"][a] = total

    loads[1].wait()
    loads[0].wait()
    df, pf, bf = m["df"], m["pf"], m["bf"]
    for x in range(4):
        pf[2 + x] = 1.0 - m["pas"][x].astype(F32)
        p4 = y_down(pf[2 + x], 4)
        m["ya_up"][x] = jnp.where(sub() >= 4, df[4 + x], p4)
        m["ya_dn"][x] = jnp.where(sub() < 4, df[4 + x], p4)
    loads[2].wait()
    loads[3].wait()
    loads[4].wait()
    for x in range(4):
        kept = 1.0 - m["sup"][x].astype(F32)
        bf[6, 1 + x] = kept
        for l in range(2):
            mask = kept * m["lod"][l, x].astype(F32)
            for c in range(3):
                bf[3 * l + c, 1 + x] = mask * m["tra"][l, c, x]
        for f in range(7):
            v = bf[f, 1 + x]
            m["yb_up"][x, f : f + 1] = v[7:8]
            m["yb_dn"][0, x, f : f + 1] = v[0:1]
            m["yb_dn"][1, x, f : f + 1] = v[1:2]
        m["yb_up"][x, 7:8] = jnp.zeros((1, BZ), F32)
        m["yb_dn"][0, x, 7:8] = jnp.zeros((1, BZ), F32)
        m["yb_dn"][1, x, 7:8] = jnp.zeros((1, BZ), F32)

    pl.semaphore_wait(barrier, len(around))

    ra_lo, ra_hi, rb_lo, rb_hi = m["ra_lo"], m["ra_hi"], m["rb_lo"], m["rb_hi"]
    own = df.at[pl.ds(4, 4)]
    first = [
        message(m["ya_up"], ra_lo.at[pl.ds(0, 4)], 1, 1),
        message(m["ya_dn"], ra_hi.at[pl.ds(0, 4)], 1, -1),
        message(m["ya_up"], ra_lo.at[pl.ds(8, 4)], -1, 1),
        message(m["ya_dn"], ra_hi.at[pl.ds(8, 4)], -1, -1),
        message(own, df.at[pl.ds(0, 4)], 1, 0),
        message(own, df.at[pl.ds(8, 4)], -1, 0),
        message(pf.at[pl.ds(4, 2)], pf.at[pl.ds(0, 2)], 1, 0),
        message(pf.at[pl.ds(2, 2)], pf.at[pl.ds(6, 2)], -1, 0),
        message(m["ya_up"], ra_lo.at[pl.ds(4, 4)], 0, 1),
        message(m["ya_dn"], ra_hi.at[pl.ds(4, 4)], 0, -1),
    ]
    second = [
        message(m["yb_up"].at[pl.ds(3, 1)], rb_lo.at[pl.ds(0, 1)], 1, 1),
        message(m["yb_dn"].at[:, pl.ds(3, 1)], rb_hi.at[:, pl.ds(0, 1)], 1, -1),
        message(m["yb_up"].at[pl.ds(0, 2)], rb_lo.at[pl.ds(5, 2)], -1, 1),
        message(m["yb_dn"].at[:, pl.ds(0, 2)], rb_hi.at[:, pl.ds(5, 2)], -1, -1),
        message(bf.at[:, pl.ds(4, 1)], bf.at[:, pl.ds(0, 1)], 1, 0),
        message(bf.at[:, pl.ds(1, 2)], bf.at[:, pl.ds(5, 2)], -1, 0),
        message(m["yb_up"], rb_lo.at[pl.ds(1, 4)], 0, 1),
        message(m["yb_dn"], rb_hi.at[:, pl.ds(1, 4)], 0, -1),
    ]
    for copy in first + second:
        copy.start()
    for copy in first:
        copy.wait_recv()

    d16, s16 = m["d16"], m["s16"]

    def put_density(p, carry):
        halo = jnp.where(sub() < 4, ra_hi[p], ra_lo[p])
        both = jnp.concatenate([df[p], halo], axis=0)
        here = in_x(gx * BX + p - 4, NX * BX)
        d16[p] = jnp.where(rows0 * here > 0.0, both, 0.0)
        return carry

    lax.fori_loop(0, 12, put_density, 0, unroll=True)

    def stiffen(i, carry):
        x = gx * BX + i - 2
        number = filter_plane(lambda p: d16[p], i + 2)
        cx1 = in_x(x - 1, NX * BX) + in_x(x + 1, NX * BX)
        cx2 = in_x(x - 2, NX * BX) + in_x(x + 2, NX * BX)
        denom = m["gden"][0] + cx1 * m["gden"][1] + cx2 * m["gden"][2]
        level = jnp.tanh(8.0 * (number / denom - 0.5))
        slope = (1.0 - level * level) * (8.0 / (2.0 * EDGE))
        halo = pltpu.roll(jnp.where(sub() >= 4, ra_hi[i + 2], ra_lo[i + 2]), 4, 0)
        solid = jnp.concatenate([pf[i], halo], axis=0)
        phys = solid * ((EDGE + level) * (1.0 / (2.0 * EDGE)))
        stiff = 0.001 + 0.999 * (phys * phys * phys)
        s16[i] = jnp.where(rows0 * in_x(x, NX * BX) > 0.0, stiff, 0.0)
        coef = -3.0 * 0.999 * (phys * phys) * solid * slope / denom
        m["coef"][i] = coef[0:8]
        return carry

    lax.fori_loop(0, 8, stiffen, 0, unroll=True)

    zi2, zo2 = iota((BZ, 128), 0), iota((BZ, 128), 1)
    pairs_z = inside(zi2 // 2 == zo2) * 0.125
    flat = jnp.concatenate([(s16[2 + 2 * i] + s16[3 + 2 * i])[0:8] for i in range(2)], axis=0)
    flat = mm(flat, pairs_z)
    for i in range(2):
        v = flat[8 * i : 8 * i + 8]
        m["zc"][i] = v + y_up(v)
        half = m["zc"][i, pl.ds(0, 4, stride=2)]
        m["s1s"][i, 0:4] = half
        m["s1s"][i, 4:8] = half

    def group(src, dst, slots, k):
        for n, (dx, dy) in enumerate(slots):
            pltpu.make_async_remote_copy(
                src_ref=src(dx, dy), dst_ref=dst.at[n], send_sem=group_send.at[k],
                recv_sem=group_recv.at[k], device_id=device(-dx, -dy),
                device_id_type=pl.DeviceIdType.MESH,
            ).start()

    def group_done(dst, sem, k):
        pltpu.make_async_copy(dst, dst, sem.at[k]).wait()

    group(lambda dx, dy: m["s1s"], m["rs1"], S1_SLOTS, 0)

    for copy in second:
        copy.wait_recv()

    x0, b16, keep, invd = m["x0"], m["b16"], m["keep"], m["invd"]

    def halo_rows(p, f):
        lo = rb_lo[p, f : f + 1]
        hi0, hi1 = rb_hi[0, p, f : f + 1], rb_hi[1, p, f : f + 1]
        return jnp.where(
            sub() == 7, lo, jnp.where(sub() == 0, hi0, jnp.where(sub() == 1, hi1, 0.0))
        )

    def begin(p, carry):
        x = gx * BX + p - 1
        t = s16[p] + s16[p + 1]
        t = t + y_down(t)
        t = t + z_down(t, BZ)
        here = rows0 * in_x(x, NX * BX)
        kept = here * jnp.concatenate([bf[6, p], halo_rows(p, 6)], axis=0)
        inv = jnp.where(here > 0.0, kept * (0.5 / DIAG) / t, 0.0)
        keep[p] = kept
        invd[p] = inv
        for f in range(6):
            b = jnp.concatenate([bf[f, p], halo_rows(p, f)], axis=0)
            b16[f, p] = b
            x0[f, p] = inv * b
        return carry

    lax.fori_loop(0, 7, begin, 0, unroll=True)

    def residual(f, e, image):
        m["r0"][f, e - 1] = keep[e, 0:8] * (b16[f, e, 0:8] - image[0:8])

    apply_level(x0, 2, 0, s16, 1, 1.0, 5, m["g"], m["h"], BZ, BZ, residual)

    near = jnp.abs(zi2 - 2 * zo2)
    rest_z = jnp.where(near == 0, 1.0, jnp.where(near == 1, 0.5, 0.0)).astype(F32)

    def rest_x(f, carry):
        r = [m["r0"][f, x] for x in range(4)]
        m["zl"][3 * f] = r[0] + 0.5 * r[1]
        m["zl"][3 * f + 1] = 0.5 * (r[1] + r[3]) + r[2]
        m["zl"][3 * f + 2] = 0.5 * r[3]
        return carry

    lax.fori_loop(0, 6, rest_x, 0, unroll=True)
    flat = mm(m["zl"][...].reshape(144, BZ), rest_z)
    m["zr"][...] = flat.reshape(18, 8, 128)
    pb, pbp, pbu, pbd, pbe = m["pb"], m["pbp"], m["pbu"], m["pbd"], m["pbe"]
    sh = sub(128)

    def rest_y(f, carry):
        for i in range(3):
            v = m["zr"][3 * f + i]
            low = jnp.where(sh > 0, y_down(v), 0.0)
            m["zr"][3 * f + i] = v + 0.5 * (low + y_up(v))
            pb[f, i] = jnp.zeros((8, 128), F32)
            pb[f, i, 0:4] = m["zr"][3 * f + i, pl.ds(0, 4, stride=2)]
            pb[f, i, 4:5] = 0.5 * v[7:8]
        return carry

    lax.fori_loop(0, 6, rest_y, 0, unroll=True)

    for i in range(3):
        for c in range(3):
            one, two = pb[c, i], pb[3 + c, i]
            turned = y_down(one, 4)
            pbu[c, i] = jnp.where(
                (sh >= 6) | (sh == 0), turned, jnp.where((sh >= 2) & (sh <= 4), two, 0.0)
            )
            pbe[c, i] = jnp.where(
                (sh == 5) | (sh == 6), turned, jnp.where((sh == 1) | (sh == 2), two, 0.0)
            )
        for k in range(4):
            rest = y_down(pb[4 + k // 2, i], 5 - 3 * (k % 2))
            pbp[k, i] = jnp.where(sh < 5, pb[k, i], rest)
        for f in range(6):
            pbd[i, f : f + 1] = pb[f, i, 0:1]
        pbd[i, 6:8] = jnp.zeros((2, 128), F32)

    rp, ru, rd, re = m["rp"], m["ru"], m["rd"], m["re"]

    def shares(ax, ay, lo, n):
        slot, at = 2 - ax, pl.ds(lo, n)
        if ay == 0:
            return message(pbp.at[:, at], rp.at[slot, :, at], ax, 0)
        if ay == 1:
            return message(pbu.at[:, at], ru.at[slot, :, at], ax, 1)
        return message(pbd.at[at], rd.at[slot, at], ax, -1)

    def late_rows(ax, lo, n):
        slot, at = 2 - ax, pl.ds(lo, n)
        return message(pbe.at[:, at], re.at[slot, :, at], ax, -1)

    third = [shares(2, ay, 2, 1) for ay in (1, -1, 0)]
    third += [shares(1, ay, 0, 3) for ay in (1, -1, 0)]
    third += [shares(-1, ay, 0, 1) for ay in (1, -1, 0)]
    third += [shares(0, 1, 0, 3), shares(0, -1, 0, 3)]
    late = [shares(-1, ay, 1, 2) for ay in (1, -1, 0)]
    late += [shares(-2, ay, 0, 1) for ay in (1, -1, 0)]
    late += [late_rows(1, 0, 3), late_rows(2, 2, 1), late_rows(0, 0, 3)]
    late += [late_rows(-1, 0, 3), late_rows(-2, 0, 1)]
    for copy in third + late:
        copy.start()

    rs1 = m["rs1"]
    group_done(rs1, group_recv, 0)
    pl.semaphore_signal(
        token.at[0], inc=1, device_id=device(2, 0), device_id_type=pl.DeviceIdType.MESH
    )

    s1, invd1 = m["s1"], m["invd1"]
    for p in range(8):
        x = p - 3
        dx, i = x // 2, x % 2
        mid = m["s1s"][i] if dx == 0 else rs1[S1_SLOTS.index((dx, 0)), i]
        top = rs1[S1_SLOTS.index((dx, 1)), i]
        low = rs1[S1_SLOTS.index((dx, -1)), i]
        frame = jnp.concatenate(
            [jnp.where(sh < 4, mid, top), jnp.where(sh >= 4, low, 0.0)], axis=0
        )
        here = rows1 * in_x(gx * 2 + x, NX * 2)
        s1[p] = jnp.where(here > 0.0, frame, 0.0)

    def diag1(p, carry):
        t = s1[p] + s1[p + 1]
        t = t + y_down(t)
        t = t + z_down(t, 128)
        here = rows1 * in_x(gx * 2 + p - 2, NX * 2)
        invd1[p] = jnp.where(here > 0.0, (0.5 / (2.0 * DIAG)) / t, 0.0)
        return carry

    lax.fori_loop(0, 7, diag1, 0, unroll=True)

    zi1, zo1 = iota((128, 128), 0), iota((128, 128), 1)
    pairs_2 = inside(zi1 // 2 == zo1 % 64) * 0.125
    t2l, t2r, t2 = m["t2l"], m["t2r"], m["t2"]
    own2 = s1[3] + s1[4]
    below2 = s1[1] + s1[2]
    wide = mm(jnp.concatenate([own2 + y_up(own2), below2 + y_up(below2)], axis=0), pairs_2)
    w_own, w_sum = wide[0:16], wide[0:16] + wide[16:32]
    dg = w_sum + y_down(w_sum, 2)
    dg = dg + z_down(dg, 64)
    dg = jnp.where(dg > 0.0, (0.5 / (4.0 * DIAG)) / dg, 0.0)
    t2r[3] = jnp.where(iota((8, 128), 1) < 64, w_own[0:8], dg[0:8])
    t2[6:8] = t2r[3, pl.ds(0, 2, stride=2)]

    for copy in third:
        copy.wait_recv()

    b1, x1 = m["b1"], m["x1"]
    okx = {d: (gx + d >= 0) & (gx + d < NX) for d in range(-2, 3)}
    oky = {d: (gy + d >= 0) & (gy + d < NY) for d in range(-1, 2)}

    def sources(x):
        return [(dx, x - 2 * dx) for dx in range(-2, 3) if 0 <= x - 2 * dx <= 2]

    def summed(x, dy, read):
        total = None
        for dx, i in sources(x):
            if (dx, dy) != (0, 0):
                v = jnp.where(okx[dx] & oky[dy], read(dx + 2, i), 0.0)
                total = v if total is None else total + v
        return total

    def right_side_1(planes, whole):
        for p in planes:
            x = p - 2
            mids = [summed(x, 0, lambda d, i, k=k: rp[d, k, i]) for k in range(4)]
            if mids[0] is not None:
                mids = [jnp.where(sh < 5, v, 0.0) for v in mids] + [
                    jnp.where(
                        sh < 3, y_down(mids[k], 3), jnp.where(sh < 5, y_up(mids[k + 1], 2), 0.0)
                    )
                    for k in (0, 2)
                ]
            line4 = summed(x, 1, lambda d, i: rd[d, i])
            for c in range(3):
                up = summed(x, -1, lambda d, i, c=c: ru[d, c, i])
                ends = summed(x, 1, lambda d, i, c=c: re[d, c, i]) if whole else None
                for l in range(2):
                    f = 3 * l + c
                    if l == 1:
                        up = y_down(up, 4)
                        ends = y_down(ends, 4) if whole else None
                    t0 = jnp.where(sh == 0, up, jnp.where(sh == 4, line4[f : f + 1], 0.0))
                    if whole:
                        t0 = jnp.where((sh == 5) | (sh == 6), ends, t0)
                    if 0 <= x <= 2:
                        t0 = t0 + pb[f, x]
                    if mids[0] is not None:
                        t0 = t0 + mids[f]
                    v = jnp.concatenate([t0, jnp.where(sh >= 6, up, 0.0)], axis=0)
                    b1[f, p] = v
                    x1[f, p] = invd1[p] * v

    right_side_1(range(5), False)

    def residual_1(f, e, image):
        m["r1"][f, e - 1] = b1[f, e] - image

    apply_level(x1, 2, 0, s1, 1, 2.0, 4, m["g1"], m["h1"], 128, 128, residual_1)

    for c in range(3):
        sides = []
        for l in range(2):
            r = [m["r1"][3 * l + c, x] for x in range(3)]
            v = r[1] + 0.5 * (r[0] + r[2])
            v = v + 0.5 * (y_up(v) + y_down(v))
            sides.append(v[0:8])
        t2l[c] = jnp.concatenate(sides, axis=1)
    t2l[3] = jnp.zeros((8, BZ), F32)
    near = jnp.abs(zi2 % 128 - 2 * (zo2 % 64))
    rest_2 = jnp.where(near == 0, 1.0, jnp.where(near == 1, 0.5, 0.0)).astype(F32)
    rest_2 = jnp.where(zi2 // 128 == zo2 // 64, rest_2, 0.0)
    flat = mm(t2l[...].reshape(32, BZ), rest_2)
    for c in range(3):
        t2r[c] = flat[8 * c : 8 * c + 8]
        t2[2 * c : 2 * c + 2] = t2r[c, pl.ds(0, 2, stride=2)]
    for k in range(4):
        m["t2v"][k] = t2[...] if k == 0 else y_down(t2[...], 2 * k)

    rb2 = m["rb2"]
    pl.semaphore_wait(token.at[0], 1)
    group(lambda dx, dy: m["t2v"].at[dy % 4], rb2, R3_SLOTS, 1)
    for copy in late:
        copy.wait_recv()
    right_side_1(range(7), True)
    group_done(rb2, group_recv, 1)
    for ax in (-8, 8):
        pl.semaphore_signal(
            token.at[1], inc=1, device_id=device(ax, 0), device_id_type=pl.DeviceIdType.MESH
        )

    s2, invd2, b2, x2 = m["s2"], m["invd2"], m["b2"], m["x2"]
    pair = sh // 2
    half = iota((16, 128), 1) < 64
    for p in range(10):
        dx = p - 4

        def tile(dy, dx=dx):
            if (dx, dy) == (0, 0):
                return m["t2v"][0]
            return rb2[R3_SLOTS.index((dx, dy))]

        high = [tile(dy) for dy in range(4)]
        low = [tile(dy) for dy in (-2, -1)]
        here = rows2 * in_x(gx + dx, NX)
        frames = []
        for c in (3, 0, 1, 2):
            t0 = high[0]
            for dy in range(1, 4):
                t0 = jnp.where(pair == (dy + c) % 4, high[dy], t0)
            t1 = jnp.where(
                pair == (2 + c) % 4, low[0], jnp.where(pair == (3 + c) % 4, low[1], 0.0)
            )
            if c:
                t0, t1 = y_up(t0, 2 * c), y_up(t1, 2 * c)
            frames.append(jnp.concatenate([t0, t1], axis=0))
        v = jnp.where(here > 0.0, frames[0], 0.0)
        turned = pltpu.roll(v, 64, 1)
        s2[p] = jnp.where(half, v, turned)
        inv = jnp.where(half, turned, v)
        invd2[p] = inv
        for c in range(3):
            b2[c, p] = frames[1 + c]
            x2[c, p] = inv * frames[1 + c]

    for sweep in range(3):

        def smooth_2(f, e, image, sweep=sweep):
            p = sweep + e
            x2[f, p] = x2[f, p] + invd2[p] * (b2[f, p] - image)

        apply_level(
            x2, 1, sweep, s2, sweep, 4.0, 9 - 2 * sweep, m["g2"], m["h2"], 64, 128, smooth_2
        )

    yy2, w2, yy1, v1 = m["yy2"], m["w2"], m["yy1"], m["v1"]

    def widen_2(p, carry):
        for c in range(3):
            v = x2[c, 3 + p]
            odd = 0.5 * (v + y_up(v))
            k = 4 * c + p
            yy2[k, 8:16] = jnp.zeros((8, 128), F32)
            yy2[k, pl.ds(0, 4, stride=2)] = v[0:4]
            yy2[k, pl.ds(1, 4, stride=2)] = odd[0:4]
            yy2[k, 14:15] = v[15:16]
            yy2[k, 15:16] = odd[15:16]
        return carry

    lax.fori_loop(0, 4, widen_2, 0, unroll=True)
    zi3, zo3 = iota((128, BZ), 0), iota((128, BZ), 1)
    near = jnp.abs(zo3 % 128 - 2 * (zi3 % 64))
    pro_2 = jnp.where(near == 0, 1.0, jnp.where(near == 1, 0.5, 0.0)).astype(F32)
    pro_2 = jnp.where(zi3 // 64 == zo3 // 128, pro_2, 0.0)
    w2[...] = mm(yy2[...].reshape(192, 128), pro_2).reshape(12, 16, BZ)
    for p in range(7):
        x = p - 2
        here = rows1 * in_x(gx * 2 + x, NX * 2)
        for c in range(3):
            k = 4 * c + x // 2 + 1
            v = w2[k] if x % 2 == 0 else 0.5 * (w2[k] + w2[k + 1])
            x1[c, p] = x1[c, p] + here * v[:, 0:128]
            x1[3 + c, p] = x1[3 + c, p] + here * v[:, 128:256]

    def smooth_1(f, e, image):
        x1[f, e] = x1[f, e] + invd1[e] * (b1[f, e] - image)

    apply_level(x1, 2, 0, s1, 1, 2.0, 6, m["g1"], m["h1"], 128, 128, smooth_1)

    def widen_1(f, carry):
        for p in range(5):
            v = x1[f, 1 + p]
            odd = 0.5 * (v + y_up(v))
            k = 5 * f + p
            yy1[k, 8:16] = jnp.zeros((8, 128), F32)
            yy1[k, pl.ds(0, 4, stride=2)] = v[0:4]
            yy1[k, pl.ds(1, 4, stride=2)] = odd[0:4]
            yy1[k, 8:9] = v[4:5]
            yy1[k, 9:10] = odd[4:5]
            yy1[k, 15:16] = odd[15:16]
        return carry

    lax.fori_loop(0, 6, widen_1, 0)
    near = jnp.abs(zo3 - 2 * zi3)
    pro_1 = jnp.where(near == 0, 1.0, jnp.where(near == 1, 0.5, 0.0)).astype(F32)

    def widen_z(f, carry):
        at = pl.ds(5 * f, 5)
        v1[at] = mm(yy1[at].reshape(80, 128), pro_1).reshape(5, 16, BZ)
        return carry

    lax.fori_loop(0, 6, widen_z, 0, unroll=True)

    def correct(f, carry):
        for p in range(7):
            x = p - 1
            k = 5 * f + x // 2 + 1
            v = v1[k] if x % 2 == 0 else 0.5 * (v1[k] + v1[k + 1])
            x0[f, p] = x0[f, p] + keep[p] * v
        return carry

    lax.fori_loop(0, 6, correct, 0)

    def smooth_0(f, e, image):
        x0[f, e] = x0[f, e] + invd[e] * (b16[f, e] - image)

    apply_level(x0, 2, 0, s16, 1, 1.0, 6, m["g"], m["h"], BZ, BZ, smooth_0)

    outs = [
        pltpu.make_async_copy(
            x0.at[pl.ds(3 * l, 3), pl.ds(1, 4), pl.ds(0, 8)], pre_out.at[l], out_sem.at[l]
        )
        for l in range(2)
    ]
    for copy in outs:
        copy.start()

    rt, yt, sums = m["rt"], m["yt"], m["sums"]
    sums[...] = jnp.zeros((1, 128), F32)
    line = iota((1, 128), 1)

    def energies(l, carry):
        spread_planes(x0, 3 * l, 1, 5, m["g"], BZ, 2)
        curve = jnp.zeros((8, 128), F32)
        dot = jnp.zeros((8, 128), F32)
        for tile in range(2):
            q = pl.ds(128 * tile, 128)
            for e in range(4):
                low = [m["g"][tile, e, k] for k in range(12)]
                high = [m["g"][tile, e + 1, k] for k in range(12)]
                a = modes_of(low, high)
                f = couple(a, None)
                energy = None
                for c in range(3):
                    for k in a[c]:
                        t = a[c][k] * f[c][k]
                        energy = t if energy is None else energy + t
                energy = energy * (LAME2 / 16.0)
                curve = curve + energy * s16[2 + e, 0:8, q]
                rt[l, 2 + e, :, q] = energy * m["coef"][2 + e, :, q]
                for c in range(3):
                    dot = dot + b16[3 * l + c, 1 + e, 0:8, q] * x0[3 * l + c, 1 + e, 0:8, q]
        for k, v in ((l, dot), (2 + l, curve)):
            v = jnp.sum(jnp.sum(v, axis=0, keepdims=True), axis=1, keepdims=True)
            sums[...] = jnp.where(line == k, v, sums[...])
        return carry

    lax.fori_loop(0, 2, energies, 0)

    rc, sc, rx = m["rc"], m["sc"], m["rx"]
    twin = pltpu.make_async_remote_copy(
        src_ref=sums, dst_ref=rc, send_sem=group_send.at[2], recv_sem=group_recv.at[2],
        device_id=(gx, gy + 1 - 2 * lax.rem(gy, 2)), device_id_type=pl.DeviceIdType.MESH,
    )
    twin.start()
    for x in range(4):
        one, two = rt[0, 2 + x], rt[1, 2 + x]
        yt[x] = jnp.where(
            (sub() < 2) | (sub() >= 6), one,
            jnp.where(sub() < 4, y_down(two, 2), y_up(two, 2)),
        )
    rt_lo, rt_hi = m["rt_lo"], m["rt_hi"]
    fourth = [
        message(yt.at[pl.ds(2, 2)], rt_lo.at[pl.ds(0, 2)], 1, 1),
        message(yt.at[pl.ds(2, 2)], rt_hi.at[pl.ds(0, 2)], 1, -1),
        message(yt.at[pl.ds(0, 2)], rt_lo.at[pl.ds(6, 2)], -1, 1),
        message(yt.at[pl.ds(0, 2)], rt_hi.at[pl.ds(6, 2)], -1, -1),
        message(rt.at[:, pl.ds(4, 2)], rt.at[:, pl.ds(0, 2)], 1, 0),
        message(rt.at[:, pl.ds(2, 2)], rt.at[:, pl.ds(6, 2)], -1, 0),
        message(yt, rt_lo.at[pl.ds(2, 4)], 0, 1),
        message(yt, rt_hi.at[pl.ds(2, 4)], 0, -1),
    ]
    for copy in fourth:
        copy.start()
    pl.semaphore_wait(token.at[1], 2)
    twin.wait_recv()
    sc[...] = sums[...] + rc[...]

    def tell(k, ax, ay):
        pltpu.make_async_remote_copy(
            src_ref=sc, dst_ref=rx.at[k], send_sem=group_send.at[3],
            recv_sem=group_recv.at[3], device_id=(lax.rem(gx + ax, NX), lax.rem(gy + ay, NY)),
            device_id_type=pl.DeviceIdType.MESH,
        ).start()

    def tell_far(k, carry):
        tell(k, 1 + lax.rem(k // 4 + 13, NX - 1), 2 * lax.rem(k, 4))
        return carry

    lax.fori_loop(0, 4 * (NX - 1), tell_far, 0)
    for k in range(3):
        tell(4 * (NX - 1) + k, 0, 2 + 2 * k)

    for copy in fourth:
        copy.wait_recv()
    f16, fil = m["f16"], m["fil"]

    def filter_load(l, carry):
        def put(p, inner):
            hi, lo = rt_hi[p], rt_lo[p]
            moved = jnp.where(sub() < 4, y_up(hi, 2), y_down(lo, 2))
            plain = jnp.where(sub() < 4, hi, lo)
            halo = jnp.where((sub() >= 2) & (sub() < 6), 0.0, jnp.where(l == 0, plain, moved))
            both = jnp.concatenate([rt[l, p], halo], axis=0)
            here = rows0 * in_x(gx * BX + p - 2, NX * BX)
            f16[p] = jnp.where(here > 0.0, both, 0.0)
            return inner

        lax.fori_loop(0, 8, put, 0, unroll=True)

        def run(x, inner):
            fil[l, x] = filter_plane(lambda p: f16[p], x + 2)[0:8]
            return inner

        lax.fori_loop(0, 4, run, 0, unroll=True)
        return carry

    lax.fori_loop(0, 2, filter_load, 0)

    outs.append(pltpu.make_async_copy(fil, fil_out, out_sem.at[2]))
    outs[2].start()
    group_done(rx, group_recv, 3)
    total = sc[...] + jnp.sum(rx[...], axis=0)
    out = jnp.zeros((1, 128), F32)
    for l in range(2):
        dot, curve = total[:, l : l + 1], total[:, 2 + l : 3 + l]
        step = dot / curve
        for k, v in ((l, step * dot * (1.0 / CELLS)), (2 + l, step), (4 + l, step * step)):
            out = jnp.where(line == k, v, out)
    scal_out[...] = out
    for copy in outs:
        copy.wait()

    for copy in first + second + third + late + fourth:
        copy.wait_send()
    group_done(m["rs1"], group_send, 0)
    group_done(rb2, group_send, 1)
    twin.wait_send()
    group_done(rx, group_send, 3)


def scale_kernel(precond, filtered, scalars, disp, sens, comp):
    for l in range(2):
        comp[l] = scalars[0, l]
        disp[l] = precond[l] * scalars[0, 2 + l]
    sens[...] = filtered[0] * scalars[0, 4] + filtered[1] * scalars[0, 5]


def per_device(density, passive_void_mask, support_node_mask, loaded_node_mask, traction):
    scratch = [
        pltpu.VMEM(shape, jnp.int32 if name in INTS else F32) for name, shape in SCRATCH.items()
    ]
    dma = pltpu.SemaphoreType.DMA
    hbm = pl.BlockSpec(memory_space=pltpu.HBM)
    precond, filtered, scalars = pl.pallas_call(
        kernel,
        out_shape=(
            jax.ShapeDtypeStruct((2, 3, BX, BY, BZ), F32),
            jax.ShapeDtypeStruct((2, BX, BY, BZ), F32),
            jax.ShapeDtypeStruct((1, 128), F32),
        ),
        in_specs=[hbm] * 5,
        out_specs=(hbm, hbm, pl.BlockSpec(memory_space=pltpu.VMEM)),
        scratch_shapes=scratch
        + [dma((5,)), dma((N_SEMS,)), dma((N_SEMS,)), dma((4,)), dma((4,))]
        + [dma((3,)), pltpu.SemaphoreType.REGULAR((2,))],
        compiler_params=pltpu.CompilerParams(
            collective_id=0, has_side_effects=True, vmem_limit_bytes=63 * 2**20
        ),
    )(density, passive_void_mask, support_node_mask, loaded_node_mask, traction)
    vmem, smem = pl.BlockSpec(memory_space=pltpu.VMEM), pl.BlockSpec(memory_space=pltpu.SMEM)
    return pl.pallas_call(
        scale_kernel,
        out_shape=(
            jax.ShapeDtypeStruct((2, 3, BX, BY, BZ), F32),
            jax.ShapeDtypeStruct((BX, BY, BZ), F32),
            jax.ShapeDtypeStruct((2,), F32),
        ),
        in_specs=[vmem, vmem, smem],
        out_specs=(vmem, vmem, smem),
        compiler_params=pltpu.CompilerParams(vmem_limit_bytes=63 * 2**20),
    )(precond, filtered, scalars)


def solution(mesh):
    in_specs = (
        P("gx", "gy", None),
        P("gx", "gy", None),
        P("gx", "gy", None),
        P(None, "gx", "gy", None),
        P(None, None, "gx", "gy", None),
    )
    out_specs = (P(None, None, "gx", "gy", None), P("gx", "gy", None), P())
    return jax.shard_map(
        per_device, mesh=mesh, in_specs=in_specs, out_specs=out_specs, check_vma=False
    )
```

```python
import math

import jax
import jax.numpy as jnp
from jax import lax
from jax.experimental import pallas as pl
from jax.experimental.pallas import tpu as pltpu
from jax.sharding import PartitionSpec as P

NX, NY = 32, 8
BX, BY, BZ = 4, 8, 256
CELLS = NX * BX * NY * BY * BZ
F32 = jnp.float32

POISSON = 0.3
LAME1 = POISSON / ((1.0 + POISSON) * (1.0 - 2.0 * POISSON))
LAME2 = 1.0 / (2.0 * (1.0 + POISSON))
RATIO = LAME1 / LAME2
DIAG = (LAME1 + 4.0 * LAME2) / 9.0
EDGE = math.tanh(4.0)


def far(slot):
    dx, dy = slot
    hops = 0
    for x in range(4):
        ring = abs((x + dx) % 4 - x)
        hops += min(ring, 4 - ring) + abs((x + dx) // 4)
    for core in range(2):
        hops += 2 * abs((core + dy) // 2)
    return -hops


R3_SLOTS = [(a, b) for a in range(-4, 6) for b in range(-2, 4) if (a, b) != (0, 0)]
R3_SLOTS.sort(key=far)
S1_SLOTS = [(a, b) for a in range(-2, 3) for b in range(-1, 2) if (a, b) != (0, 0)]


def iota(shape, dim):
    return lax.broadcasted_iota(jnp.int32, shape, dim)


def weight(a, b, c):
    return max(3.0 - math.sqrt(a * a + b * b + c * c), 0.0)


def z_up(v, z, by=1):
    n = v.shape[1]
    return jnp.where(iota(v.shape, 1) % z < z - by, pltpu.roll(v, n - by, 1), 0.0)


def z_down(v, z, by=1):
    n = v.shape[1]
    return jnp.where(iota(v.shape, 1) % z >= by, pltpu.roll(v, by, 1), 0.0)


def y_up(v, by=1):
    return pltpu.roll(v, v.shape[0] - by, 0)


def y_down(v, by=1):
    return pltpu.roll(v, by, 0)


def mm(a, b):
    return jnp.dot(a, b, preferred_element_type=F32, precision=lax.Precision.HIGHEST)


def couple(a, s):
    def key(*dims):
        return tuple(1 if d in dims else 0 for d in range(3))

    f = [dict() for _ in range(3)]
    trace = RATIO * (a[0][key(0)] + a[1][key(1)] + a[2][key(2)])
    third = None if s is None else s * (1.0 / 3.0)

    def times(x, scale, k):
        if scale is None:
            return x if k == 1.0 else x * k
        return x * scale

    for i in range(3):
        f[i][key(i)] = times(trace + 2.0 * a[i][key(i)], s, 1.0)
    for i in range(3):
        for j in range(i + 1, 3):
            shear = times(a[i][key(j)] + a[j][key(i)], s, 1.0)
            f[i][key(j)] = shear
            f[j][key(i)] = shear
    for k in range(3):
        i, j = [d for d in range(3) if d != k]
        p, q = a[i][key(i, k)], a[j][key(j, k)]
        both = RATIO * (p + q)
        f[i][key(i, k)] = times(both + 3.0 * p, third, 1.0 / 3.0)
        f[j][key(j, k)] = times(both + 3.0 * q, third, 1.0 / 3.0)
    mixed = [a[i][key(*[d for d in range(3) if d != i])] for i in range(3)]
    total = mixed[0] + mixed[1] + mixed[2]
    for i in range(3):
        f[i][key(*[d for d in range(3) if d != i])] = times(mixed[i] + total, third, 1.0 / 3.0)
        bubble = a[i][(1, 1, 1)] * ((RATIO + 4.0) / 9.0)
        f[i][(1, 1, 1)] = bubble if s is None else bubble * s
    return f


HYZ = [(0, 0), (0, 1), (1, 0), (1, 1)]


def modes_of(low, high):
    a = [dict() for _ in range(3)]
    for c in range(3):
        for k, (hy, hz) in enumerate(HYZ):
            if k:
                a[c][(0, hy, hz)] = low[4 * c + k] + high[4 * c + k]
            a[c][(1, hy, hz)] = high[4 * c + k] - low[4 * c + k]
    return a


def spread_planes(x_ref, first, xoff, planes, g_ref, z, tiles):
    def body(p, carry):
        for c in range(3):
            v = x_ref[first + c, xoff + p]
            up = z_up(v, z)
            for hz, t in ((0, v + up), (1, up - v)):
                tu = y_up(t)
                for hy, g in ((0, t + tu), (1, tu - t)):
                    for tile in range(tiles):
                        r, q = tile_place(tile, v.shape[1])
                        g_ref[tile, p, 4 * c + 2 * hy + hz] = g[r : r + 8, q : q + 128]
        return carry

    lax.fori_loop(0, planes, body, 0, unroll=True)


def tile_place(tile, lanes):
    per = lanes // 128
    return 8 * (tile // per), 128 * (tile % per)


def element_planes(g_ref, h_ref, s_ref, soff, scale, elements, tiles, lanes):
    per = lanes // 128

    def over_tile(tile, carry):
        r = pl.multiple_of(8 * (tile // per), 8)
        q = pl.multiple_of(128 * (tile % per), 128)

        def body(e, held):
            low, acc = held[:12], held[12:]
            high = tuple(g_ref[tile, e + 1, k] for k in range(12))
            s = s_ref[soff + e, pl.ds(r, 8), pl.ds(q, 128)] * (scale * LAME2 / 16.0)
            f = couple(modes_of(low, high), s)
            fresh = []
            for c in range(3):
                for k, (hy, hz) in enumerate(HYZ):
                    fd = f[c][(1, hy, hz)]
                    if k:
                        fs = f[c][(0, hy, hz)]
                        h_ref[tile, e, 4 * c + k] = acc[4 * c + k] + (fs - fd)
                        fresh.append(fs + fd)
                    else:
                        h_ref[tile, e, 4 * c + k] = acc[4 * c + k] - fd
                        fresh.append(fd)
            return high + tuple(fresh)

        start = tuple(g_ref[tile, 0, k] for k in range(12))
        zeros = tuple(jnp.zeros((8, 128), F32) for _ in range(12))
        lax.fori_loop(0, elements, body, start + zeros, unroll=True)
        return carry

    lax.fori_loop(0, tiles, over_tile, 0, unroll=True)


def gather_nodes(h_ref, e, c, z, lanes):
    def load(k):
        rows = []
        for half in range(2):
            tiles = [h_ref[half * (lanes // 128) + q, e, 4 * c + k] for q in range(lanes // 128)]
            rows.append(tiles[0] if len(tiles) == 1 else jnp.concatenate(tiles, axis=1))
        return jnp.concatenate(rows, axis=0)

    t = []
    for hz in range(2):
        hs, hd = load(hz), load(2 + hz)
        t.append((hs - hd) + y_down(hs + hd))
    return (t[0] - t[1]) + z_down(t[0] + t[1], z)


def apply_level(x_ref, groups, xoff, s_ref, soff, scale, elements, g_ref, h_ref, z, lanes, use):
    tiles = 2 * lanes // 128

    def one(l, carry):
        spread_planes(x_ref, 3 * l, xoff, elements + 1, g_ref.at[l], z, tiles)
        element_planes(g_ref.at[l], h_ref.at[l], s_ref, soff, scale, elements, tiles, lanes)

        def nodes(e, inner):
            for c in range(3):
                use(3 * l + c, e, gather_nodes(h_ref.at[l], e, c, z, lanes))
            return inner

        lax.fori_loop(1, elements, nodes, 0, unroll=True)
        return carry

    lax.fori_loop(0, groups, one, 0, unroll=True)


def filter_plane(load, p):
    a = [load(p), load(p - 1) + load(p + 1), load(p - 2) + load(p + 2)]
    f = []
    for c in range(3):
        h = []
        for b in range(3):
            t = None
            for i in range(3):
                w = weight(i, b, c)
                if w > 0.0:
                    t = w * a[i] if t is None else t + w * a[i]
            h.append(t)
        out = h[0]
        if h[1] is not None:
            out = out + (y_up(h[1]) + y_down(h[1]))
        if h[2] is not None:
            out = out + (y_up(h[2], 2) + y_down(h[2], 2))
        f.append(out)
    z = f[0].shape[1]
    return (
        f[0]
        + (z_up(f[1], z) + z_down(f[1], z))
        + (z_up(f[2], z, 2) + z_down(f[2], z, 2))
    )


SCRATCH = dict(
    df=(12, 8, BZ), pf=(8, 8, BZ), bf=(7, 7, 8, BZ),
    sup=(4, 8, BZ), lod=(2, 4, 8, BZ), tra=(2, 3, 4, 8, BZ), pas=(4, 8, BZ),
    ya_up=(4, 8, BZ), ya_dn=(4, 8, BZ), yb_up=(4, 8, BZ), yb_dn=(2, 4, 8, BZ),
    ra_lo=(12, 8, BZ), ra_hi=(12, 8, BZ), rb_lo=(7, 8, BZ), rb_hi=(2, 7, 8, BZ),
    gden=(3, 16, BZ), d16=(12, 16, BZ), s16=(8, 16, BZ), coef=(8, 8, BZ),
    b16=(6, 7, 16, BZ), x0=(6, 7, 16, BZ), keep=(7, 16, BZ), invd=(7, 16, BZ),
    g=(2, 4, 7, 12, 8, 128), h=(2, 4, 6, 12, 8, 128), r0=(6, 4, 8, BZ),
    zl=(18, 8, BZ), zr=(18, 8, 128), zc=(2, 8, 128),
    pb=(6, 3, 8, 128), pbp=(4, 3, 8, 128), pbu=(3, 3, 8, 128), pbd=(3, 8, 128),
    pbe=(3, 3, 8, 128),
    s1s=(2, 8, 128), rs1=(len(S1_SLOTS), 2, 8, 128),
    rp=(5, 4, 3, 8, 128), ru=(5, 3, 3, 8, 128), rd=(5, 3, 8, 128), re=(5, 3, 3, 8, 128),
    s1=(8, 16, 128), invd1=(7, 16, 128), b1=(6, 7, 16, 128), x1=(6, 7, 16, 128),
    g1=(2, 2, 7, 12, 8, 128), h1=(2, 2, 6, 12, 8, 128), r1=(6, 3, 16, 128),
    t2l=(4, 8, BZ), t2r=(4, 8, 128), t2=(8, 128), t2v=(4, 8, 128), rb2=(len(R3_SLOTS), 8, 128),
    s2=(10, 16, 128), invd2=(10, 16, 128), b2=(3, 10, 16, 128), x2=(3, 10, 16, 128),
    g2=(1, 2, 10, 12, 8, 128), h2=(1, 2, 9, 12, 8, 128),
    yy2=(12, 16, 128), w2=(12, 16, BZ), yy1=(30, 16, 128), v1=(30, 16, BZ),
    sums=(1, 128), rc=(1, 128), sc=(1, 128), rx=(127, 1, 128),
    rt=(2, 8, 8, BZ), yt=(4, 8, BZ), rt_lo=(8, 8, BZ), rt_hi=(8, 8, BZ),
    f16=(8, 16, BZ), fil=(2, 4, 8, BZ),
)
INTS = ("sup", "lod", "pas")
NAMES = list(SCRATCH)
N_SEMS = 64


def kernel(dens, pas_in, sup_in, lod_in, tra_in, pre_out, fil_out, scal_out, *scratch):
    m = dict(zip(NAMES, scratch))
    load_sem, send_sem, recv_sem, group_send, group_recv, out_sem, token = scratch[len(NAMES) :]
    gx, gy = lax.axis_index("gx"), lax.axis_index("gy")

    def device(ax, ay):
        return lax.rem(gx + ax + NX, NX), lax.rem(gy + ay + NY, NY)

    barrier = pltpu.get_barrier_semaphore()

    around = [(a, b) for a in (-1, 0, 1) for b in (-1, 0, 1) if (a, b) != (0, 0)]
    for ax, ay in around:
        pl.semaphore_signal(
            barrier, inc=1, device_id=device(ax, ay), device_id_type=pl.DeviceIdType.MESH
        )

    loads = [
        pltpu.make_async_copy(dens, m["df"].at[pl.ds(4, 4)], load_sem.at[0]),
        pltpu.make_async_copy(pas_in, m["pas"], load_sem.at[1]),
        pltpu.make_async_copy(sup_in, m["sup"], load_sem.at[2]),
        pltpu.make_async_copy(lod_in, m["lod"], load_sem.at[3]),
        pltpu.make_async_copy(tra_in, m["tra"], load_sem.at[4]),
    ]
    for copy in loads:
        copy.start()

    counter = [0]

    def message(src, dst, ax, ay):
        k = counter[0]
        counter[0] += 1
        return pltpu.make_async_remote_copy(
            src_ref=src, dst_ref=dst, send_sem=send_sem.at[k], recv_sem=recv_sem.at[k],
            device_id=device(ax, ay), device_id_type=pl.DeviceIdType.MESH,
        )

    def sub(z=BZ):
        return iota((8, z), 0)

    def inside(cond):
        return jnp.where(cond, 1.0, 0.0).astype(F32)

    def in_x(x, size):
        return inside((x >= 0) & (x < size))

    row16 = iota((16, BZ), 0)
    y0 = gy * BY + jnp.where(row16 < 12, row16, row16 - 16)
    rows0 = inside((y0 >= 0) & (y0 < NY * BY))
    row16h = iota((16, 128), 0)
    y1 = gy * 4 + jnp.where(row16h < 8, row16h, row16h - 16)
    rows1 = inside((y1 >= 0) & (y1 < NY * 4))
    y2 = gy * 2 + jnp.where(row16h < 8, row16h, row16h - 16)
    rows2 = inside((y2 >= 0) & (y2 < NY * 2))

    def in_y(y):
        return inside((y >= 0) & (y < NY * BY))

    zi = iota((16, BZ), 1)
    cz = [None] + [inside(zi >= d) + inside(zi < BZ - d) for d in (1, 2)]
    cy = [None] + [in_y(y0 - d) + in_y(y0 + d) for d in (1, 2)]
    for a in range(3):
        total = None
        for b in range(3):
            w = weight(a, b, 0) + weight(a, b, 1) * cz[1]
            if weight(a, b, 2) > 0.0:
                w = w + weight(a, b, 2) * cz[2]
            w = w if b == 0 else w * cy[b]
            total = w if total is None else total + w
        m["gden"][a] = total

    loads[1].wait()
    loads[0].wait()
    df, pf, bf = m["df"], m["pf"], m["bf"]
    for x in range(4):
        pf[2 + x] = 1.0 - m["pas"][x].astype(F32)
        p4 = y_down(pf[2 + x], 4)
        m["ya_up"][x] = jnp.where(sub() >= 4, df[4 + x], p4)
        m["ya_dn"][x] = jnp.where(sub() < 4, df[4 + x], p4)
    loads[2].wait()
    loads[3].wait()
    loads[4].wait()
    for x in range(4):
        kept = 1.0 - m["sup"][x].astype(F32)
        bf[6, 1 + x] = kept
        for l in range(2):
            mask = kept * m["lod"][l, x].astype(F32)
            for c in range(3):
                bf[3 * l + c, 1 + x] = mask * m["tra"][l, c, x]
        for f in range(7):
            v = bf[f, 1 + x]
            m["yb_up"][x, f : f + 1] = v[7:8]
            m["yb_dn"][0, x, f : f + 1] = v[0:1]
            m["yb_dn"][1, x, f : f + 1] = v[1:2]
        m["yb_up"][x, 7:8] = jnp.zeros((1, BZ), F32)
        m["yb_dn"][0, x, 7:8] = jnp.zeros((1, BZ), F32)
        m["yb_dn"][1, x, 7:8] = jnp.zeros((1, BZ), F32)

    pl.semaphore_wait(barrier, len(around))

    ra_lo, ra_hi, rb_lo, rb_hi = m["ra_lo"], m["ra_hi"], m["rb_lo"], m["rb_hi"]
    own = df.at[pl.ds(4, 4)]
    first = [
        message(m["ya_up"], ra_lo.at[pl.ds(0, 4)], 1, 1),
        message(m["ya_dn"], ra_hi.at[pl.ds(0, 4)], 1, -1),
        message(m["ya_up"], ra_lo.at[pl.ds(8, 4)], -1, 1),
        message(m["ya_dn"], ra_hi.at[pl.ds(8, 4)], -1, -1),
        message(own, df.at[pl.ds(0, 4)], 1, 0),
        message(own, df.at[pl.ds(8, 4)], -1, 0),
        message(pf.at[pl.ds(4, 2)], pf.at[pl.ds(0, 2)], 1, 0),
        message(pf.at[pl.ds(2, 2)], pf.at[pl.ds(6, 2)], -1, 0),
        message(m["ya_up"], ra_lo.at[pl.ds(4, 4)], 0, 1),
        message(m["ya_dn"], ra_hi.at[pl.ds(4, 4)], 0, -1),
    ]
    second = [
        message(m["yb_up"].at[pl.ds(3, 1)], rb_lo.at[pl.ds(0, 1)], 1, 1),
        message(m["yb_dn"].at[:, pl.ds(3, 1)], rb_hi.at[:, pl.ds(0, 1)], 1, -1),
        message(m["yb_up"].at[pl.ds(0, 2)], rb_lo.at[pl.ds(5, 2)], -1, 1),
        message(m["yb_dn"].at[:, pl.ds(0, 2)], rb_hi.at[:, pl.ds(5, 2)], -1, -1),
        message(bf.at[:, pl.ds(4, 1)], bf.at[:, pl.ds(0, 1)], 1, 0),
        message(bf.at[:, pl.ds(1, 2)], bf.at[:, pl.ds(5, 2)], -1, 0),
        message(m["yb_up"], rb_lo.at[pl.ds(1, 4)], 0, 1),
        message(m["yb_dn"], rb_hi.at[:, pl.ds(1, 4)], 0, -1),
    ]
    for copy in first + second:
        copy.start()
    for copy in first:
        copy.wait_recv()

    d16, s16 = m["d16"], m["s16"]

    def put_density(p, carry):
        halo = jnp.where(sub() < 4, ra_hi[p], ra_lo[p])
        both = jnp.concatenate([df[p], halo], axis=0)
        here = in_x(gx * BX + p - 4, NX * BX)
        d16[p] = jnp.where(rows0 * here > 0.0, both, 0.0)
        return carry

    lax.fori_loop(0, 12, put_density, 0, unroll=True)

    def stiffen(i, carry):
        x = gx * BX + i - 2
        number = filter_plane(lambda p: d16[p], i + 2)
        cx1 = in_x(x - 1, NX * BX) + in_x(x + 1, NX * BX)
        cx2 = in_x(x - 2, NX * BX) + in_x(x + 2, NX * BX)
        denom = m["gden"][0] + cx1 * m["gden"][1] + cx2 * m["gden"][2]
        level = jnp.tanh(8.0 * (number / denom - 0.5))
        slope = (1.0 - level * level) * (8.0 / (2.0 * EDGE))
        halo = pltpu.roll(jnp.where(sub() >= 4, ra_hi[i + 2], ra_lo[i + 2]), 4, 0)
        solid = jnp.concatenate([pf[i], halo], axis=0)
        phys = solid * ((EDGE + level) * (1.0 / (2.0 * EDGE)))
        stiff = 0.001 + 0.999 * (phys * phys * phys)
        s16[i] = jnp.where(rows0 * in_x(x, NX * BX) > 0.0, stiff, 0.0)
        coef = -3.0 * 0.999 * (phys * phys) * solid * slope / denom
        m["coef"][i] = coef[0:8]
        return carry

    lax.fori_loop(0, 8, stiffen, 0, unroll=True)

    zi2, zo2 = iota((BZ, 128), 0), iota((BZ, 128), 1)
    pairs_z = inside(zi2 // 2 == zo2) * 0.125
    flat = jnp.concatenate([(s16[2 + 2 * i] + s16[3 + 2 * i])[0:8] for i in range(2)], axis=0)
    flat = mm(flat, pairs_z)
    for i in range(2):
        v = flat[8 * i : 8 * i + 8]
        m["zc"][i] = v + y_up(v)
        half = m["zc"][i, pl.ds(0, 4, stride=2)]
        m["s1s"][i, 0:4] = half
        m["s1s"][i, 4:8] = half

    def group(src, dst, slots, k):
        for n, (dx, dy) in enumerate(slots):
            pltpu.make_async_remote_copy(
                src_ref=src(dx, dy), dst_ref=dst.at[n], send_sem=group_send.at[k],
                recv_sem=group_recv.at[k], device_id=device(-dx, -dy),
                device_id_type=pl.DeviceIdType.MESH,
            ).start()

    def group_done(dst, sem, k):
        pltpu.make_async_copy(dst, dst, sem.at[k]).wait()

    for copy in second:
        copy.wait_recv()
    group(lambda dx, dy: m["s1s"], m["rs1"], S1_SLOTS, 0)


    x0, b16, keep, invd = m["x0"], m["b16"], m["keep"], m["invd"]

    def halo_rows(p, f):
        lo = rb_lo[p, f : f + 1]
        hi0, hi1 = rb_hi[0, p, f : f + 1], rb_hi[1, p, f : f + 1]
        return jnp.where(
            sub() == 7, lo, jnp.where(sub() == 0, hi0, jnp.where(sub() == 1, hi1, 0.0))
        )

    def begin(p, carry):
        x = gx * BX + p - 1
        t = s16[p] + s16[p + 1]
        t = t + y_down(t)
        t = t + z_down(t, BZ)
        here = rows0 * in_x(x, NX * BX)
        kept = here * jnp.concatenate([bf[6, p], halo_rows(p, 6)], axis=0)
        inv = jnp.where(here > 0.0, kept * (0.5 / DIAG) / t, 0.0)
        keep[p] = kept
        invd[p] = inv
        for f in range(6):
            b = jnp.concatenate([bf[f, p], halo_rows(p, f)], axis=0)
            b16[f, p] = b
            x0[f, p] = inv * b
        return carry

    lax.fori_loop(0, 7, begin, 0, unroll=True)

    def residual(f, e, image):
        m["r0"][f, e - 1] = keep[e, 0:8] * (b16[f, e, 0:8] - image[0:8])

    apply_level(x0, 2, 0, s16, 1, 1.0, 5, m["g"], m["h"], BZ, BZ, residual)

    near = jnp.abs(zi2 - 2 * zo2)
    rest_z = jnp.where(near == 0, 1.0, jnp.where(near == 1, 0.5, 0.0)).astype(F32)

    def rest_x(f, carry):
        r = [m["r0"][f, x] for x in range(4)]
        m["zl"][3 * f] = r[0] + 0.5 * r[1]
        m["zl"][3 * f + 1] = 0.5 * (r[1] + r[3]) + r[2]
        m["zl"][3 * f + 2] = 0.5 * r[3]
        return carry

    lax.fori_loop(0, 6, rest_x, 0, unroll=True)
    flat = mm(m["zl"][...].reshape(144, BZ), rest_z)
    m["zr"][...] = flat.reshape(18, 8, 128)
    pb, pbp, pbu, pbd, pbe = m["pb"], m["pbp"], m["pbu"], m["pbd"], m["pbe"]
    sh = sub(128)

    def rest_y(f, carry):
        for i in range(3):
            v = m["zr"][3 * f + i]
            low = jnp.where(sh > 0, y_down(v), 0.0)
            m["zr"][3 * f + i] = v + 0.5 * (low + y_up(v))
            pb[f, i] = jnp.zeros((8, 128), F32)
            pb[f, i, 0:4] = m["zr"][3 * f + i, pl.ds(0, 4, stride=2)]
            pb[f, i, 4:5] = 0.5 * v[7:8]
        return carry

    lax.fori_loop(0, 6, rest_y, 0, unroll=True)

    for i in range(3):
        for c in range(3):
            one, two = pb[c, i], pb[3 + c, i]
            turned = y_down(one, 4)
            pbu[c, i] = jnp.where(
                (sh >= 6) | (sh == 0), turned, jnp.where((sh >= 2) & (sh <= 4), two, 0.0)
            )
            pbe[c, i] = jnp.where(
                (sh == 5) | (sh == 6), turned, jnp.where((sh == 1) | (sh == 2), two, 0.0)
            )
        for k in range(4):
            rest = y_down(pb[4 + k // 2, i], 5 - 3 * (k % 2))
            pbp[k, i] = jnp.where(sh < 5, pb[k, i], rest)
        for f in range(6):
            pbd[i, f : f + 1] = pb[f, i, 0:1]
        pbd[i, 6:8] = jnp.zeros((2, 128), F32)

    rp, ru, rd, re = m["rp"], m["ru"], m["rd"], m["re"]

    def shares(ax, ay, lo, n):
        slot, at = 2 - ax, pl.ds(lo, n)
        if ay == 0:
            return message(pbp.at[:, at], rp.at[slot, :, at], ax, 0)
        if ay == 1:
            return message(pbu.at[:, at], ru.at[slot, :, at], ax, 1)
        return message(pbd.at[at], rd.at[slot, at], ax, -1)

    def late_rows(ax, lo, n):
        slot, at = 2 - ax, pl.ds(lo, n)
        return message(pbe.at[:, at], re.at[slot, :, at], ax, -1)

    third = [shares(1, ay, 0, 3) for ay in (1, -1, 0)]
    third += [shares(2, ay, 2, 1) for ay in (1, -1, 0)]
    third += [shares(-1, ay, 0, 1) for ay in (1, -1, 0)]
    third += [shares(0, 1, 0, 3), shares(0, -1, 0, 3)]
    late = [shares(-1, ay, 1, 2) for ay in (1, -1, 0)]
    late += [shares(-2, ay, 0, 1) for ay in (1, -1, 0)]
    late += [late_rows(1, 0, 3), late_rows(2, 2, 1), late_rows(0, 0, 3)]
    late += [late_rows(-1, 0, 3), late_rows(-2, 0, 1)]
    for copy in third + late:
        copy.start()

    rs1 = m["rs1"]
    group_done(rs1, group_recv, 0)
    pl.semaphore_signal(
        token.at[0], inc=1, device_id=device(2, 0), device_id_type=pl.DeviceIdType.MESH
    )

    s1, invd1 = m["s1"], m["invd1"]
    for p in range(8):
        x = p - 3
        dx, i = x // 2, x % 2
        mid = m["s1s"][i] if dx == 0 else rs1[S1_SLOTS.index((dx, 0)), i]
        top = rs1[S1_SLOTS.index((dx, 1)), i]
        low = rs1[S1_SLOTS.index((dx, -1)), i]
        frame = jnp.concatenate(
            [jnp.where(sh < 4, mid, top), jnp.where(sh >= 4, low, 0.0)], axis=0
        )
        here = rows1 * in_x(gx * 2 + x, NX * 2)
        s1[p] = jnp.where(here > 0.0, frame, 0.0)

    def diag1(p, carry):
        t = s1[p] + s1[p + 1]
        t = t + y_down(t)
        t = t + z_down(t, 128)
        here = rows1 * in_x(gx * 2 + p - 2, NX * 2)
        invd1[p] = jnp.where(here > 0.0, (0.5 / (2.0 * DIAG)) / t, 0.0)
        return carry

    lax.fori_loop(0, 7, diag1, 0, unroll=True)

    zi1, zo1 = iota((128, 128), 0), iota((128, 128), 1)
    pairs_2 = inside(zi1 // 2 == zo1 % 64) * 0.125
    t2l, t2r, t2 = m["t2l"], m["t2r"], m["t2"]
    own2 = s1[3] + s1[4]
    below2 = s1[1] + s1[2]
    wide = mm(jnp.concatenate([own2 + y_up(own2), below2 + y_up(below2)], axis=0), pairs_2)
    w_own, w_sum = wide[0:16], wide[0:16] + wide[16:32]
    dg = w_sum + y_down(w_sum, 2)
    dg = dg + z_down(dg, 64)
    dg = jnp.where(dg > 0.0, (0.5 / (4.0 * DIAG)) / dg, 0.0)
    t2r[3] = jnp.where(iota((8, 128), 1) < 64, w_own[0:8], dg[0:8])
    t2[6:8] = t2r[3, pl.ds(0, 2, stride=2)]

    for copy in third:
        copy.wait_recv()

    b1, x1 = m["b1"], m["x1"]
    okx = {d: (gx + d >= 0) & (gx + d < NX) for d in range(-2, 3)}
    oky = {d: (gy + d >= 0) & (gy + d < NY) for d in range(-1, 2)}

    def sources(x):
        return [(dx, x - 2 * dx) for dx in range(-2, 3) if 0 <= x - 2 * dx <= 2]

    def summed(x, dy, read):
        total = None
        for dx, i in sources(x):
            if (dx, dy) != (0, 0):
                v = jnp.where(okx[dx] & oky[dy], read(dx + 2, i), 0.0)
                total = v if total is None else total + v
        return total

    def right_side_1(planes, whole):
        for p in planes:
            x = p - 2
            mids = [summed(x, 0, lambda d, i, k=k: rp[d, k, i]) for k in range(4)]
            if mids[0] is not None:
                mids = [jnp.where(sh < 5, v, 0.0) for v in mids] + [
                    jnp.where(
                        sh < 3, y_down(mids[k], 3), jnp.where(sh < 5, y_up(mids[k + 1], 2), 0.0)
                    )
                    for k in (0, 2)
                ]
            line4 = summed(x, 1, lambda d, i: rd[d, i])
            for c in range(3):
                up = summed(x, -1, lambda d, i, c=c: ru[d, c, i])
                ends = summed(x, 1, lambda d, i, c=c: re[d, c, i]) if whole else None
                for l in range(2):
                    f = 3 * l + c
                    if l == 1:
                        up = y_down(up, 4)
                        ends = y_down(ends, 4) if whole else None
                    t0 = jnp.where(sh == 0, up, jnp.where(sh == 4, line4[f : f + 1], 0.0))
                    if whole:
                        t0 = jnp.where((sh == 5) | (sh == 6), ends, t0)
                    if 0 <= x <= 2:
                        t0 = t0 + pb[f, x]
                    if mids[0] is not None:
                        t0 = t0 + mids[f]
                    v = jnp.concatenate([t0, jnp.where(sh >= 6, up, 0.0)], axis=0)
                    b1[f, p] = v
                    x1[f, p] = invd1[p] * v

    right_side_1(range(5), False)

    def residual_1(f, e, image):
        m["r1"][f, e - 1] = b1[f, e] - image

    apply_level(x1, 2, 0, s1, 1, 2.0, 4, m["g1"], m["h1"], 128, 128, residual_1)

    for c in range(3):
        sides = []
        for l in range(2):
            r = [m["r1"][3 * l + c, x] for x in range(3)]
            v = r[1] + 0.5 * (r[0] + r[2])
            v = v + 0.5 * (y_up(v) + y_down(v))
            sides.append(v[0:8])
        t2l[c] = jnp.concatenate(sides, axis=1)
    t2l[3] = jnp.zeros((8, BZ), F32)
    near = jnp.abs(zi2 % 128 - 2 * (zo2 % 64))
    rest_2 = jnp.where(near == 0, 1.0, jnp.where(near == 1, 0.5, 0.0)).astype(F32)
    rest_2 = jnp.where(zi2 // 128 == zo2 // 64, rest_2, 0.0)
    flat = mm(t2l[...].reshape(32, BZ), rest_2)
    for c in range(3):
        t2r[c] = flat[8 * c : 8 * c + 8]
        t2[2 * c : 2 * c + 2] = t2r[c, pl.ds(0, 2, stride=2)]
    for k in range(4):
        m["t2v"][k] = t2[...] if k == 0 else y_down(t2[...], 2 * k)

    rb2 = m["rb2"]
    pl.semaphore_wait(token.at[0], 1)
    group(lambda dx, dy: m["t2v"].at[dy % 4], rb2, R3_SLOTS, 1)
    for copy in late:
        copy.wait_recv()
    right_side_1(range(7), True)
    group_done(rb2, group_recv, 1)
    for ax in (-8, 8):
        pl.semaphore_signal(
            token.at[1], inc=1, device_id=device(ax, 0), device_id_type=pl.DeviceIdType.MESH
        )

    s2, invd2, b2, x2 = m["s2"], m["invd2"], m["b2"], m["x2"]
    pair = sh // 2
    half = iota((16, 128), 1) < 64
    for p in range(10):
        dx = p - 4

        def tile(dy, dx=dx):
            if (dx, dy) == (0, 0):
                return m["t2v"][0]
            return rb2[R3_SLOTS.index((dx, dy))]

        high = [tile(dy) for dy in range(4)]
        low = [tile(dy) for dy in (-2, -1)]
        here = rows2 * in_x(gx + dx, NX)
        frames = []
        for c in (3, 0, 1, 2):
            t0 = high[0]
            for dy in range(1, 4):
                t0 = jnp.where(pair == (dy + c) % 4, high[dy], t0)
            t1 = jnp.where(
                pair == (2 + c) % 4, low[0], jnp.where(pair == (3 + c) % 4, low[1], 0.0)
            )
            if c:
                t0, t1 = y_up(t0, 2 * c), y_up(t1, 2 * c)
            frames.append(jnp.concatenate([t0, t1], axis=0))
        v = jnp.where(here > 0.0, frames[0], 0.0)
        turned = pltpu.roll(v, 64, 1)
        s2[p] = jnp.where(half, v, turned)
        inv = jnp.where(half, turned, v)
        invd2[p] = inv
        for c in range(3):
            b2[c, p] = frames[1 + c]
            x2[c, p] = inv * frames[1 + c]

    for sweep in range(3):

        def smooth_2(f, e, image, sweep=sweep):
            p = sweep + e
            x2[f, p] = x2[f, p] + invd2[p] * (b2[f, p] - image)

        apply_level(
            x2, 1, sweep, s2, sweep, 4.0, 9 - 2 * sweep, m["g2"], m["h2"], 64, 128, smooth_2
        )

    yy2, w2, yy1, v1 = m["yy2"], m["w2"], m["yy1"], m["v1"]

    def widen_2(p, carry):
        for c in range(3):
            v = x2[c, 3 + p]
            odd = 0.5 * (v + y_up(v))
            k = 4 * c + p
            yy2[k, 8:16] = jnp.zeros((8, 128), F32)
            yy2[k, pl.ds(0, 4, stride=2)] = v[0:4]
            yy2[k, pl.ds(1, 4, stride=2)] = odd[0:4]
            yy2[k, 14:15] = v[15:16]
            yy2[k, 15:16] = odd[15:16]
        return carry

    lax.fori_loop(0, 4, widen_2, 0, unroll=True)
    zi3, zo3 = iota((128, BZ), 0), iota((128, BZ), 1)
    near = jnp.abs(zo3 % 128 - 2 * (zi3 % 64))
    pro_2 = jnp.where(near == 0, 1.0, jnp.where(near == 1, 0.5, 0.0)).astype(F32)
    pro_2 = jnp.where(zi3 // 64 == zo3 // 128, pro_2, 0.0)
    w2[...] = mm(yy2[...].reshape(192, 128), pro_2).reshape(12, 16, BZ)
    for p in range(7):
        x = p - 2
        here = rows1 * in_x(gx * 2 + x, NX * 2)
        for c in range(3):
            k = 4 * c + x // 2 + 1
            v = w2[k] if x % 2 == 0 else 0.5 * (w2[k] + w2[k + 1])
            x1[c, p] = x1[c, p] + here * v[:, 0:128]
            x1[3 + c, p] = x1[3 + c, p] + here * v[:, 128:256]

    def smooth_1(f, e, image):
        x1[f, e] = x1[f, e] + invd1[e] * (b1[f, e] - image)

    apply_level(x1, 2, 0, s1, 1, 2.0, 6, m["g1"], m["h1"], 128, 128, smooth_1)

    def widen_1(f, carry):
        for p in range(5):
            v = x1[f, 1 + p]
            odd = 0.5 * (v + y_up(v))
            k = 5 * f + p
            yy1[k, 8:16] = jnp.zeros((8, 128), F32)
            yy1[k, pl.ds(0, 4, stride=2)] = v[0:4]
            yy1[k, pl.ds(1, 4, stride=2)] = odd[0:4]
            yy1[k, 8:9] = v[4:5]
            yy1[k, 9:10] = odd[4:5]
            yy1[k, 15:16] = odd[15:16]
        return carry

    lax.fori_loop(0, 6, widen_1, 0, unroll=True)
    near = jnp.abs(zo3 - 2 * zi3)
    pro_1 = jnp.where(near == 0, 1.0, jnp.where(near == 1, 0.5, 0.0)).astype(F32)

    def widen_z(f, carry):
        at = pl.ds(5 * f, 5)
        v1[at] = mm(yy1[at].reshape(80, 128), pro_1).reshape(5, 16, BZ)
        return carry

    lax.fori_loop(0, 6, widen_z, 0, unroll=True)

    def correct(f, carry):
        for p in range(7):
            x = p - 1
            k = 5 * f + x // 2 + 1
            v = v1[k] if x % 2 == 0 else 0.5 * (v1[k] + v1[k + 1])
            x0[f, p] = x0[f, p] + keep[p] * v
        return carry

    lax.fori_loop(0, 6, correct, 0, unroll=True)

    def smooth_0(f, e, image):
        x0[f, e] = x0[f, e] + invd[e] * (b16[f, e] - image)

    apply_level(x0, 2, 0, s16, 1, 1.0, 6, m["g"], m["h"], BZ, BZ, smooth_0)

    outs = [
        pltpu.make_async_copy(
            x0.at[pl.ds(3 * l, 3), pl.ds(1, 4), pl.ds(0, 8)], pre_out.at[l], out_sem.at[l]
        )
        for l in range(2)
    ]
    for copy in outs:
        copy.start()

    rt, yt, sums = m["rt"], m["yt"], m["sums"]
    sums[...] = jnp.zeros((1, 128), F32)
    line = iota((1, 128), 1)

    def energies(l, carry):
        spread_planes(x0, 3 * l, 1, 5, m["g"].at[l], BZ, 2)
        curve = jnp.zeros((8, 128), F32)
        dot = jnp.zeros((8, 128), F32)
        for tile in range(2):
            q = pl.ds(128 * tile, 128)
            for e in range(4):
                low = [m["g"][l, tile, e, k] for k in range(12)]
                high = [m["g"][l, tile, e + 1, k] for k in range(12)]
                a = modes_of(low, high)
                f = couple(a, None)
                energy = None
                for c in range(3):
                    for k in a[c]:
                        t = a[c][k] * f[c][k]
                        energy = t if energy is None else energy + t
                energy = energy * (LAME2 / 16.0)
                curve = curve + energy * s16[2 + e, 0:8, q]
                rt[l, 2 + e, :, q] = energy * m["coef"][2 + e, :, q]
                for c in range(3):
                    dot = dot + b16[3 * l + c, 1 + e, 0:8, q] * x0[3 * l + c, 1 + e, 0:8, q]
        for k, v in ((l, dot), (2 + l, curve)):
            v = jnp.sum(jnp.sum(v, axis=0, keepdims=True), axis=1, keepdims=True)
            sums[...] = jnp.where(line == k, v, sums[...])
        return carry

    lax.fori_loop(0, 2, energies, 0, unroll=True)

    rc, sc, rx = m["rc"], m["sc"], m["rx"]
    twin = pltpu.make_async_remote_copy(
        src_ref=sums, dst_ref=rc, send_sem=group_send.at[2], recv_sem=group_recv.at[2],
        device_id=(gx, gy + 1 - 2 * lax.rem(gy, 2)), device_id_type=pl.DeviceIdType.MESH,
    )
    twin.start()
    for x in range(4):
        one, two = rt[0, 2 + x], rt[1, 2 + x]
        yt[x] = jnp.where(
            (sub() < 2) | (sub() >= 6), one,
            jnp.where(sub() < 4, y_down(two, 2), y_up(two, 2)),
        )
    rt_lo, rt_hi = m["rt_lo"], m["rt_hi"]
    fourth = [
        message(yt.at[pl.ds(2, 2)], rt_lo.at[pl.ds(0, 2)], 1, 1),
        message(yt.at[pl.ds(2, 2)], rt_hi.at[pl.ds(0, 2)], 1, -1),
        message(yt.at[pl.ds(0, 2)], rt_lo.at[pl.ds(6, 2)], -1, 1),
        message(yt.at[pl.ds(0, 2)], rt_hi.at[pl.ds(6, 2)], -1, -1),
        message(rt.at[:, pl.ds(4, 2)], rt.at[:, pl.ds(0, 2)], 1, 0),
        message(rt.at[:, pl.ds(2, 2)], rt.at[:, pl.ds(6, 2)], -1, 0),
        message(yt, rt_lo.at[pl.ds(2, 4)], 0, 1),
        message(yt, rt_hi.at[pl.ds(2, 4)], 0, -1),
    ]
    for copy in fourth:
        copy.start()
    pl.semaphore_wait(token.at[1], 2)
    twin.wait_recv()
    sc[...] = sums[...] + rc[...]

    rows_of = [lax.rem(gy + 2 * k, NY) for k in range(4)]
    k = 0
    for ax in sorted(range(NX), key=lambda d: -min(d, NX - d)):
        other = lax.rem(gx + ax, NX)
        for j in (2, 1, 3, 0):
            if (ax, j) != (0, 0):
                pltpu.make_async_remote_copy(
                    src_ref=sc, dst_ref=rx.at[k], send_sem=group_send.at[3],
                    recv_sem=group_recv.at[3], device_id=(other, rows_of[j]),
                    device_id_type=pl.DeviceIdType.MESH,
                ).start()
                k += 1

    for copy in fourth:
        copy.wait_recv()
    f16, fil = m["f16"], m["fil"]

    def filter_load(l, carry):
        def put(p, inner):
            hi, lo = rt_hi[p], rt_lo[p]
            moved = jnp.where(sub() < 4, y_up(hi, 2), y_down(lo, 2))
            plain = jnp.where(sub() < 4, hi, lo)
            halo = jnp.where((sub() >= 2) & (sub() < 6), 0.0, jnp.where(l == 0, plain, moved))
            both = jnp.concatenate([rt[l, p], halo], axis=0)
            here = rows0 * in_x(gx * BX + p - 2, NX * BX)
            f16[p] = jnp.where(here > 0.0, both, 0.0)
            return inner

        lax.fori_loop(0, 8, put, 0, unroll=True)

        def run(x, inner):
            fil[l, x] = filter_plane(lambda p: f16[p], x + 2)[0:8]
            return inner

        lax.fori_loop(0, 4, run, 0, unroll=True)
        return carry

    lax.fori_loop(0, 2, filter_load, 0)

    outs.append(pltpu.make_async_copy(fil, fil_out, out_sem.at[2]))
    outs[2].start()
    group_done(rx, group_recv, 3)
    total = sc[...] + jnp.sum(rx[...], axis=0)
    out = jnp.zeros((1, 128), F32)
    for l in range(2):
        dot, curve = total[:, l : l + 1], total[:, 2 + l : 3 + l]
        step = dot / curve
        for k, v in ((l, step * dot * (1.0 / CELLS)), (2 + l, step), (4 + l, step * step)):
            out = jnp.where(line == k, v, out)
    scal_out[...] = out
    for copy in outs:
        copy.wait()

    for copy in first + second + third + late + fourth:
        copy.wait_send()
    group_done(m["rs1"], group_send, 0)
    group_done(rb2, group_send, 1)
    twin.wait_send()
    group_done(rx, group_send, 3)


def scale_kernel(precond, filtered, scalars, disp, sens, comp):
    for l in range(2):
        comp[l] = scalars[0, l]
        disp[l] = precond[l] * scalars[0, 2 + l]
    sens[...] = filtered[0] * scalars[0, 4] + filtered[1] * scalars[0, 5]


def per_device(density, passive_void_mask, support_node_mask, loaded_node_mask, traction):
    scratch = [
        pltpu.VMEM(shape, jnp.int32 if name in INTS else F32) for name, shape in SCRATCH.items()
    ]
    dma = pltpu.SemaphoreType.DMA
    hbm = pl.BlockSpec(memory_space=pltpu.HBM)
    precond, filtered, scalars = pl.pallas_call(
        kernel,
        out_shape=(
            jax.ShapeDtypeStruct((2, 3, BX, BY, BZ), F32),
            jax.ShapeDtypeStruct((2, BX, BY, BZ), F32),
            jax.ShapeDtypeStruct((1, 128), F32),
        ),
        in_specs=[hbm] * 5,
        out_specs=(hbm, hbm, pl.BlockSpec(memory_space=pltpu.VMEM)),
        scratch_shapes=scratch
        + [dma((5,)), dma((N_SEMS,)), dma((N_SEMS,)), dma((4,)), dma((4,))]
        + [dma((3,)), pltpu.SemaphoreType.REGULAR((2,))],
        compiler_params=pltpu.CompilerParams(
            collective_id=0, has_side_effects=True, vmem_limit_bytes=63 * 2**20
        ),
    )(density, passive_void_mask, support_node_mask, loaded_node_mask, traction)
    vmem, smem = pl.BlockSpec(memory_space=pltpu.VMEM), pl.BlockSpec(memory_space=pltpu.SMEM)
    return pl.pallas_call(
        scale_kernel,
        out_shape=(
            jax.ShapeDtypeStruct((2, 3, BX, BY, BZ), F32),
            jax.ShapeDtypeStruct((BX, BY, BZ), F32),
            jax.ShapeDtypeStruct((2,), F32),
        ),
        in_specs=[vmem, vmem, smem],
        out_specs=(vmem, vmem, smem),
        compiler_params=pltpu.CompilerParams(vmem_limit_bytes=63 * 2**20),
    )(precond, filtered, scalars)


def solution(mesh):
    in_specs = (
        P("gx", "gy", None),
        P("gx", "gy", None),
        P("gx", "gy", None),
        P(None, "gx", "gy", None),
        P(None, None, "gx", "gy", None),
    )
    out_specs = (P(None, None, "gx", "gy", None), P("gx", "gy", None), P())
    return jax.shard_map(
        per_device, mesh=mesh, in_specs=in_specs, out_specs=out_specs, check_vma=False
    )
```

```python
import math

import jax
import jax.numpy as jnp
from jax import lax
from jax.experimental import pallas as pl
from jax.experimental.pallas import tpu as pltpu
from jax.sharding import PartitionSpec as P

NX, NY = 32, 8
BX, BY, BZ = 4, 8, 256
CELLS = NX * BX * NY * BY * BZ
F32 = jnp.float32

POISSON = 0.3
LAME1 = POISSON / ((1.0 + POISSON) * (1.0 - 2.0 * POISSON))
LAME2 = 1.0 / (2.0 * (1.0 + POISSON))
RATIO = LAME1 / LAME2
DIAG = (LAME1 + 4.0 * LAME2) / 9.0
EDGE = math.tanh(4.0)


def far(slot):
    dx, dy = slot
    hops = 0
    for x in range(4):
        ring = abs((x + dx) % 4 - x)
        hops += min(ring, 4 - ring) + abs((x + dx) // 4)
    for core in range(2):
        hops += 2 * abs((core + dy) // 2)
    return -hops


R3_SLOTS = [(a, b) for a in range(-4, 6) for b in range(-2, 4) if (a, b) != (0, 0)]
R3_SLOTS.sort(key=far)
S1_SLOTS = [(a, b) for a in range(-2, 3) for b in range(-1, 2) if (a, b) != (0, 0)]


def iota(shape, dim):
    return lax.broadcasted_iota(jnp.int32, shape, dim)


def weight(a, b, c):
    return max(3.0 - math.sqrt(a * a + b * b + c * c), 0.0)


def z_up(v, z, by=1):
    n = v.shape[1]
    return jnp.where(iota(v.shape, 1) % z < z - by, pltpu.roll(v, n - by, 1), 0.0)


def z_down(v, z, by=1):
    n = v.shape[1]
    return jnp.where(iota(v.shape, 1) % z >= by, pltpu.roll(v, by, 1), 0.0)


def y_up(v, by=1):
    return pltpu.roll(v, v.shape[0] - by, 0)


def y_down(v, by=1):
    return pltpu.roll(v, by, 0)


def mm(a, b):
    b = b.astype(jnp.bfloat16)
    high = a.astype(jnp.bfloat16)
    low = (a - high.astype(F32)).astype(jnp.bfloat16)
    return jnp.dot(high, b, preferred_element_type=F32) + jnp.dot(
        low, b, preferred_element_type=F32
    )


def couple(a, s):
    def key(*dims):
        return tuple(1 if d in dims else 0 for d in range(3))

    f = [dict() for _ in range(3)]
    trace = RATIO * (a[0][key(0)] + a[1][key(1)] + a[2][key(2)])
    third = None if s is None else s * (1.0 / 3.0)

    def times(x, scale, k):
        if scale is None:
            return x if k == 1.0 else x * k
        return x * scale

    for i in range(3):
        f[i][key(i)] = times(trace + 2.0 * a[i][key(i)], s, 1.0)
    for i in range(3):
        for j in range(i + 1, 3):
            shear = times(a[i][key(j)] + a[j][key(i)], s, 1.0)
            f[i][key(j)] = shear
            f[j][key(i)] = shear
    for k in range(3):
        i, j = [d for d in range(3) if d != k]
        p, q = a[i][key(i, k)], a[j][key(j, k)]
        both = RATIO * (p + q)
        f[i][key(i, k)] = times(both + 3.0 * p, third, 1.0 / 3.0)
        f[j][key(j, k)] = times(both + 3.0 * q, third, 1.0 / 3.0)
    mixed = [a[i][key(*[d for d in range(3) if d != i])] for i in range(3)]
    total = mixed[0] + mixed[1] + mixed[2]
    for i in range(3):
        f[i][key(*[d for d in range(3) if d != i])] = times(mixed[i] + total, third, 1.0 / 3.0)
        bubble = a[i][(1, 1, 1)] * ((RATIO + 4.0) / 9.0)
        f[i][(1, 1, 1)] = bubble if s is None else bubble * s
    return f


HYZ = [(0, 0), (0, 1), (1, 0), (1, 1)]


def modes_of(low, high):
    a = [dict() for _ in range(3)]
    for c in range(3):
        for k, (hy, hz) in enumerate(HYZ):
            if k:
                a[c][(0, hy, hz)] = low[4 * c + k] + high[4 * c + k]
            a[c][(1, hy, hz)] = high[4 * c + k] - low[4 * c + k]
    return a


def spread_planes(x_ref, first, xoff, planes, g_ref, z, tiles):
    def body(p, carry):
        for c in range(3):
            v = x_ref[first + c, xoff + p]
            up = z_up(v, z)
            for hz, t in ((0, v + up), (1, up - v)):
                tu = y_up(t)
                for hy, g in ((0, t + tu), (1, tu - t)):
                    for tile in range(tiles):
                        r, q = tile_place(tile, v.shape[1])
                        g_ref[tile, p, 4 * c + 2 * hy + hz] = g[r : r + 8, q : q + 128]
        return carry

    lax.fori_loop(0, planes, body, 0, unroll=True)


def tile_place(tile, lanes):
    per = lanes // 128
    return 8 * (tile // per), 128 * (tile % per)


def element_planes(g_ref, h_ref, s_ref, soff, scale, elements, tiles, lanes):
    per = lanes // 128

    def over_tile(tile, carry):
        r = pl.multiple_of(8 * (tile // per), 8)
        q = pl.multiple_of(128 * (tile % per), 128)

        def body(e, held):
            low, acc = held[:12], held[12:]
            high = tuple(g_ref[tile, e + 1, k] for k in range(12))
            s = s_ref[soff + e, pl.ds(r, 8), pl.ds(q, 128)] * (scale * LAME2 / 16.0)
            f = couple(modes_of(low, high), s)
            fresh = []
            for c in range(3):
                for k, (hy, hz) in enumerate(HYZ):
                    fd = f[c][(1, hy, hz)]
                    if k:
                        fs = f[c][(0, hy, hz)]
                        h_ref[tile, e, 4 * c + k] = acc[4 * c + k] + (fs - fd)
                        fresh.append(fs + fd)
                    else:
                        h_ref[tile, e, 4 * c + k] = acc[4 * c + k] - fd
                        fresh.append(fd)
            return high + tuple(fresh)

        start = tuple(g_ref[tile, 0, k] for k in range(12))
        zeros = tuple(jnp.zeros((8, 128), F32) for _ in range(12))
        lax.fori_loop(0, elements, body, start + zeros, unroll=True)
        return carry

    lax.fori_loop(0, tiles, over_tile, 0, unroll=True)


def gather_nodes(h_ref, e, c, z, lanes, rows=16):
    def load(k):
        parts = []
        for half in range(rows // 8):
            tiles = [h_ref[half * (lanes // 128) + q, e, 4 * c + k] for q in range(lanes // 128)]
            parts.append(tiles[0] if len(tiles) == 1 else jnp.concatenate(tiles, axis=1))
        return parts[0] if len(parts) == 1 else jnp.concatenate(parts, axis=0)

    t = []
    for hz in range(2):
        hs, hd = load(hz), load(2 + hz)
        t.append((hs - hd) + y_down(hs + hd))
    return (t[0] - t[1]) + z_down(t[0] + t[1], z)


def apply_level(
    x_ref, groups, xoff, s_ref, soff, scale, elements, g_ref, h_ref, z, lanes, use, rows=16
):
    tiles = rows // 8 * lanes // 128

    def one(l, carry):
        spread_planes(x_ref, 3 * l, xoff, elements + 1, g_ref.at[l], z, tiles)
        element_planes(g_ref.at[l], h_ref.at[l], s_ref, soff, scale, elements, tiles, lanes)

        def nodes(e, inner):
            for c in range(3):
                use(3 * l + c, e, gather_nodes(h_ref.at[l], e, c, z, lanes, rows))
            return inner

        lax.fori_loop(1, elements, nodes, 0, unroll=True)
        return carry

    lax.fori_loop(0, groups, one, 0, unroll=True)


def put_plane(ref, p, v):
    ref[0, p] = v
    ref[1, p] = y_up(v) + y_down(v)
    ref[2, p] = y_up(v, 2) + y_down(v, 2)


def filter_plane(ref, p, rows=16):
    f = [None, None, None]
    for b in range(3):
        a = [ref[b, p, 0:rows]]
        a += [ref[b, p - d, 0:rows] + ref[b, p + d, 0:rows] for d in (1, 2)]
        for i in range(3):
            for c in range(3):
                w = weight(i, b, c)
                if w > 0.0:
                    f[c] = w * a[i] if f[c] is None else f[c] + w * a[i]
    z = f[0].shape[1]
    return (
        f[0]
        + (z_up(f[1], z) + z_down(f[1], z))
        + (z_up(f[2], z, 2) + z_down(f[2], z, 2))
    )


SCRATCH = dict(
    df=(12, 8, BZ), pf=(8, 8, BZ), bf=(7, 7, 8, BZ),
    sup=(4, 8, BZ), lod=(2, 4, 8, BZ), tra=(2, 3, 4, 8, BZ), pas=(4, 8, BZ),
    ya_up=(4, 8, BZ), ya_dn=(4, 8, BZ), yb_up=(4, 8, BZ), yb_dn=(2, 4, 8, BZ),
    ra_lo=(12, 8, BZ), ra_hi=(12, 8, BZ), rb_lo=(7, 8, BZ), rb_hi=(2, 7, 8, BZ),
    gden=(3, 16, BZ), iden=(8, 16, BZ), d16=(3, 12, 16, BZ), s16=(8, 16, BZ), coef=(8, 8, BZ),
    b16=(6, 7, 16, BZ), x0=(6, 7, 16, BZ), keep=(7, 16, BZ), invd=(7, 16, BZ),
    g=(2, 4, 7, 12, 8, 128), h=(2, 4, 6, 12, 8, 128), r0=(6, 4, 8, BZ),
    zl=(18, 8, BZ), zr=(18, 8, 128), zc=(2, 8, 128),
    pb=(6, 3, 8, 128), pbp=(4, 3, 8, 128), pbu=(3, 3, 8, 128), pbd=(3, 8, 128),
    pbe=(3, 3, 8, 128),
    s1s=(2, 8, 128), rs1=(len(S1_SLOTS), 2, 8, 128),
    rp=(5, 4, 3, 8, 128), ru=(5, 3, 3, 8, 128), rd=(5, 3, 8, 128), re=(5, 3, 3, 8, 128),
    s1=(8, 16, 128), invd1=(7, 16, 128), b1=(6, 7, 16, 128), x1=(6, 7, 16, 128),
    g1=(2, 2, 7, 12, 8, 128), h1=(2, 2, 6, 12, 8, 128), r1=(6, 3, 8, 128),
    s1h=(5, 8, 128), invd1h=(5, 8, 128), b1h=(6, 5, 8, 128), x1h=(6, 5, 8, 128),
    t2l=(4, 8, BZ), t2r=(4, 8, 128), t2=(8, 128), t2v=(4, 8, 128), rb2=(len(R3_SLOTS), 8, 128),
    s2=(10, 16, 128), invd2=(10, 16, 128), b2=(3, 10, 16, 128), x2=(3, 10, 16, 128),
    g2=(1, 2, 10, 12, 8, 128), h2=(1, 2, 9, 12, 8, 128),
    yy2=(12, 16, 128), w2=(12, 16, BZ), yy1=(30, 16, 128), v1=(30, 16, BZ),
    sums=(1, 128), rc=(1, 128), sc=(1, 128), rx=(127, 1, 128),
    rt=(2, 8, 8, BZ), yt=(4, 8, BZ), rt_lo=(8, 8, BZ), rt_hi=(8, 8, BZ),
    f16=(3, 8, 16, BZ), fil=(2, 4, 8, BZ),
)
INTS = ("sup", "lod", "pas")
NAMES = list(SCRATCH)
N_SEMS = 64


def kernel(dens, pas_in, sup_in, lod_in, tra_in, pre_out, fil_out, scal_out, *scratch):
    m = dict(zip(NAMES, scratch))
    load_sem, send_sem, recv_sem, group_send, group_recv, out_sem, token = scratch[len(NAMES) :]
    gx, gy = lax.axis_index("gx"), lax.axis_index("gy")

    def device(ax, ay):
        return lax.rem(gx + ax + NX, NX), lax.rem(gy + ay + NY, NY)

    barrier = pltpu.get_barrier_semaphore()

    around = [(a, b) for a in (-1, 0, 1) for b in (-1, 0, 1) if (a, b) != (0, 0)]
    for ax, ay in around:
        pl.semaphore_signal(
            barrier, inc=1, device_id=device(ax, ay), device_id_type=pl.DeviceIdType.MESH
        )

    loads = [
        pltpu.make_async_copy(dens, m["df"].at[pl.ds(4, 4)], load_sem.at[0]),
        pltpu.make_async_copy(pas_in, m["pas"], load_sem.at[1]),
        pltpu.make_async_copy(sup_in, m["sup"], load_sem.at[2]),
        pltpu.make_async_copy(lod_in, m["lod"], load_sem.at[3]),
        pltpu.make_async_copy(tra_in, m["tra"], load_sem.at[4]),
    ]
    for copy in loads:
        copy.start()

    counter = [0]

    def message(src, dst, ax, ay):
        k = counter[0]
        counter[0] += 1
        return pltpu.make_async_remote_copy(
            src_ref=src, dst_ref=dst, send_sem=send_sem.at[k], recv_sem=recv_sem.at[k],
            device_id=device(ax, ay), device_id_type=pl.DeviceIdType.MESH,
        )

    def sub(z=BZ):
        return iota((8, z), 0)

    def inside(cond):
        return jnp.where(cond, 1.0, 0.0).astype(F32)

    def in_x(x, size):
        return inside((x >= 0) & (x < size))

    row16 = iota((16, BZ), 0)
    y0 = gy * BY + jnp.where(row16 < 12, row16, row16 - 16)
    rows0 = inside((y0 >= 0) & (y0 < NY * BY))
    row16h = iota((16, 128), 0)
    y1 = gy * 4 + jnp.where(row16h < 8, row16h, row16h - 16)
    rows1 = inside((y1 >= 0) & (y1 < NY * 4))
    y2 = gy * 2 + jnp.where(row16h < 8, row16h, row16h - 16)
    rows2 = inside((y2 >= 0) & (y2 < NY * 2))

    def in_y(y):
        return inside((y >= 0) & (y < NY * BY))

    zi = iota((16, BZ), 1)
    cz = [None] + [inside(zi >= d) + inside(zi < BZ - d) for d in (1, 2)]
    cy = [None] + [in_y(y0 - d) + in_y(y0 + d) for d in (1, 2)]
    for a in range(3):
        total = None
        for b in range(3):
            w = weight(a, b, 0) + weight(a, b, 1) * cz[1]
            if weight(a, b, 2) > 0.0:
                w = w + weight(a, b, 2) * cz[2]
            w = w if b == 0 else w * cy[b]
            total = w if total is None else total + w
        m["gden"][a] = total
    for i in range(8):
        x = gx * BX + i - 2
        cx1 = in_x(x - 1, NX * BX) + in_x(x + 1, NX * BX)
        cx2 = in_x(x - 2, NX * BX) + in_x(x + 2, NX * BX)
        m["iden"][i] = 1.0 / (m["gden"][0] + cx1 * m["gden"][1] + cx2 * m["gden"][2])

    loads[1].wait()
    loads[0].wait()
    df, pf, bf = m["df"], m["pf"], m["bf"]
    for x in range(4):
        pf[2 + x] = 1.0 - m["pas"][x].astype(F32)
        p4 = y_down(pf[2 + x], 4)
        m["ya_up"][x] = jnp.where(sub() >= 4, df[4 + x], p4)
        m["ya_dn"][x] = jnp.where(sub() < 4, df[4 + x], p4)
    loads[2].wait()
    loads[3].wait()
    loads[4].wait()
    for x in range(4):
        kept = 1.0 - m["sup"][x].astype(F32)
        bf[6, 1 + x] = kept
        for l in range(2):
            mask = kept * m["lod"][l, x].astype(F32)
            for c in range(3):
                bf[3 * l + c, 1 + x] = mask * m["tra"][l, c, x]
        for f in range(7):
            v = bf[f, 1 + x]
            m["yb_up"][x, f : f + 1] = v[7:8]
            m["yb_dn"][0, x, f : f + 1] = v[0:1]
            m["yb_dn"][1, x, f : f + 1] = v[1:2]
        m["yb_up"][x, 7:8] = jnp.zeros((1, BZ), F32)
        m["yb_dn"][0, x, 7:8] = jnp.zeros((1, BZ), F32)
        m["yb_dn"][1, x, 7:8] = jnp.zeros((1, BZ), F32)

    pl.semaphore_wait(barrier, len(around))

    ra_lo, ra_hi, rb_lo, rb_hi = m["ra_lo"], m["ra_hi"], m["rb_lo"], m["rb_hi"]
    own = df.at[pl.ds(4, 4)]
    first = [
        message(own, df.at[pl.ds(0, 4)], 1, 0),
        message(own, df.at[pl.ds(8, 4)], -1, 0),
        message(pf.at[pl.ds(4, 2)], pf.at[pl.ds(0, 2)], 1, 0),
        message(pf.at[pl.ds(2, 2)], pf.at[pl.ds(6, 2)], -1, 0),
        message(m["ya_up"], ra_lo.at[pl.ds(0, 4)], 1, 1),
        message(m["ya_dn"], ra_hi.at[pl.ds(0, 4)], 1, -1),
        message(m["ya_up"], ra_lo.at[pl.ds(8, 4)], -1, 1),
        message(m["ya_dn"], ra_hi.at[pl.ds(8, 4)], -1, -1),
        message(m["ya_up"], ra_lo.at[pl.ds(4, 4)], 0, 1),
        message(m["ya_dn"], ra_hi.at[pl.ds(4, 4)], 0, -1),
    ]
    second = [
        message(m["yb_up"].at[pl.ds(3, 1)], rb_lo.at[pl.ds(0, 1)], 1, 1),
        message(m["yb_dn"].at[:, pl.ds(3, 1)], rb_hi.at[:, pl.ds(0, 1)], 1, -1),
        message(m["yb_up"].at[pl.ds(0, 1)], rb_lo.at[pl.ds(5, 1)], -1, 1),
        message(m["yb_dn"].at[:, pl.ds(0, 1)], rb_hi.at[:, pl.ds(5, 1)], -1, -1),
        message(bf.at[:, pl.ds(4, 1)], bf.at[:, pl.ds(0, 1)], 1, 0),
        message(bf.at[:, pl.ds(1, 1)], bf.at[:, pl.ds(5, 1)], -1, 0),
        message(m["yb_up"], rb_lo.at[pl.ds(1, 4)], 0, 1),
        message(m["yb_dn"], rb_hi.at[:, pl.ds(1, 4)], 0, -1),
    ]
    last = [
        message(m["yb_up"].at[pl.ds(1, 1)], rb_lo.at[pl.ds(6, 1)], -1, 1),
        message(m["yb_dn"].at[:, pl.ds(1, 1)], rb_hi.at[:, pl.ds(6, 1)], -1, -1),
        message(bf.at[:, pl.ds(2, 1)], bf.at[:, pl.ds(6, 1)], -1, 0),
    ]
    for copy in first + second:
        copy.start()
    for copy in first:
        copy.wait_recv()

    d16, s16 = m["d16"], m["s16"]

    def put_density(p, carry):
        halo = jnp.where(sub() < 4, ra_hi[p], ra_lo[p])
        both = jnp.concatenate([df[p], halo], axis=0)
        here = in_x(gx * BX + p - 4, NX * BX)
        put_plane(d16, p, jnp.where(rows0 * here > 0.0, both, 0.0))
        return carry

    lax.fori_loop(0, 12, put_density, 0, unroll=True)

    def stiffen(i, carry):
        x = gx * BX + i - 2
        number = filter_plane(d16, i + 2)
        level = jnp.tanh(8.0 * (number * m["iden"][i] - 0.5))
        slope = (1.0 - level * level) * (8.0 / (2.0 * EDGE))
        halo = pltpu.roll(jnp.where(sub() >= 4, ra_hi[i + 2], ra_lo[i + 2]), 4, 0)
        solid = jnp.concatenate([pf[i], halo], axis=0)
        phys = solid * ((EDGE + level) * (1.0 / (2.0 * EDGE)))
        stiff = 0.001 + 0.999 * (phys * phys * phys)
        s16[i] = jnp.where(rows0 * in_x(x, NX * BX) > 0.0, stiff, 0.0)
        coef = -3.0 * 0.999 * (phys * phys) * solid * slope * m["iden"][i]
        m["coef"][i] = coef[0:8]
        return carry

    lax.fori_loop(0, 8, stiffen, 0, unroll=True)

    zi2, zo2 = iota((BZ, 128), 0), iota((BZ, 128), 1)
    pairs_z = inside(zi2 // 2 == zo2) * 0.125
    flat = jnp.concatenate([(s16[2 + 2 * i] + s16[3 + 2 * i])[0:8] for i in range(2)], axis=0)
    flat = mm(flat, pairs_z)
    for i in range(2):
        v = flat[8 * i : 8 * i + 8]
        m["zc"][i] = v + y_up(v)
        half = m["zc"][i, pl.ds(0, 4, stride=2)]
        m["s1s"][i, 0:4] = half
        m["s1s"][i, 4:8] = half

    def group(src, dst, slots, k):
        for n, (dx, dy) in enumerate(slots):
            pltpu.make_async_remote_copy(
                src_ref=src(dx, dy), dst_ref=dst.at[n], send_sem=group_send.at[k],
                recv_sem=group_recv.at[k], device_id=device(-dx, -dy),
                device_id_type=pl.DeviceIdType.MESH,
            ).start()

    def group_done(dst, sem, k):
        pltpu.make_async_copy(dst, dst, sem.at[k]).wait()

    for copy in second:
        copy.wait_recv()
    for copy in last:
        copy.start()
    group(lambda dx, dy: m["s1s"], m["rs1"], S1_SLOTS, 0)


    x0, b16, keep, invd = m["x0"], m["b16"], m["keep"], m["invd"]

    def halo_rows(p, f):
        lo = rb_lo[p, f : f + 1]
        hi0, hi1 = rb_hi[0, p, f : f + 1], rb_hi[1, p, f : f + 1]
        return jnp.where(
            sub() == 7, lo, jnp.where(sub() == 0, hi0, jnp.where(sub() == 1, hi1, 0.0))
        )

    def begin(p, carry):
        x = gx * BX + p - 1
        t = s16[p] + s16[p + 1]
        t = t + y_down(t)
        t = t + z_down(t, BZ)
        here = rows0 * in_x(x, NX * BX)
        kept = here * jnp.concatenate([bf[6, p], halo_rows(p, 6)], axis=0)
        inv = jnp.where(here > 0.0, kept * (0.5 / DIAG) / t, 0.0)
        keep[p] = kept
        invd[p] = inv
        for f in range(6):
            b = jnp.concatenate([bf[f, p], halo_rows(p, f)], axis=0)
            b16[f, p] = b
            x0[f, p] = inv * b
        return carry

    lax.fori_loop(0, 6, begin, 0, unroll=True)

    def residual(f, e, image):
        m["r0"][f, e - 1] = keep[e, 0:8] * (b16[f, e, 0:8] - image[0:8])

    apply_level(x0, 2, 0, s16, 1, 1.0, 5, m["g"], m["h"], BZ, BZ, residual)

    near = jnp.abs(zi2 - 2 * zo2)
    rest_z = jnp.where(near == 0, 1.0, jnp.where(near == 1, 0.5, 0.0)).astype(F32)

    def rest_x(f, carry):
        r = [m["r0"][f, x] for x in range(4)]
        m["zl"][3 * f] = r[0] + 0.5 * r[1]
        m["zl"][3 * f + 1] = 0.5 * (r[1] + r[3]) + r[2]
        m["zl"][3 * f + 2] = 0.5 * r[3]
        return carry

    lax.fori_loop(0, 6, rest_x, 0, unroll=True)
    flat = mm(m["zl"][...].reshape(144, BZ), rest_z)
    m["zr"][...] = flat.reshape(18, 8, 128)
    pb, pbp, pbu, pbd, pbe = m["pb"], m["pbp"], m["pbu"], m["pbd"], m["pbe"]
    sh = sub(128)

    def rest_y(f, carry):
        for i in range(3):
            v = m["zr"][3 * f + i]
            low = jnp.where(sh > 0, y_down(v), 0.0)
            m["zr"][3 * f + i] = v + 0.5 * (low + y_up(v))
            pb[f, i] = jnp.zeros((8, 128), F32)
            pb[f, i, 0:4] = m["zr"][3 * f + i, pl.ds(0, 4, stride=2)]
            pb[f, i, 4:5] = 0.5 * v[7:8]
        return carry

    lax.fori_loop(0, 6, rest_y, 0, unroll=True)

    for i in range(3):
        for c in range(3):
            one, two = pb[c, i], pb[3 + c, i]
            turned = y_down(one, 4)
            pbu[c, i] = jnp.where(
                (sh >= 6) | (sh == 0), turned, jnp.where((sh >= 2) & (sh <= 4), two, 0.0)
            )
            pbe[c, i] = jnp.where(
                (sh == 5) | (sh == 6), turned, jnp.where((sh == 1) | (sh == 2), two, 0.0)
            )
        for k in range(4):
            rest = y_down(pb[4 + k // 2, i], 5 - 3 * (k % 2))
            pbp[k, i] = jnp.where(sh < 5, pb[k, i], rest)
        for f in range(6):
            pbd[i, f : f + 1] = pb[f, i, 0:1]
        pbd[i, 6:8] = jnp.zeros((2, 128), F32)

    rp, ru, rd, re = m["rp"], m["ru"], m["rd"], m["re"]

    def shares(ax, ay, lo, n):
        slot, at = 2 - ax, pl.ds(lo, n)
        if ay == 0:
            return message(pbp.at[:, at], rp.at[slot, :, at], ax, 0)
        if ay == 1:
            return message(pbu.at[:, at], ru.at[slot, :, at], ax, 1)
        return message(pbd.at[at], rd.at[slot, at], ax, -1)

    def late_rows(ax, lo, n):
        slot, at = 2 - ax, pl.ds(lo, n)
        return message(pbe.at[:, at], re.at[slot, :, at], ax, -1)

    third = [shares(1, ay, 0, 3) for ay in (1, -1, 0)]
    third += [shares(2, ay, 2, 1) for ay in (1, -1, 0)]
    third += [shares(-1, ay, 0, 1) for ay in (1, -1, 0)]
    third += [shares(0, 1, 0, 3), shares(0, -1, 0, 3)]
    late = [shares(-1, ay, 1, 2) for ay in (1, -1, 0)]
    late += [shares(-2, ay, 0, 1) for ay in (1, -1, 0)]
    late += [late_rows(1, 0, 3), late_rows(2, 2, 1), late_rows(0, 0, 3)]
    late += [late_rows(-1, 0, 3), late_rows(-2, 0, 1)]
    for copy in third + late:
        copy.start()

    rs1 = m["rs1"]
    group_done(rs1, group_recv, 0)
    pl.semaphore_signal(
        token.at[0], inc=1, device_id=device(2, 0), device_id_type=pl.DeviceIdType.MESH
    )

    s1, invd1 = m["s1"], m["invd1"]
    for p in range(8):
        x = p - 3
        dx, i = x // 2, x % 2
        mid = m["s1s"][i] if dx == 0 else rs1[S1_SLOTS.index((dx, 0)), i]
        top = rs1[S1_SLOTS.index((dx, 1)), i]
        low = rs1[S1_SLOTS.index((dx, -1)), i]
        frame = jnp.concatenate(
            [jnp.where(sh < 4, mid, top), jnp.where(sh >= 4, low, 0.0)], axis=0
        )
        here = rows1 * in_x(gx * 2 + x, NX * 2)
        s1[p] = jnp.where(here > 0.0, frame, 0.0)

    def diag1(p, carry):
        t = s1[p] + s1[p + 1]
        t = t + y_down(t)
        t = t + z_down(t, 128)
        here = rows1 * in_x(gx * 2 + p - 2, NX * 2)
        invd1[p] = jnp.where(here > 0.0, (0.5 / (2.0 * DIAG)) / t, 0.0)
        return carry

    lax.fori_loop(0, 7, diag1, 0, unroll=True)

    s1h, invd1h = m["s1h"], m["invd1h"]
    for p in range(5):
        s1h[p] = jnp.where(sh < 5, s1[p, 0:8], s1[p, 8:16])
        invd1h[p] = jnp.where(sh < 5, invd1[p, 0:8], invd1[p, 8:16])

    zi1, zo1 = iota((128, 128), 0), iota((128, 128), 1)
    pairs_2 = inside(zi1 // 2 == zo1 % 64) * 0.125
    t2l, t2r, t2 = m["t2l"], m["t2r"], m["t2"]
    own2 = s1[3] + s1[4]
    below2 = s1[1] + s1[2]
    wide = mm(jnp.concatenate([own2 + y_up(own2), below2 + y_up(below2)], axis=0), pairs_2)
    w_own, w_sum = wide[0:16], wide[0:16] + wide[16:32]
    dg = w_sum + y_down(w_sum, 2)
    dg = dg + z_down(dg, 64)
    dg = jnp.where(dg > 0.0, (0.5 / (4.0 * DIAG)) / dg, 0.0)
    t2r[3] = jnp.where(iota((8, 128), 1) < 64, w_own[0:8], dg[0:8])
    t2[6:8] = t2r[3, pl.ds(0, 2, stride=2)]

    for copy in last:
        copy.wait_recv()
    begin(6, 0)
    for copy in third:
        copy.wait_recv()

    b1, x1, b1h, x1h = m["b1"], m["x1"], m["b1h"], m["x1h"]
    okx = {d: (gx + d >= 0) & (gx + d < NX) for d in range(-2, 3)}
    oky = {d: (gy + d >= 0) & (gy + d < NY) for d in range(-1, 2)}

    def sources(x):
        return [(dx, x - 2 * dx) for dx in range(-2, 3) if 0 <= x - 2 * dx <= 2]

    def summed(x, dy, read):
        total = None
        for dx, i in sources(x):
            if (dx, dy) != (0, 0):
                v = jnp.where(okx[dx] & oky[dy], read(dx + 2, i), 0.0)
                total = v if total is None else total + v
        return total

    def right_side_1(planes, whole):
        for p in planes:
            x = p - 2
            mids = [summed(x, 0, lambda d, i, k=k: rp[d, k, i]) for k in range(4)]
            if mids[0] is not None:
                mids = [jnp.where(sh < 5, v, 0.0) for v in mids] + [
                    jnp.where(
                        sh < 3, y_down(mids[k], 3), jnp.where(sh < 5, y_up(mids[k + 1], 2), 0.0)
                    )
                    for k in (0, 2)
                ]
            line4 = summed(x, 1, lambda d, i: rd[d, i])
            for c in range(3):
                up = summed(x, -1, lambda d, i, c=c: ru[d, c, i])
                ends = summed(x, 1, lambda d, i, c=c: re[d, c, i]) if whole else None
                for l in range(2):
                    f = 3 * l + c
                    if l == 1:
                        up = y_down(up, 4)
                        ends = y_down(ends, 4) if whole else None
                    t0 = jnp.where(sh == 0, up, jnp.where(sh == 4, line4[f : f + 1], 0.0))
                    if whole:
                        t0 = jnp.where((sh == 5) | (sh == 6), ends, t0)
                    if 0 <= x <= 2:
                        t0 = t0 + pb[f, x]
                    if mids[0] is not None:
                        t0 = t0 + mids[f]
                    t1 = jnp.where(sh >= 6, up, 0.0)
                    if whole:
                        v = jnp.concatenate([t0, t1], axis=0)
                        b1[f, p] = v
                        x1[f, p] = invd1[p] * v
                    else:
                        b1h[f, p] = t0 + t1
                        x1h[f, p] = invd1h[p] * (t0 + t1)

    right_side_1(range(5), False)

    def residual_1(f, e, image):
        m["r1"][f, e - 1] = b1h[f, e] - image

    apply_level(x1h, 2, 0, s1h, 1, 2.0, 4, m["g1"], m["h1"], 128, 128, residual_1, 8)

    for c in range(3):
        sides = []
        for l in range(2):
            r = [m["r1"][3 * l + c, x] for x in range(3)]
            v = r[1] + 0.5 * (r[0] + r[2])
            v = v + 0.5 * (y_up(v) + y_down(v))
            sides.append(v)
        t2l[c] = jnp.concatenate(sides, axis=1)
    t2l[3] = jnp.zeros((8, BZ), F32)
    near = jnp.abs(zi2 % 128 - 2 * (zo2 % 64))
    rest_2 = jnp.where(near == 0, 1.0, jnp.where(near == 1, 0.5, 0.0)).astype(F32)
    rest_2 = jnp.where(zi2 // 128 == zo2 // 64, rest_2, 0.0)
    flat = mm(t2l[...].reshape(32, BZ), rest_2)
    for c in range(3):
        t2r[c] = flat[8 * c : 8 * c + 8]
        t2[2 * c : 2 * c + 2] = t2r[c, pl.ds(0, 2, stride=2)]
    for k in range(4):
        m["t2v"][k] = t2[...] if k == 0 else y_down(t2[...], 2 * k)

    rb2 = m["rb2"]
    pl.semaphore_wait(token.at[0], 1)
    group(lambda dx, dy: m["t2v"].at[dy % 4], rb2, R3_SLOTS, 1)
    for copy in late:
        copy.wait_recv()
    right_side_1(range(7), True)
    group_done(rb2, group_recv, 1)
    for ax in (-8, 8):
        pl.semaphore_signal(
            token.at[1], inc=1, device_id=device(ax, 0), device_id_type=pl.DeviceIdType.MESH
        )

    s2, invd2, b2, x2 = m["s2"], m["invd2"], m["b2"], m["x2"]
    pair = sh // 2
    half = iota((16, 128), 1) < 64
    for p in range(10):
        dx = p - 4

        def tile(dy, dx=dx):
            if (dx, dy) == (0, 0):
                return m["t2v"][0]
            return rb2[R3_SLOTS.index((dx, dy))]

        high = [tile(dy) for dy in range(4)]
        low = [tile(dy) for dy in (-2, -1)]
        here = rows2 * in_x(gx + dx, NX)
        frames = []
        for c in (3, 0, 1, 2):
            t0 = high[0]
            for dy in range(1, 4):
                t0 = jnp.where(pair == (dy + c) % 4, high[dy], t0)
            t1 = jnp.where(
                pair == (2 + c) % 4, low[0], jnp.where(pair == (3 + c) % 4, low[1], 0.0)
            )
            if c:
                t0, t1 = y_up(t0, 2 * c), y_up(t1, 2 * c)
            frames.append(jnp.concatenate([t0, t1], axis=0))
        v = jnp.where(here > 0.0, frames[0], 0.0)
        turned = pltpu.roll(v, 64, 1)
        s2[p] = jnp.where(half, v, turned)
        inv = jnp.where(half, turned, v)
        invd2[p] = inv
        for c in range(3):
            b2[c, p] = frames[1 + c]
            x2[c, p] = inv * frames[1 + c]

    for sweep in range(3):

        def smooth_2(f, e, image, sweep=sweep):
            p = sweep + e
            x2[f, p] = x2[f, p] + invd2[p] * (b2[f, p] - image)

        apply_level(
            x2, 1, sweep, s2, sweep, 4.0, 9 - 2 * sweep, m["g2"], m["h2"], 64, 128, smooth_2
        )

    yy2, w2, yy1, v1 = m["yy2"], m["w2"], m["yy1"], m["v1"]

    def widen_2(p, carry):
        for c in range(3):
            v = x2[c, 3 + p]
            odd = 0.5 * (v + y_up(v))
            k = 4 * c + p
            yy2[k, 8:16] = jnp.zeros((8, 128), F32)
            yy2[k, pl.ds(0, 4, stride=2)] = v[0:4]
            yy2[k, pl.ds(1, 4, stride=2)] = odd[0:4]
            yy2[k, 14:15] = v[15:16]
            yy2[k, 15:16] = odd[15:16]
        return carry

    lax.fori_loop(0, 4, widen_2, 0, unroll=True)
    zi3, zo3 = iota((128, BZ), 0), iota((128, BZ), 1)
    near = jnp.abs(zo3 % 128 - 2 * (zi3 % 64))
    pro_2 = jnp.where(near == 0, 1.0, jnp.where(near == 1, 0.5, 0.0)).astype(F32)
    pro_2 = jnp.where(zi3 // 64 == zo3 // 128, pro_2, 0.0)
    w2[...] = mm(yy2[...].reshape(192, 128), pro_2).reshape(12, 16, BZ)
    for p in range(7):
        x = p - 2
        here = rows1 * in_x(gx * 2 + x, NX * 2)
        for c in range(3):
            k = 4 * c + x // 2 + 1
            v = w2[k] if x % 2 == 0 else 0.5 * (w2[k] + w2[k + 1])
            x1[c, p] = x1[c, p] + here * v[:, 0:128]
            x1[3 + c, p] = x1[3 + c, p] + here * v[:, 128:256]

    def smooth_1(f, e, image):
        x1[f, e] = x1[f, e] + invd1[e] * (b1[f, e] - image)

    apply_level(x1, 2, 0, s1, 1, 2.0, 6, m["g1"], m["h1"], 128, 128, smooth_1)

    def widen_1(f, carry):
        for p in range(5):
            v = x1[f, 1 + p]
            odd = 0.5 * (v + y_up(v))
            k = 5 * f + p
            yy1[k, 8:16] = jnp.zeros((8, 128), F32)
            yy1[k, pl.ds(0, 4, stride=2)] = v[0:4]
            yy1[k, pl.ds(1, 4, stride=2)] = odd[0:4]
            yy1[k, 8:9] = v[4:5]
            yy1[k, 9:10] = odd[4:5]
            yy1[k, 15:16] = odd[15:16]
        return carry

    lax.fori_loop(0, 6, widen_1, 0, unroll=True)
    near = jnp.abs(zo3 - 2 * zi3)
    pro_1 = jnp.where(near == 0, 1.0, jnp.where(near == 1, 0.5, 0.0)).astype(F32)

    def widen_z(f, carry):
        at = pl.ds(5 * f, 5)
        v1[at] = mm(yy1[at].reshape(80, 128), pro_1).reshape(5, 16, BZ)
        return carry

    lax.fori_loop(0, 6, widen_z, 0, unroll=True)

    def correct(f, carry):
        for p in range(7):
            x = p - 1
            k = 5 * f + x // 2 + 1
            v = v1[k] if x % 2 == 0 else 0.5 * (v1[k] + v1[k + 1])
            x0[f, p] = x0[f, p] + keep[p] * v
        return carry

    lax.fori_loop(0, 6, correct, 0, unroll=True)

    def smooth_0(f, e, image):
        x0[f, e] = x0[f, e] + invd[e] * (b16[f, e] - image)

    apply_level(x0, 2, 0, s16, 1, 1.0, 6, m["g"], m["h"], BZ, BZ, smooth_0)

    outs = [
        pltpu.make_async_copy(
            x0.at[pl.ds(3 * l, 3), pl.ds(1, 4), pl.ds(0, 8)], pre_out.at[l], out_sem.at[l]
        )
        for l in range(2)
    ]
    for copy in outs:
        copy.start()

    rt, yt, sums = m["rt"], m["yt"], m["sums"]
    sums[...] = jnp.zeros((1, 128), F32)
    line = iota((1, 128), 1)

    def energies(l, carry):
        spread_planes(x0, 3 * l, 1, 5, m["g"].at[l], BZ, 2)
        curve = jnp.zeros((8, 128), F32)
        dot = jnp.zeros((8, 128), F32)
        for tile in range(2):
            q = pl.ds(128 * tile, 128)
            for e in range(4):
                low = [m["g"][l, tile, e, k] for k in range(12)]
                high = [m["g"][l, tile, e + 1, k] for k in range(12)]
                a = modes_of(low, high)
                f = couple(a, None)
                energy = None
                for c in range(3):
                    for k in a[c]:
                        t = a[c][k] * f[c][k]
                        energy = t if energy is None else energy + t
                energy = energy * (LAME2 / 16.0)
                curve = curve + energy * s16[2 + e, 0:8, q]
                rt[l, 2 + e, :, q] = energy * m["coef"][2 + e, :, q]
                for c in range(3):
                    dot = dot + b16[3 * l + c, 1 + e, 0:8, q] * x0[3 * l + c, 1 + e, 0:8, q]
        for k, v in ((l, dot), (2 + l, curve)):
            v = jnp.sum(jnp.sum(v, axis=0, keepdims=True), axis=1, keepdims=True)
            sums[...] = jnp.where(line == k, v, sums[...])
        return carry

    lax.fori_loop(0, 2, energies, 0, unroll=True)

    rc, sc, rx = m["rc"], m["sc"], m["rx"]
    twin = pltpu.make_async_remote_copy(
        src_ref=sums, dst_ref=rc, send_sem=group_send.at[2], recv_sem=group_recv.at[2],
        device_id=(gx, gy + 1 - 2 * lax.rem(gy, 2)), device_id_type=pl.DeviceIdType.MESH,
    )
    twin.start()
    for x in range(4):
        one, two = rt[0, 2 + x], rt[1, 2 + x]
        yt[x] = jnp.where(
            (sub() < 2) | (sub() >= 6), one,
            jnp.where(sub() < 4, y_down(two, 2), y_up(two, 2)),
        )
    rt_lo, rt_hi = m["rt_lo"], m["rt_hi"]
    fourth = [
        message(yt.at[pl.ds(2, 2)], rt_lo.at[pl.ds(0, 2)], 1, 1),
        message(yt.at[pl.ds(2, 2)], rt_hi.at[pl.ds(0, 2)], 1, -1),
        message(yt.at[pl.ds(0, 2)], rt_lo.at[pl.ds(6, 2)], -1, 1),
        message(yt.at[pl.ds(0, 2)], rt_hi.at[pl.ds(6, 2)], -1, -1),
        message(rt.at[:, pl.ds(4, 2)], rt.at[:, pl.ds(0, 2)], 1, 0),
        message(rt.at[:, pl.ds(2, 2)], rt.at[:, pl.ds(6, 2)], -1, 0),
        message(yt, rt_lo.at[pl.ds(2, 4)], 0, 1),
        message(yt, rt_hi.at[pl.ds(2, 4)], 0, -1),
    ]
    for copy in fourth:
        copy.start()
    pl.semaphore_wait(token.at[1], 2)
    twin.wait_recv()
    sc[...] = sums[...] + rc[...]

    rows_of = [lax.rem(gy + 2 * k, NY) for k in range(4)]
    k = 0
    for ax in sorted(range(NX), key=lambda d: -min(d, NX - d)):
        other = lax.rem(gx + ax, NX)
        for j in (2, 1, 3, 0):
            if (ax, j) != (0, 0):
                pltpu.make_async_remote_copy(
                    src_ref=sc, dst_ref=rx.at[k], send_sem=group_send.at[3],
                    recv_sem=group_recv.at[3], device_id=(other, rows_of[j]),
                    device_id_type=pl.DeviceIdType.MESH,
                ).start()
                k += 1

    for copy in fourth:
        copy.wait_recv()
    f16, fil = m["f16"], m["fil"]

    def filter_load(l, carry):
        def put(p, inner):
            hi, lo = rt_hi[p], rt_lo[p]
            moved = jnp.where(sub() < 4, y_up(hi, 2), y_down(lo, 2))
            plain = jnp.where(sub() < 4, hi, lo)
            halo = jnp.where((sub() >= 2) & (sub() < 6), 0.0, jnp.where(l == 0, plain, moved))
            both = jnp.concatenate([rt[l, p], halo], axis=0)
            here = rows0 * in_x(gx * BX + p - 2, NX * BX)
            put_plane(f16, p, jnp.where(here > 0.0, both, 0.0))
            return inner

        lax.fori_loop(0, 8, put, 0, unroll=True)

        def run(x, inner):
            fil[l, x] = filter_plane(f16, x + 2, 8)
            return inner

        lax.fori_loop(0, 4, run, 0, unroll=True)
        return carry

    lax.fori_loop(0, 2, filter_load, 0)

    outs.append(pltpu.make_async_copy(fil, fil_out, out_sem.at[2]))
    outs[2].start()
    group_done(rx, group_recv, 3)
    total = sc[...] + jnp.sum(rx[...], axis=0)
    out = jnp.zeros((1, 128), F32)
    for l in range(2):
        dot, curve = total[:, l : l + 1], total[:, 2 + l : 3 + l]
        step = dot / curve
        for k, v in ((l, step * dot * (1.0 / CELLS)), (2 + l, step), (4 + l, step * step)):
            out = jnp.where(line == k, v, out)
    scal_out[...] = out
    for copy in outs:
        copy.wait()

    for copy in first + second + last + third + late + fourth:
        copy.wait_send()
    group_done(m["rs1"], group_send, 0)
    group_done(rb2, group_send, 1)
    twin.wait_send()
    group_done(rx, group_send, 3)


def scale_kernel(precond, filtered, scalars, disp, sens, comp):
    for l in range(2):
        comp[l] = scalars[0, l]
        disp[l] = precond[l] * scalars[0, 2 + l]
    sens[...] = filtered[0] * scalars[0, 4] + filtered[1] * scalars[0, 5]


def per_device(density, passive_void_mask, support_node_mask, loaded_node_mask, traction):
    scratch = [
        pltpu.VMEM(shape, jnp.int32 if name in INTS else F32) for name, shape in SCRATCH.items()
    ]
    dma = pltpu.SemaphoreType.DMA
    hbm = pl.BlockSpec(memory_space=pltpu.HBM)
    precond, filtered, scalars = pl.pallas_call(
        kernel,
        out_shape=(
            jax.ShapeDtypeStruct((2, 3, BX, BY, BZ), F32),
            jax.ShapeDtypeStruct((2, BX, BY, BZ), F32),
            jax.ShapeDtypeStruct((1, 128), F32),
        ),
        in_specs=[hbm] * 5,
        out_specs=(hbm, hbm, pl.BlockSpec(memory_space=pltpu.VMEM)),
        scratch_shapes=scratch
        + [dma((5,)), dma((N_SEMS,)), dma((N_SEMS,)), dma((4,)), dma((4,))]
        + [dma((3,)), pltpu.SemaphoreType.REGULAR((2,))],
        compiler_params=pltpu.CompilerParams(
            collective_id=0, has_side_effects=True, vmem_limit_bytes=63 * 2**20
        ),
    )(density, passive_void_mask, support_node_mask, loaded_node_mask, traction)
    vmem, smem = pl.BlockSpec(memory_space=pltpu.VMEM), pl.BlockSpec(memory_space=pltpu.SMEM)
    return pl.pallas_call(
        scale_kernel,
        out_shape=(
            jax.ShapeDtypeStruct((2, 3, BX, BY, BZ), F32),
            jax.ShapeDtypeStruct((BX, BY, BZ), F32),
            jax.ShapeDtypeStruct((2,), F32),
        ),
        in_specs=[vmem, vmem, smem],
        out_specs=(vmem, vmem, smem),
        compiler_params=pltpu.CompilerParams(vmem_limit_bytes=63 * 2**20),
    )(precond, filtered, scalars)


def solution(mesh):
    in_specs = (
        P("gx", "gy", None),
        P("gx", "gy", None),
        P("gx", "gy", None),
        P(None, "gx", "gy", None),
        P(None, None, "gx", "gy", None),
    )
    out_specs = (P(None, None, "gx", "gy", None), P("gx", "gy", None), P())
    return jax.shard_map(
        per_device, mesh=mesh, in_specs=in_specs, out_specs=out_specs, check_vma=False
    )
```
